256 devices in a mesh: dp: 4 (over y_hi, core), seq: 64 (over z, y_lo, x).
Axes of the slice: x: 4, y: 4 (y_hi: 2, y_lo: 2; y = y_hi * 2 + y_lo), z: 8, core: 2. Of those that a mesh axis runs over, the one named last changes fastest.
Arguments:
- hidden: bfloat16 [4, 64, 128, 1152], P('dp', 'seq'), may hold values from -6 to 6
- query_space: bfloat16 [4, 64, 128, 1152], P('dp', 'seq'), may hold values from -42 to 42
- key_space: bfloat16 [4, 64, 128, 1152], P('dp', 'seq'), may hold values from -42 to 42
- value_space: bfloat16 [4, 64, 128, 1152], P('dp', 'seq'), may hold values from -6 to 6
- positions: int32 [3, 4, 64, 128], P(None, 'dp'), may hold values from 0 to 252, as said below
- proj_space: bfloat16 [1152, 1152], P('dp'), may hold values from -0.1875 to 0.1875
- shift_time: float32 [4, 1152], P('dp'), may hold values from -3 to 3
- scale_time: float32 [4, 1152], P('dp'), may hold values from -1.8 to 1.8
- qkv_time: bfloat16 [1152, 3456], P('dp'), may hold values from -0.35355339 to 0.35355339
- grad_attn_time: bfloat16 [4, 64, 128, 1152], P('dp', None, 'seq'), may hold values from -6 to 6
- grad_resid: bfloat16 [4, 64, 128, 1152], P('dp', 'seq'), may hold values from -6 to 6
Outputs:
- grad_hidden: bfloat16 [4, 64, 128, 1152], P('dp', 'seq')
- grad_query: bfloat16 [4, 64, 128, 1152], P('dp', 'seq')
- grad_key: bfloat16 [4, 64, 128, 1152], P('dp', 'seq')
- grad_value: bfloat16 [4, 64, 128, 1152], P('dp', 'seq')
- grad_proj_space: float32 [1152, 1152], P('dp', 'seq')
- grad_qkv_time: float32 [1152, 3456], P('dp', 'seq')
- grad_shift: float32 [4, 1152], P('dp')
- grad_scale: float32 [4, 1152], P('dp')
The draws below stay inside these ranges and needn't reach their ends.
Inputs may be any that keep to these rules, and one draw needn't show every extreme that they name: positions[0] is s * f for frame f with a stride s of 1 to 4 per clip, 4 in the first clip; positions[1] and positions[2] are the token's row p // 16 and column p % 16 within the frame plus an offset of 0 to 8 per clip, 8 in the first clip.
All inputs are finite; a program needn't handle non-finite values.
Results may differ from the reference program's by a relative error of at most 0.02.
The reference program's roundings to bfloat16 on the way count: a program that leaves them out, or rounds other values in their place, can miss the bound.
Values may be sent and summed in bfloat16 or wider, within the bound.
A program may use at most 128 MiB of HBM per device.

```python
import math
import jax
import jax.numpy as jnp
from jax import lax

D = 1152
HEADS = 16
HW = 128
FRAMES = 64
CLIPS = 4


def draw_query_space(key, part):
    key = jax.random.fold_in(key, 21)
    values = jnp.clip(jax.random.normal(key, (CLIPS, FRAMES, HW, D), jnp.float32), -6.0, 6.0)
    return values.astype(jnp.bfloat16)


def draw_key_space(key, part):
    key = jax.random.fold_in(key, 22)
    values = jnp.clip(jax.random.normal(key, (CLIPS, FRAMES, HW, D), jnp.float32), -6.0, 6.0)
    return values.astype(jnp.bfloat16)


def draw_qkv_time(key, part):
    key = jax.random.fold_in(key, 23)
    weights = jnp.clip(jax.random.normal(key, (D, 3 * D), jnp.float32), -6.0, 6.0) * D ** (-0.5)
    return weights.astype(jnp.bfloat16)


def draw_positions(key, part):
    key = jax.random.fold_in(key, 31)
    key_stride, key_offset = jax.random.split(key)
    strides = jax.random.randint(key_stride, (CLIPS,), 1, 5).at[0].set(4)
    offsets = jax.random.randint(key_offset, (2, CLIPS), 0, 9).at[:, 0].set(8)
    frame_index = jnp.arange(FRAMES, dtype=jnp.int32)
    spot_index = jnp.arange(HW, dtype=jnp.int32)
    full_shape = (CLIPS, FRAMES, HW)
    frame_places = jnp.broadcast_to(strides[:, None, None] * frame_index[None, :, None], full_shape)
    row_places = jnp.broadcast_to((spot_index // 16)[None, None, :] + offsets[0][:, None, None], full_shape)
    col_places = jnp.broadcast_to((spot_index % 16)[None, None, :] + offsets[1][:, None, None], full_shape)
    return jnp.stack([frame_places, row_places, col_places]).astype(jnp.int32)


def steps_of(own_key, shape, shards, low, largest):
    factor_of, own = 1.0, jax.random.fold_in(own_key, 6)
    for axis_at, blocks in shards:
        steps = jnp.exp(jax.random.uniform(jax.random.fold_in(own, axis_at), (blocks,), jnp.float32, low / len(shards), largest / len(shards)))
        factor_of = factor_of * jnp.repeat(steps, shape[axis_at] // blocks).reshape([-1 if axis == axis_at else 1 for axis in range(len(shape))])
    return factor_of


def bell_draw(key, shape, spread, bound, cuts=(), kind=jnp.bfloat16):
    array = jax.random.normal(key, shape, jnp.float32) * spread
    if len(cuts) > 0:
        array = steps_of(key, shape, cuts, -0.22, 0.18) * array
    return jnp.clip(array, min=-bound, max=bound).astype(kind)


def setup_inputs(seed: int = 0) -> dict:
    key_list = jax.random.split(jax.random.key(seed), 12)
    return {
        "hidden": bell_draw(key_list[0], (CLIPS, FRAMES, HW, D), 1.0, 6.0, ((0, 4), (1, 64))),
        "query_space": draw_query_space(jax.random.fold_in(key_list[11], 71), 0),
        "key_space": draw_key_space(jax.random.fold_in(key_list[11], 71), 0),
        "value_space": bell_draw(key_list[3], (CLIPS, FRAMES, HW, D), 1.0, 6.0, ((0, 4), (1, 64))),
        "positions": draw_positions(jax.random.fold_in(key_list[11], 71), 0),
        "proj_space": bell_draw(key_list[5], (D, D), D ** -0.5, 0.1875, ((0, 4),)),
        "shift_time": bell_draw(key_list[6], (CLIPS, D), 0.5, 3.0, ((0, 4),), jnp.float32),
        "scale_time": bell_draw(key_list[7], (CLIPS, D), 0.3, 1.8, ((0, 4),), jnp.float32),
        "qkv_time": draw_qkv_time(jax.random.fold_in(key_list[11], 71), 0),
        "grad_attn_time": bell_draw(key_list[9], (CLIPS, FRAMES, HW, D), 1.0, 6.0, ((0, 4), (2, 64))),
        "grad_resid": bell_draw(key_list[10], (CLIPS, FRAMES, HW, D), 1.0, 6.0, ((0, 4), (1, 64))),
    }


epsilon = 1e-06

def stored(values):
    return lax.optimization_barrier(values.astype(jnp.bfloat16))

def rotate(values, places, direction):
    half_width = values.shape[-1] // 2
    frequency = 10000.0 ** (-jnp.arange(half_width, dtype=jnp.float32) / half_width)
    angles = places.astype(jnp.float32)[..., None] * frequency
    cosine = jnp.cos(angles)[..., None, :]
    sine_part = direction * jnp.sin(angles)[..., None, :]
    first_half = values[..., :half_width]
    second = values[..., half_width:]
    return jnp.concatenate([first_half * cosine - second * sine_part, second * cosine + first_half * sine_part], axis=-1)

def rotate_space(values, row_places, col_places, direction):
    half_width = values.shape[-1] // 2
    return jnp.concatenate([rotate(values[..., :half_width], row_places, direction), rotate(values[..., half_width:], col_places, direction)], axis=-1)

def attend(query_rows, key_rows, value_rows):
    factor = 1.0 / math.sqrt(query_rows.shape[-1])
    scores = jnp.einsum('gqhe,gkhe->ghqk', query_rows.astype(jnp.float32), key_rows.astype(jnp.float32)) * factor
    exponent = jnp.exp(scores - lax.optimization_barrier(jnp.max(scores, axis=-1, keepdims=True)))
    weights = exponent / lax.optimization_barrier(jnp.sum(exponent, axis=-1, keepdims=True))
    rounded = stored(weights)
    output = jnp.einsum('ghqk,gkhe->gqhe', rounded.astype(jnp.float32), value_rows.astype(jnp.float32))
    return (weights, rounded, output)

def attend_back(query_rows, key_rows, value_rows, weights, rounded, output, grad_rows):
    factor = 1.0 / math.sqrt(query_rows.shape[-1])
    grad_wide = grad_rows.astype(jnp.float32)
    row_delta = jnp.einsum('gqhe,gqhe->ghq', grad_wide, output)
    grad_value = jnp.einsum('ghqk,gqhe->gkhe', rounded.astype(jnp.float32), grad_wide)
    grad_weights = jnp.einsum('gqhe,gkhe->ghqk', grad_wide, value_rows.astype(jnp.float32))
    grad_scores = stored(weights * (grad_weights - row_delta[..., None]) * factor).astype(jnp.float32)
    grad_query = jnp.einsum('ghqk,gkhe->gqhe', grad_scores, key_rows.astype(jnp.float32))
    grad_key = jnp.einsum('ghqk,gqhe->gkhe', grad_scores, query_rows.astype(jnp.float32))
    return (grad_query, grad_key, grad_value)

def reference(hidden, query_space, key_space, value_space, positions, proj_space, shift_time, scale_time, qkv_time, grad_attn_time, grad_resid):
    clip_count, frames, spot_count, model_width = hidden.shape
    head_count = HEADS
    head_size = model_width // head_count
    groups = clip_count * frames
    tokens = frames * spot_count
    per_frame = (groups, spot_count, head_count, head_size)
    row_places = positions[1].reshape(groups, spot_count)
    col_places = positions[2].reshape(groups, spot_count)
    space_inputs = (query_space.reshape(per_frame), key_space.reshape(per_frame), value_space.reshape(per_frame), row_places, col_places)

    def turn_pair(query_rows, key_rows, row_place, col_place):
        space_query = stored(rotate_space(query_rows.astype(jnp.float32), row_place, col_place, 1.0))
        space_key = stored(rotate_space(key_rows.astype(jnp.float32), row_place, col_place, 1.0))
        return (space_query, space_key)

    def space_forward(inputs):
        query_rows, key_rows, value_rows, row_place, col_place = inputs
        space_query, space_key = turn_pair(query_rows, key_rows, row_place, col_place)
        weights, rounded, output = attend(space_query[None], space_key[None], value_rows[None])
        return output[0].astype(jnp.bfloat16)
    space_mixed = lax.map(space_forward, space_inputs).reshape(groups * spot_count, model_width)
    resid = stored(hidden.reshape(-1, model_width).astype(jnp.float32) + jnp.dot(space_mixed, proj_space, preferred_element_type=jnp.float32))
    resid_wide = resid.astype(jnp.float32)
    centered = resid_wide - lax.optimization_barrier(jnp.mean(resid_wide, axis=-1, keepdims=True))
    inverse = lax.rsqrt(lax.optimization_barrier(jnp.mean(centered * centered, axis=-1, keepdims=True)) + epsilon)
    normed = (centered * inverse).reshape(clip_count, tokens, model_width)
    inverse = inverse.reshape(clip_count, tokens, 1)
    modulated = (normed * (1.0 + scale_time[:, None, :]) + shift_time[:, None, :]).astype(jnp.bfloat16)
    modulated_flat = modulated.reshape(-1, model_width)
    projected = jnp.dot(modulated_flat, qkv_time, preferred_element_type=jnp.float32).reshape(clip_count, tokens, 3 * model_width)

    def arrange(values):
        return jnp.transpose(values.reshape(frames, spot_count, head_count, head_size), (1, 0, 2, 3))

    def restore(values):
        return jnp.transpose(values, (1, 0, 2, 3)).reshape(tokens, model_width)

    def time_backward(inputs):
        proj_rows, frame_place, grad_rows = inputs
        places = frame_place.T
        time_query = stored(rotate(arrange(proj_rows[:, :model_width]), places, 1.0))
        time_key = stored(rotate(arrange(proj_rows[:, model_width:2 * model_width]), places, 1.0))
        time_value = stored(arrange(proj_rows[:, 2 * model_width:]))
        weights, rounded, output = attend(time_query, time_key, time_value)
        grad_time_query, grad_time_key, grad_time_value = attend_back(time_query, time_key, time_value, weights, rounded, output, arrange(grad_rows))
        return stored(jnp.concatenate([restore(rotate(grad_time_query, places, -1.0)), restore(rotate(grad_time_key, places, -1.0)), restore(grad_time_value)], axis=-1))
    grad_projected = lax.map(time_backward, (projected, positions[0], grad_attn_time.reshape(clip_count, tokens, model_width)))
    grad_projected = grad_projected.reshape(-1, 3 * model_width)
    grad_qkv_time = jnp.dot(modulated_flat.T, grad_projected, preferred_element_type=jnp.float32)
    grad_modulated = jnp.dot(grad_projected, qkv_time.T, preferred_element_type=jnp.float32).reshape(clip_count, tokens, model_width)
    grad_shift = lax.optimization_barrier(jnp.sum(grad_modulated, axis=1))
    grad_scale = lax.optimization_barrier(jnp.sum(grad_modulated * normed, axis=1))
    grad_normed = grad_modulated * (1.0 + scale_time[:, None, :])
    resid_back = stored((grad_normed - lax.optimization_barrier(jnp.mean(grad_normed, axis=-1, keepdims=True)) - normed * lax.optimization_barrier(jnp.mean(grad_normed * normed, axis=-1, keepdims=True))) * inverse)
    grad_hidden = (grad_resid.reshape(clip_count, tokens, model_width).astype(jnp.float32) + resid_back.astype(jnp.float32)).astype(jnp.bfloat16)
    grad_flat = grad_hidden.reshape(-1, model_width)
    grad_proj_space = jnp.dot(space_mixed.T, grad_flat, preferred_element_type=jnp.float32)
    grad_space_out = stored(jnp.dot(grad_flat, proj_space.T, preferred_element_type=jnp.float32)).reshape(per_frame)

    def space_backward(inputs):
        query_rows, key_rows, value_rows, row_place, col_place, grad_rows = inputs
        space_query, space_key = turn_pair(query_rows, key_rows, row_place, col_place)
        weights, rounded, output = attend(space_query[None], space_key[None], value_rows[None])
        grad_q, grad_k, grad_v = attend_back(space_query[None], space_key[None], value_rows[None], weights, rounded, output, grad_rows[None])
        return (rotate_space(grad_q[0], row_place, col_place, -1.0).astype(jnp.bfloat16), rotate_space(grad_k[0], row_place, col_place, -1.0).astype(jnp.bfloat16), grad_v[0].astype(jnp.bfloat16))
    grad_query, grad_key, grad_value = lax.map(space_backward, space_inputs + (grad_space_out,))
    full_shape = hidden.shape
    return (grad_hidden.reshape(full_shape), grad_query.reshape(full_shape), grad_key.reshape(full_shape), grad_value.reshape(full_shape), grad_proj_space, grad_qkv_time, grad_shift, grad_scale)
```

```python
import math

import jax
import jax.numpy as jnp
from jax import lax
from jax.experimental import pallas as pl
from jax.experimental.pallas import tpu as pltpu
from jax.sharding import PartitionSpec as P

HEADS = 16


epsilon = 1e-06


def rotate(values, places, direction):
    half_width = values.shape[-1] // 2
    frequency = 10000.0 ** (-jnp.arange(half_width, dtype=jnp.float32) / half_width)
    angles = places.astype(jnp.float32)[..., None] * frequency
    cosine = jnp.cos(angles)[..., None, :]
    sine_part = direction * jnp.sin(angles)[..., None, :]
    first_half = values[..., :half_width]
    second = values[..., half_width:]
    return jnp.concatenate(
        [first_half * cosine - second * sine_part, second * cosine + first_half * sine_part],
        axis=-1,
    )


def rotate_space(values, row_places, col_places, direction):
    half_width = values.shape[-1] // 2
    return jnp.concatenate(
        [
            rotate(values[..., :half_width], row_places, direction),
            rotate(values[..., half_width:], col_places, direction),
        ],
        axis=-1,
    )


def attend(query_rows, key_rows, value_rows):
    factor = 1.0 / math.sqrt(query_rows.shape[-1])
    scores = (
        jnp.einsum("gqhe,gkhe->ghqk", query_rows, key_rows, preferred_element_type=jnp.float32)
        * factor
    )
    exponent = jnp.exp(scores - jnp.max(scores, axis=-1, keepdims=True))
    weights = exponent / jnp.sum(exponent, axis=-1, keepdims=True)
    rounded = weights.astype(jnp.bfloat16)
    output = jnp.einsum("ghqk,gkhe->gqhe", rounded, value_rows, preferred_element_type=jnp.float32)
    return (weights, rounded, output)


def attend_back(query_rows, key_rows, value_rows, weights, rounded, output, grad_rows):
    factor = 1.0 / math.sqrt(query_rows.shape[-1])
    row_delta = jnp.einsum("gqhe,gqhe->ghq", grad_rows.astype(jnp.float32), output)
    grad_value = jnp.einsum(
        "ghqk,gqhe->gkhe", rounded, grad_rows, preferred_element_type=jnp.float32
    )
    grad_weights = jnp.einsum(
        "gqhe,gkhe->ghqk", grad_rows, value_rows, preferred_element_type=jnp.float32
    )
    grad_scores = (weights * (grad_weights - row_delta[..., None]) * factor).astype(jnp.bfloat16)
    grad_query = jnp.einsum(
        "ghqk,gkhe->gqhe", grad_scores, key_rows, preferred_element_type=jnp.float32
    )
    grad_key = jnp.einsum(
        "ghqk,gqhe->gkhe", grad_scores, query_rows, preferred_element_type=jnp.float32
    )
    return (grad_query, grad_key, grad_value)


def add_columns(left_side, piece_rows):
    return jnp.dot(left_side, piece_rows, preferred_element_type=jnp.float32)


def place_columns(right_side, piece_rows):
    product = lax.dot_general(
        right_side, piece_rows, (((1,), (1,)), ((), ())), preferred_element_type=jnp.float32
    )
    return product


MESH = pl.DeviceIdType.MESH

PIECE_ROWS = 80
HALF_LANES = 640
KEEP_LANES = 384
ORDER = ("x_near", "y_near", "x_far", "z_near")


def place():
    dp, seq = lax.axis_index("dp"), lax.axis_index("seq")
    hi, core = dp // 2, dp % 2
    z, lo, x = seq // 8, (seq // 4) % 2, seq % 4
    return hi, core, z, lo, x


def device(hi, core, z, lo, x):
    return (hi * 2 + core, z * 8 + lo * 4 + x)


def order_of(group):
    return [ORDER[(group + step) % 4] for step in range(4)]


def piece_of(group, block):
    bits = {name: (block // (8 >> step)) % 2 for step, name in enumerate(order_of(group))}
    x = bits["x_far"] * 2 + (bits["x_near"] + bits["x_far"]) % 2
    return (group * 2 + bits["z_near"]) * 8 + bits["y_near"] * 4 + x


def sum_kernel(
    left_ref, right_ref, out_ref, twin_left, twin_right, work, got0, got1, got2, got3, last, final,
    twin_send, twin_recv, step_send, step_recv, final_send, final_recv,
):
    hi, core, z, lo, x = place()
    near, pair = z % 2, z // 2
    bits = {"x_near": (x % 2 + x // 2) % 2, "x_far": x // 2, "y_near": lo, "z_near": near}
    partners = {
        "x_near": device(hi, core, z, lo, x + 1 - 2 * (x % 2)),
        "x_far": device(hi, core, z, lo, 3 - x),
        "y_near": device(hi, core, z, 1 - lo, x),
        "z_near": device(hi, core, z + 1 - 2 * near, lo, x),
    }
    twin = device(hi, 1 - core, z, lo, x)
    others = []
    for step_hi in range(2):
        for step_pair in range(4):
            if step_hi + step_pair > 0:
                to_hi, to_pair = (hi + step_hi) % 2, (pair + step_pair) % 4
                others.append(
                    (step_hi * 4 + step_pair, to_hi, to_pair,
                     device(to_hi, core, to_pair * 2 + near, lo, x))
                )

    barrier = pltpu.get_barrier_semaphore()
    everyone = [twin] + list(partners.values()) + [other[3] for other in others]
    for peer in everyone:
        pl.semaphore_signal(barrier, inc=1, device_id=peer, device_id_type=MESH)
    pl.semaphore_wait(barrier, len(everyone))

    def send(source, target, send_sem, recv_sem, peer):
        copy = pltpu.make_async_remote_copy(
            src_ref=source, dst_ref=target, send_sem=send_sem, recv_sem=recv_sem,
            device_id=peer, device_id_type=MESH,
        )
        copy.start()
        return copy

    twin_copies = [
        send(right_ref.at[1 - core], twin_right, twin_send.at[0], twin_recv.at[0], twin),
        send(left_ref, twin_left, twin_send.at[1], twin_recv.at[1], twin),
    ]
    for copy in twin_copies:
        copy.wait_recv()

    got = [got0, got1, got2, got3]
    copies = {}

    def fill(group, start):
        def quarter(at, _):
            first = start + at * 4
            pieces = [piece_of(group, first + j) for j in range(4)]
            own = jnp.concatenate([left_ref[piece] for piece in pieces], axis=0)
            other = jnp.concatenate([twin_left[piece] for piece in pieces], axis=0)
            total = jnp.dot(own, right_ref[core], preferred_element_type=jnp.float32)
            total += jnp.dot(other, twin_right[...], preferred_element_type=jnp.float32)
            work[group, pl.ds(first, 4)] = total.astype(jnp.bfloat16).reshape(
                4, PIECE_ROWS, HALF_LANES
            )
            return 0

        lax.fori_loop(0, 2, quarter, 0)

    def take(group, step, start, count, offset):
        def one(at, _):
            total = work[group, start + at].astype(jnp.float32)
            total += got[step][group, offset + at].astype(jnp.float32)
            work[group, start + at] = total.astype(jnp.bfloat16)
            return 0

        lax.fori_loop(0, count, one, 0)

    base = [0, 0, 0, 0]
    for group in range(4):
        name = order_of(group)[0]
        away = (1 - bits[name]) * 8
        fill(group, away)
        copies[group, 0] = send(
            work.at[group, pl.ds(away, 8)], got[0].at[group],
            step_send.at[group, 0], step_recv.at[group, 0], partners[name],
        )
    for group in range(4):
        base[group] = bits[order_of(group)[0]] * 8
        fill(group, base[group])
    for step in range(1, 4):
        half = 8 >> step
        for group in range(4):
            name = order_of(group)[step]
            away = (1 - bits[name]) * half
            copies[group, step - 1].wait_recv()
            take(group, step - 1, base[group] + away, half, away)
            copies[group, step] = send(
                work.at[group, pl.ds(base[group] + away, half)], got[step].at[group],
                step_send.at[group, step], step_recv.at[group, step], partners[name],
            )
            mine = bits[name] * half
            take(group, step - 1, base[group] + mine, half, mine)
            base[group] = base[group] + mine
    for group in range(4):
        copies[group, 3].wait_recv()
        total = work[group, base[group]].astype(jnp.float32) + got3[group, 0].astype(jnp.float32)
        total = total.astype(jnp.bfloat16)
        last[group, 0] = total[:, :KEEP_LANES]
        last[group, 1] = total[:, HALF_LANES - KEEP_LANES :]
    ends = []
    for slot, to_hi, to_pair, peer in others:
        ends.append(
            send(
                last.at[to_pair, to_hi], final.at[slot], final_send.at[slot], final_recv.at[slot], peer
            )
        )
    total = last[pair, hi].astype(jnp.float32)
    for (slot, _, _, _), copy in zip(others, ends):
        copy.wait_recv()
        total += final[slot].astype(jnp.float32)
    out_ref[...] = total
    for copy in twin_copies + list(copies.values()) + ends:
        copy.wait_send()


def sum_products(left, right):
    depth = left.shape[2]
    block = (PIECE_ROWS, HALF_LANES)
    return pl.pallas_call(
        sum_kernel,
        out_shape=jax.ShapeDtypeStruct((PIECE_ROWS, KEEP_LANES), jnp.float32),
        in_specs=[pl.BlockSpec(memory_space=pltpu.VMEM)] * 2,
        out_specs=pl.BlockSpec(memory_space=pltpu.VMEM),
        scratch_shapes=[
            pltpu.VMEM(left.shape, jnp.bfloat16),
            pltpu.VMEM((depth, HALF_LANES), jnp.bfloat16),
            pltpu.VMEM((4, 16) + block, jnp.bfloat16),
            pltpu.VMEM((4, 8) + block, jnp.bfloat16),
            pltpu.VMEM((4, 4) + block, jnp.bfloat16),
            pltpu.VMEM((4, 2) + block, jnp.bfloat16),
            pltpu.VMEM((4, 1) + block, jnp.bfloat16),
            pltpu.VMEM((4, 2, PIECE_ROWS, KEEP_LANES), jnp.bfloat16),
            pltpu.VMEM((8, PIECE_ROWS, KEEP_LANES), jnp.bfloat16),
            pltpu.SemaphoreType.DMA((2,)),
            pltpu.SemaphoreType.DMA((2,)),
            pltpu.SemaphoreType.DMA((4, 4)),
            pltpu.SemaphoreType.DMA((4, 4)),
            pltpu.SemaphoreType.DMA((8,)),
            pltpu.SemaphoreType.DMA((8,)),
        ],
        compiler_params=pltpu.CompilerParams(
            collective_id=3, has_side_effects=True, vmem_limit_bytes=40 * 1024 * 1024
        ),
    )(left, right)


def weight_gradients(grad_projected, modulated, grad_flat, space_mixed):
    tokens, width = modulated.shape
    qkv_rows = grad_projected.T.reshape(64, -1, tokens)
    proj_rows = grad_flat.T.reshape(64, -1, tokens)
    n_qkv, n_proj = qkv_rows.shape[1], proj_rows.shape[1]
    left = jnp.concatenate(
        [
            jnp.pad(qkv_rows, ((0, 0), (0, PIECE_ROWS - n_qkv), (0, 0))),
            jnp.pad(proj_rows, ((0, 0), (n_qkv, PIECE_ROWS - n_qkv - n_proj), (0, 0))),
        ],
        axis=2,
    )
    part = width // 4
    right = jnp.concatenate([modulated, space_mixed], axis=0).reshape(2 * tokens, 2, 2, part)
    right = jnp.transpose(right, (2, 0, 1, 3)).reshape(2, 2 * tokens, 2 * part)
    right = jnp.pad(right, ((0, 0), (0, 0), (0, HALF_LANES - 2 * part)))
    summed = sum_products(left, right)
    hi = lax.axis_index("dp") // 2
    start = hi * (part + KEEP_LANES - HALF_LANES)
    kept = lax.dynamic_slice(summed, (0, start), (n_qkv + n_proj, part)).T
    return kept[:, n_qkv:], kept[:, :n_qkv]


def body(
    hidden,
    query_space,
    key_space,
    value_space,
    positions,
    proj_space,
    shift_time,
    scale_time,
    qkv_time,
    grad_attn_time,
    grad_resid,
):
    frames_dev, spot_count, model_width = (hidden.shape[1], hidden.shape[2], hidden.shape[3])
    frames, spots_dev = (grad_attn_time.shape[1], grad_attn_time.shape[2])
    head_count = HEADS
    head_size = model_width // head_count
    token_count = frames * spots_dev
    seq_place = lax.axis_index("seq")
    row_places = lax.dynamic_slice_in_dim(positions[1, 0], seq_place * frames_dev, frames_dev, 0)
    col_places = lax.dynamic_slice_in_dim(positions[2, 0], seq_place * frames_dev, frames_dev, 0)
    frame_places = lax.dynamic_slice_in_dim(positions[0, 0], seq_place * spots_dev, spots_dev, 1).T
    per_frame = (frames_dev, spot_count, head_count, head_size)
    space_query = rotate_space(
        query_space.reshape(per_frame).astype(jnp.float32), row_places, col_places, 1.0
    ).astype(jnp.bfloat16)
    space_key = rotate_space(
        key_space.reshape(per_frame).astype(jnp.float32), row_places, col_places, 1.0
    ).astype(jnp.bfloat16)
    space_value = value_space.reshape(per_frame)
    space_weights, space_rounded, space_out = attend(space_query, space_key, space_value)
    space_mixed = space_out.astype(jnp.bfloat16).reshape(frames_dev * spot_count, model_width)
    full_proj = lax.all_gather(proj_space, "dp", axis=0, tiled=True)
    resid = (
        hidden.reshape(-1, model_width).astype(jnp.float32)
        + jnp.dot(space_mixed, full_proj, preferred_element_type=jnp.float32)
    ).astype(jnp.bfloat16)
    resid_space = lax.all_to_all(
        resid.reshape(1, frames_dev, spot_count, model_width),
        "seq",
        split_axis=2,
        concat_axis=1,
        tiled=True,
    )
    resid_wide = resid_space.reshape(token_count, model_width).astype(jnp.float32)
    centered = resid_wide - jnp.mean(resid_wide, axis=-1, keepdims=True)
    inverse = lax.rsqrt(jnp.mean(centered * centered, axis=-1, keepdims=True) + epsilon)
    normed = centered * inverse
    modulated = (normed * (1.0 + scale_time) + shift_time).astype(jnp.bfloat16)
    projected = add_columns(modulated, lax.all_gather(qkv_time, "dp", axis=0, tiled=True))

    def arrange(values):
        return jnp.transpose(values.reshape(frames, spots_dev, head_count, head_size), (1, 0, 2, 3))

    def restore(values):
        return jnp.transpose(values, (1, 0, 2, 3)).reshape(token_count, model_width)

    time_query = rotate(arrange(projected[:, :model_width]), frame_places, 1.0).astype(jnp.bfloat16)
    time_key = rotate(
        arrange(projected[:, model_width : 2 * model_width]), frame_places, 1.0
    ).astype(jnp.bfloat16)
    time_value = arrange(projected[:, 2 * model_width :]).astype(jnp.bfloat16)
    time_weights, time_rounded, time_out = attend(time_query, time_key, time_value)
    grad_time = arrange(grad_attn_time.reshape(token_count, model_width))
    grad_time_query, grad_time_key, grad_time_value = attend_back(
        time_query, time_key, time_value, time_weights, time_rounded, time_out, grad_time
    )
    grad_projected = jnp.concatenate(
        [
            restore(rotate(grad_time_query, frame_places, -1.0)),
            restore(rotate(grad_time_key, frame_places, -1.0)),
            restore(grad_time_value),
        ],
        axis=-1,
    ).astype(jnp.bfloat16)
    grad_modulated = place_columns(
        grad_projected, lax.all_gather(qkv_time, "dp", axis=0, tiled=True)
    )
    grad_shift, grad_scale = lax.psum(
        (
            jnp.sum(grad_modulated, axis=0, keepdims=True),
            jnp.sum(grad_modulated * normed, axis=0, keepdims=True),
        ),
        "seq",
    )
    grad_normed = grad_modulated * (1.0 + scale_time)
    resid_back = (
        (
            grad_normed
            - jnp.mean(grad_normed, axis=-1, keepdims=True)
            - normed * jnp.mean(grad_normed * normed, axis=-1, keepdims=True)
        )
        * inverse
    ).astype(jnp.bfloat16)
    back_frames = lax.all_to_all(
        resid_back.reshape(1, frames, spots_dev, model_width),
        "seq",
        split_axis=1,
        concat_axis=2,
        tiled=True,
    )
    grad_hidden = (grad_resid.astype(jnp.float32) + back_frames.astype(jnp.float32)).astype(
        jnp.bfloat16
    )
    grad_flat = grad_hidden.reshape(-1, model_width)
    grad_space_out = (
        lax.dot_general(
            grad_flat, full_proj, (((1,), (1,)), ((), ())), preferred_element_type=jnp.float32
        )
        .astype(jnp.bfloat16)
        .reshape(per_frame)
    )
    grad_space_query, grad_space_key, grad_space_value = attend_back(
        space_query, space_key, space_value, space_weights, space_rounded, space_out, grad_space_out
    )
    full_shape = hidden.shape
    grad_query = (
        rotate_space(grad_space_query, row_places, col_places, -1.0)
        .astype(jnp.bfloat16)
        .reshape(full_shape)
    )
    grad_key = (
        rotate_space(grad_space_key, row_places, col_places, -1.0)
        .astype(jnp.bfloat16)
        .reshape(full_shape)
    )
    grad_value = grad_space_value.astype(jnp.bfloat16).reshape(full_shape)
    grad_proj_space, grad_qkv_time = weight_gradients(
        grad_projected, modulated, grad_flat, space_mixed
    )
    return (
        grad_hidden,
        grad_query,
        grad_key,
        grad_value,
        grad_proj_space,
        grad_qkv_time,
        grad_shift,
        grad_scale,
    )


def solution(mesh):
    in_specs = (
        P("dp", "seq", None, None),
        P("dp", "seq", None, None),
        P("dp", "seq", None, None),
        P("dp", "seq", None, None),
        P(None, "dp", None, None),
        P("dp", None),
        P("dp", None),
        P("dp", None),
        P("dp", None),
        P("dp", None, "seq", None),
        P("dp", "seq", None, None),
    )
    out_specs = (
        P("dp", "seq", None, None),
        P("dp", "seq", None, None),
        P("dp", "seq", None, None),
        P("dp", "seq", None, None),
        P("dp", "seq"),
        P("dp", "seq"),
        P("dp", None),
        P("dp", None),
    )
    return jax.shard_map(body, mesh=mesh, in_specs=in_specs, out_specs=out_specs, check_vma=False)
```

```python
import math

import jax
import jax.numpy as jnp
from jax import lax
from jax.experimental import pallas as pl
from jax.experimental.pallas import tpu as pltpu
from jax.sharding import PartitionSpec as P

HEADS = 16


epsilon = 1e-06


def rotate(values, places, direction):
    half_width = values.shape[-1] // 2
    frequency = 10000.0 ** (-jnp.arange(half_width, dtype=jnp.float32) / half_width)
    angles = places.astype(jnp.float32)[..., None] * frequency
    cosine = jnp.cos(angles)[..., None, :]
    sine_part = direction * jnp.sin(angles)[..., None, :]
    first_half = values[..., :half_width]
    second = values[..., half_width:]
    return jnp.concatenate(
        [first_half * cosine - second * sine_part, second * cosine + first_half * sine_part],
        axis=-1,
    )


def rotate_space(values, row_places, col_places, direction):
    half_width = values.shape[-1] // 2
    return jnp.concatenate(
        [
            rotate(values[..., :half_width], row_places, direction),
            rotate(values[..., half_width:], col_places, direction),
        ],
        axis=-1,
    )


def attend(query_rows, key_rows, value_rows):
    factor = 1.0 / math.sqrt(query_rows.shape[-1])
    scores = (
        jnp.einsum("gqhe,gkhe->ghqk", query_rows, key_rows, preferred_element_type=jnp.float32)
        * factor
    )
    exponent = jnp.exp(scores - jnp.max(scores, axis=-1, keepdims=True))
    weights = exponent / jnp.sum(exponent, axis=-1, keepdims=True)
    rounded = weights.astype(jnp.bfloat16)
    output = jnp.einsum("ghqk,gkhe->gqhe", rounded, value_rows, preferred_element_type=jnp.float32)
    return (weights, rounded, output)


def attend_back(query_rows, key_rows, value_rows, weights, rounded, output, grad_rows):
    factor = 1.0 / math.sqrt(query_rows.shape[-1])
    row_delta = jnp.einsum("gqhe,gqhe->ghq", grad_rows.astype(jnp.float32), output)
    grad_value = jnp.einsum(
        "ghqk,gqhe->gkhe", rounded, grad_rows, preferred_element_type=jnp.float32
    )
    grad_weights = jnp.einsum(
        "gqhe,gkhe->ghqk", grad_rows, value_rows, preferred_element_type=jnp.float32
    )
    grad_scores = (weights * (grad_weights - row_delta[..., None]) * factor).astype(jnp.bfloat16)
    grad_query = jnp.einsum(
        "ghqk,gkhe->gqhe", grad_scores, key_rows, preferred_element_type=jnp.float32
    )
    grad_key = jnp.einsum(
        "ghqk,gqhe->gkhe", grad_scores, query_rows, preferred_element_type=jnp.float32
    )
    return (grad_query, grad_key, grad_value)


def add_columns(left_side, piece_rows):
    return jnp.dot(left_side, piece_rows, preferred_element_type=jnp.float32)


def place_columns(right_side, piece_rows):
    product = lax.dot_general(
        right_side, piece_rows, (((1,), (1,)), ((), ())), preferred_element_type=jnp.float32
    )
    return product


MESH = pl.DeviceIdType.MESH

PIECE_ROWS = 80
HALF_LANES = 640
KEEP_LANES = 384
ORDER = ("x_near", "y_near", "x_far", "z_near")


def place():
    dp, seq = lax.axis_index("dp"), lax.axis_index("seq")
    hi, core = dp // 2, dp % 2
    z, lo, x = seq // 8, (seq // 4) % 2, seq % 4
    return hi, core, z, lo, x


def device(hi, core, z, lo, x):
    return (hi * 2 + core, z * 8 + lo * 4 + x)


def send(source, target, sends, recvs, at, peer):
    copy = pltpu.make_async_remote_copy(
        src_ref=source, dst_ref=target, send_sem=sends.at[at], recv_sem=recvs.at[at],
        device_id=peer, device_id_type=MESH,
    )
    copy.start()
    return copy


def meet(peers):
    barrier = pltpu.get_barrier_semaphore()
    for peer in peers:
        pl.semaphore_signal(barrier, inc=1, device_id=peer, device_id_type=MESH)
    pl.semaphore_wait(barrier, len(peers))


def order_of(group):
    return [ORDER[(group + step) % 4] for step in range(4)]


def piece_of(group, block):
    bits = {name: (block // (8 >> step)) % 2 for step, name in enumerate(order_of(group))}
    x = bits["x_far"] * 2 + (bits["x_near"] + bits["x_far"]) % 2
    return (group * 2 + bits["z_near"]) * 8 + bits["y_near"] * 4 + x


def sum_kernel(
    left_ref, right_ref, out_ref, twin_left, twin_right, work, got0, got1, got2, got3, last, final,
    twin_send, twin_recv, step_send, step_recv, final_send, final_recv,
):
    hi, core, z, lo, x = place()
    near, pair = z % 2, z // 2
    bits = {"x_near": (x % 2 + x // 2) % 2, "x_far": x // 2, "y_near": lo, "z_near": near}
    partners = {
        "x_near": device(hi, core, z, lo, x + 1 - 2 * (x % 2)),
        "x_far": device(hi, core, z, lo, 3 - x),
        "y_near": device(hi, core, z, 1 - lo, x),
        "z_near": device(hi, core, z + 1 - 2 * near, lo, x),
    }
    twin = device(hi, 1 - core, z, lo, x)
    others = []
    for step_hi in range(2):
        for step_pair in range(4):
            if step_hi + step_pair > 0:
                to_hi, to_pair = (hi + step_hi) % 2, (pair + step_pair) % 4
                others.append(
                    (step_hi * 4 + step_pair, to_hi, to_pair,
                     device(to_hi, core, to_pair * 2 + near, lo, x))
                )

    meet([twin] + list(partners.values()) + [other[3] for other in others])
    twin_copies = [
        send(right_ref.at[1 - core], twin_right, twin_send, twin_recv, 0, twin),
        send(left_ref, twin_left, twin_send, twin_recv, 1, twin),
    ]
    for copy in twin_copies:
        copy.wait_recv()

    got = [got0, got1, got2, got3]
    copies = {}

    def fill(group, start):
        def quarter(at, _):
            first = start + at * 4
            pieces = [piece_of(group, first + j) for j in range(4)]
            own = jnp.concatenate([left_ref[piece] for piece in pieces], axis=0)
            other = jnp.concatenate([twin_left[piece] for piece in pieces], axis=0)
            total = jnp.dot(own, right_ref[core], preferred_element_type=jnp.float32)
            total += jnp.dot(other, twin_right[...], preferred_element_type=jnp.float32)
            work[group, pl.ds(first, 4)] = total.astype(jnp.bfloat16).reshape(
                4, PIECE_ROWS, HALF_LANES
            )
            return 0

        lax.fori_loop(0, 2, quarter, 0)

    def take(group, step, start, count, offset):
        def one(at, _):
            total = work[group, start + at].astype(jnp.float32)
            total += got[step][group, offset + at].astype(jnp.float32)
            work[group, start + at] = total.astype(jnp.bfloat16)
            return 0

        lax.fori_loop(0, count, one, 0)

    base = [0, 0, 0, 0]
    for group in range(4):
        name = order_of(group)[0]
        away = (1 - bits[name]) * 8
        fill(group, away)
        copies[group, 0] = send(
            work.at[group, pl.ds(away, 8)], got[0].at[group],
            step_send, step_recv, (group, 0), partners[name],
        )
    for group in range(4):
        base[group] = bits[order_of(group)[0]] * 8
        fill(group, base[group])
    for step in range(1, 4):
        half = 8 >> step
        for group in range(4):
            name = order_of(group)[step]
            away = (1 - bits[name]) * half
            copies[group, step - 1].wait_recv()
            take(group, step - 1, base[group] + away, half, away)
            copies[group, step] = send(
                work.at[group, pl.ds(base[group] + away, half)], got[step].at[group],
                step_send, step_recv, (group, step), partners[name],
            )
            mine = bits[name] * half
            take(group, step - 1, base[group] + mine, half, mine)
            base[group] = base[group] + mine
    for group in range(4):
        copies[group, 3].wait_recv()
        total = work[group, base[group]].astype(jnp.float32) + got3[group, 0].astype(jnp.float32)
        total = total.astype(jnp.bfloat16)
        last[group, 0] = total[:, :KEEP_LANES]
        last[group, 1] = total[:, HALF_LANES - KEEP_LANES :]
    ends = []
    for slot, to_hi, to_pair, peer in others:
        ends.append(
            send(
                last.at[to_pair, to_hi], final.at[slot], final_send, final_recv, slot, peer
            )
        )
    total = last[pair, hi].astype(jnp.float32)
    for (slot, _, _, _), copy in zip(others, ends):
        copy.wait_recv()
        total += final[slot].astype(jnp.float32)
    out_ref[...] = total
    for copy in twin_copies + list(copies.values()) + ends:
        copy.wait_send()


def sum_products(left, right):
    depth = left.shape[2]
    block = (PIECE_ROWS, HALF_LANES)
    return pl.pallas_call(
        sum_kernel,
        out_shape=jax.ShapeDtypeStruct((PIECE_ROWS, KEEP_LANES), jnp.float32),
        in_specs=[pl.BlockSpec(memory_space=pltpu.VMEM)] * 2,
        out_specs=pl.BlockSpec(memory_space=pltpu.VMEM),
        scratch_shapes=[
            pltpu.VMEM(left.shape, jnp.bfloat16),
            pltpu.VMEM((depth, HALF_LANES), jnp.bfloat16),
            pltpu.VMEM((4, 16) + block, jnp.bfloat16),
            pltpu.VMEM((4, 8) + block, jnp.bfloat16),
            pltpu.VMEM((4, 4) + block, jnp.bfloat16),
            pltpu.VMEM((4, 2) + block, jnp.bfloat16),
            pltpu.VMEM((4, 1) + block, jnp.bfloat16),
            pltpu.VMEM((4, 2, PIECE_ROWS, KEEP_LANES), jnp.bfloat16),
            pltpu.VMEM((8, PIECE_ROWS, KEEP_LANES), jnp.bfloat16),
            pltpu.SemaphoreType.DMA((2,)),
            pltpu.SemaphoreType.DMA((2,)),
            pltpu.SemaphoreType.DMA((4, 4)),
            pltpu.SemaphoreType.DMA((4, 4)),
            pltpu.SemaphoreType.DMA((8,)),
            pltpu.SemaphoreType.DMA((8,)),
        ],
        compiler_params=pltpu.CompilerParams(
            collective_id=3, has_side_effects=True, vmem_limit_bytes=40 * 1024 * 1024
        ),
    )(left, right)


def weight_gradients(grad_projected, modulated, grad_flat, space_mixed):
    tokens, width = modulated.shape
    qkv_rows = grad_projected.T.reshape(64, -1, tokens)
    proj_rows = grad_flat.T.reshape(64, -1, tokens)
    n_qkv, n_proj = qkv_rows.shape[1], proj_rows.shape[1]
    left = jnp.concatenate(
        [
            jnp.pad(qkv_rows, ((0, 0), (0, PIECE_ROWS - n_qkv), (0, 0))),
            jnp.pad(proj_rows, ((0, 0), (n_qkv, PIECE_ROWS - n_qkv - n_proj), (0, 0))),
        ],
        axis=2,
    )
    part = width // 4
    right = jnp.concatenate([modulated, space_mixed], axis=0).reshape(2 * tokens, 2, 2, part)
    right = jnp.transpose(right, (2, 0, 1, 3)).reshape(2, 2 * tokens, 2 * part)
    right = jnp.pad(right, ((0, 0), (0, 0), (0, HALF_LANES - 2 * part)))
    summed = sum_products(left, right)
    hi = lax.axis_index("dp") // 2
    start = hi * (part + KEEP_LANES - HALF_LANES)
    kept = lax.dynamic_slice(summed, (0, start), (n_qkv + n_proj, part)).T
    return kept[:, n_qkv:], kept[:, :n_qkv]


def near_peers():
    hi, core, z, lo, x = place()
    group = lo * 4 + x
    plane = [(hi * 2 + core, z * 8 + (group + step) % 8) for step in range(1, 8)]
    line = [(hi * 2 + core, ((z + step) % 8) * 8 + group) for step in range(1, 8)]
    return plane, line


def swap_eights(rows):
    count = rows.shape[0]
    at = lax.broadcasted_iota(jnp.int32, (count, count), 0)
    origin = lax.broadcasted_iota(jnp.int32, (count, count), 1)
    wanted = (at // 2 % 8) * 16 + at // 16 * 2 + at % 2
    chosen = jnp.where(origin == wanted, 1.0, 0.0).astype(jnp.bfloat16)
    moved = jnp.dot(chosen, rows, preferred_element_type=jnp.float32)
    return moved.astype(jnp.bfloat16)


class Exchange:
    def __init__(self, first, got_first, second, got_second, sends, recvs):
        self.first, self.got_first = first, got_first
        self.second, self.got_second = second, got_second
        self.sends, self.recvs = sends, recvs
        self.plane, self.line = near_peers()
        _, _, self.z, lo, x = place()
        self.group = lo * 4 + x

    def start_plane(self, rows):
        self.first[...] = swap_eights(rows).reshape(self.first.shape)
        self.copies = [
            send(
                self.first.at[(self.group + step) % 8], self.got_first.at[self.group],
                self.sends, self.recvs, step, self.plane[step - 1],
            )
            for step in range(1, 8)
        ]
        self.got_first[self.group] = self.first[self.group]

    def start_line(self):
        for copy in self.copies:
            copy.wait_recv()
        rows = self.got_first[...].reshape(128, -1)
        self.second[...] = swap_eights(rows).reshape(self.second.shape)
        more = [
            send(
                self.second.at[(self.z + step) % 8], self.got_second.at[self.z],
                self.sends, self.recvs, 8 + step, self.line[step - 1],
            )
            for step in range(1, 8)
        ]
        self.got_second[self.z] = self.second[self.z]
        self.copies = self.copies + more
        return more

    def finish(self):
        for copy in self.copies[7:]:
            copy.wait_recv()
        for copy in self.copies:
            copy.wait_send()
        return self.got_second[...].reshape(128, -1)


EXCHANGE_SCRATCH = [pltpu.VMEM((8, 16, 1152), jnp.bfloat16)] * 4 + [
    pltpu.SemaphoreType.DMA((16,)),
    pltpu.SemaphoreType.DMA((16,)),
]


class Gather:
    def __init__(self, own, full, cut, sends, recvs, local):
        self.own, self.full, self.cut = own, full, cut
        self.sends, self.recvs = sends, recvs
        self.hi, self.core, z, lo, self.x = place()
        hi, core, x = self.hi, self.core, self.x
        self.mine, self.far = hi * 2 + core, (1 - hi) * 2 + core
        self.twin = device(hi, 1 - core, z, lo, x)
        self.across = device(1 - hi, core, z, 1 - lo, x)
        self.right = device(hi, core, z, lo, (x + 1) % 4)
        self.left = device(hi, core, z, lo, (x + 3) % 4)
        self.copies = {}
        self.local = pltpu.make_async_copy(own, full.at[self.mine], local)

    def go(self, at, source, target, peer):
        self.copies[at] = send(source, target, self.sends, self.recvs, at, peer)

    def same(self, at, ref, peer):
        self.go(at, ref, ref, peer)

    def start(self):
        self.go(0, self.own.at[self.x], self.full.at[self.mine, self.x], self.across)
        self.go(1, self.own, self.full.at[self.mine], self.twin)
        self.local.start()

    def spread(self):
        self.copies[0].wait_recv()
        piece = self.full.at[self.far, self.x]
        self.same(2, piece, self.right)
        self.same(3, piece, self.left)
        self.same(4, piece, self.twin)

    def pass_on(self):
        cut, width = self.cut, self.full.shape[3]
        self.copies[2].wait_recv()
        from_left = (self.far, (self.x + 3) % 4)
        self.same(5, self.full.at[from_left + (slice(None), pl.ds(0, cut))], self.right)
        self.same(6, self.full.at[from_left], self.twin)
        self.copies[3].wait_recv()
        from_right = (self.far, (self.x + 1) % 4)
        self.same(7, self.full.at[from_right + (slice(None), pl.ds(cut, width - cut))], self.left)
        self.same(8, self.full.at[from_right], self.twin)

    def last(self):
        self.copies[5].wait_recv()
        self.copies[7].wait_recv()
        self.same(9, self.full.at[self.far, (self.x + 2) % 4], self.twin)

    def arrive(self):
        self.local.wait()
        for at in (1, 4, 6, 8, 9):
            self.copies[at].wait_recv()

    def finish(self):
        for copy in self.copies.values():
            copy.wait_send()


GATHER_SCRATCH = [
    pltpu.SemaphoreType.DMA((10,)), pltpu.SemaphoreType.DMA((10,)), pltpu.SemaphoreType.DMA
]


def front_kernel(
    mixed_ref, hidden_ref, proj_ref, qkv_ref, rows_ref, proj_full, qkv_full, *scratch
):
    proj = Gather(proj_ref, proj_full, 640, *scratch[:3])
    qkv = Gather(qkv_ref, qkv_full, 1792, *scratch[3:6])
    exchange = Exchange(*scratch[6:])
    meet([proj.twin, proj.across] + exchange.plane + exchange.line)
    proj.start()
    qkv.start()
    proj.spread()
    proj.pass_on()
    proj.last()
    proj.arrive()
    weight = proj_full[...].reshape(-1, proj_full.shape[3])
    resid = hidden_ref[...].astype(jnp.float32) + jnp.dot(
        mixed_ref[...], weight, preferred_element_type=jnp.float32
    )
    exchange.start_plane(resid.astype(jnp.bfloat16))
    qkv.spread()
    exchange.start_line()
    qkv.pass_on()
    qkv.last()
    rows_ref[...] = exchange.finish()
    qkv.arrive()
    proj.finish()
    qkv.finish()


def front(mixed, hidden, proj, qkv):
    def whole(weight):
        return jax.ShapeDtypeStruct((4,) + weight.shape, weight.dtype)

    vmem, anywhere = pl.BlockSpec(memory_space=pltpu.VMEM), pl.BlockSpec(memory_space=pl.ANY)
    return pl.pallas_call(
        front_kernel,
        out_shape=(
            jax.ShapeDtypeStruct(hidden.shape, jnp.bfloat16), whole(proj), whole(qkv)
        ),
        in_specs=[vmem, vmem, anywhere, anywhere],
        out_specs=(vmem, vmem, anywhere),
        scratch_shapes=GATHER_SCRATCH + GATHER_SCRATCH + EXCHANGE_SCRATCH,
        compiler_params=pltpu.CompilerParams(
            collective_id=1, has_side_effects=True, vmem_limit_bytes=24 * 1024 * 1024
        ),
    )(mixed, hidden, proj, qkv)


def back_kernel(rows_ref, sums_ref, out_ref, total_ref, plane_sums, line_sums, *scratch):
    sum_sends, sum_recvs = scratch[:2]
    exchange = Exchange(*scratch[2:])
    z, group = exchange.z, exchange.group
    meet(exchange.plane + exchange.line)
    exchange.start_plane(rows_ref[...])
    copies = [
        send(sums_ref, plane_sums.at[group], sum_sends, sum_recvs, step, exchange.plane[step - 1])
        for step in range(1, 8)
    ]
    plane_sums[group] = sums_ref[...]
    exchange.start_line()
    for copy in copies:
        copy.wait_recv()
    line_sums[z] = jnp.sum(plane_sums[...], axis=0)
    more = [
        send(
            line_sums.at[z], line_sums.at[z], sum_sends, sum_recvs, 8 + step,
            exchange.line[step - 1],
        )
        for step in range(1, 8)
    ]
    out_ref[...] = exchange.finish()
    for copy in more:
        copy.wait_recv()
    total_ref[...] = jnp.sum(line_sums[...], axis=0)
    for copy in copies + more:
        copy.wait_send()


def back(rows, sums):
    vmem = pl.BlockSpec(memory_space=pltpu.VMEM)
    return pl.pallas_call(
        back_kernel,
        out_shape=(
            jax.ShapeDtypeStruct(rows.shape, rows.dtype),
            jax.ShapeDtypeStruct(sums.shape, sums.dtype),
        ),
        in_specs=[vmem] * 2,
        out_specs=(vmem, vmem),
        scratch_shapes=[
            pltpu.VMEM((8,) + sums.shape, sums.dtype),
            pltpu.VMEM((8,) + sums.shape, sums.dtype),
            pltpu.SemaphoreType.DMA((16,)),
            pltpu.SemaphoreType.DMA((16,)),
        ] + EXCHANGE_SCRATCH,
        compiler_params=pltpu.CompilerParams(
            collective_id=2, has_side_effects=True, vmem_limit_bytes=16 * 1024 * 1024
        ),
    )(rows, sums)


def pad_rows(weight):
    return jnp.pad(weight.reshape(4, -1, weight.shape[1]), ((0, 0), (0, 8), (0, 0)))


def pad_columns(rows):
    count = rows.shape[0]
    return jnp.pad(rows.reshape(count, 16, -1), ((0, 0), (0, 0), (0, 8))).reshape(count, -1)


def cut_columns(rows):
    count = rows.shape[0]
    return rows.reshape(count, 16, -1)[:, :, :-8].reshape(count, -1)


def body(
    hidden,
    query_space,
    key_space,
    value_space,
    positions,
    proj_space,
    shift_time,
    scale_time,
    qkv_time,
    grad_attn_time,
    grad_resid,
):
    frames_dev, spot_count, model_width = (hidden.shape[1], hidden.shape[2], hidden.shape[3])
    frames, spots_dev = (grad_attn_time.shape[1], grad_attn_time.shape[2])
    head_count = HEADS
    head_size = model_width // head_count
    token_count = frames * spots_dev
    seq_place = lax.axis_index("seq")
    row_places = lax.dynamic_slice_in_dim(positions[1, 0], seq_place * frames_dev, frames_dev, 0)
    col_places = lax.dynamic_slice_in_dim(positions[2, 0], seq_place * frames_dev, frames_dev, 0)
    frame_places = lax.dynamic_slice_in_dim(positions[0, 0], seq_place * spots_dev, spots_dev, 1).T
    per_frame = (frames_dev, spot_count, head_count, head_size)
    space_query = rotate_space(
        query_space.reshape(per_frame).astype(jnp.float32), row_places, col_places, 1.0
    ).astype(jnp.bfloat16)
    space_key = rotate_space(
        key_space.reshape(per_frame).astype(jnp.float32), row_places, col_places, 1.0
    ).astype(jnp.bfloat16)
    space_value = value_space.reshape(per_frame)
    space_weights, space_rounded, space_out = attend(space_query, space_key, space_value)
    space_mixed = space_out.astype(jnp.bfloat16).reshape(frames_dev * spot_count, model_width)
    resid_space, proj_full, qkv_full = front(
        pad_columns(space_mixed), hidden.reshape(-1, model_width), pad_rows(proj_space), pad_rows(qkv_time)
    )
    proj_full = proj_full.reshape(-1, model_width)
    qkv_full = qkv_full.reshape(-1, qkv_time.shape[1])
    resid_wide = resid_space.astype(jnp.float32)
    centered = resid_wide - jnp.mean(resid_wide, axis=-1, keepdims=True)
    inverse = lax.rsqrt(jnp.mean(centered * centered, axis=-1, keepdims=True) + epsilon)
    normed = centered * inverse
    modulated = (normed * (1.0 + scale_time) + shift_time).astype(jnp.bfloat16)
    projected = add_columns(pad_columns(modulated), qkv_full)

    def arrange(values):
        return jnp.transpose(values.reshape(frames, spots_dev, head_count, head_size), (1, 0, 2, 3))

    def restore(values):
        return jnp.transpose(values, (1, 0, 2, 3)).reshape(token_count, model_width)

    time_query = rotate(arrange(projected[:, :model_width]), frame_places, 1.0).astype(jnp.bfloat16)
    time_key = rotate(
        arrange(projected[:, model_width : 2 * model_width]), frame_places, 1.0
    ).astype(jnp.bfloat16)
    time_value = arrange(projected[:, 2 * model_width :]).astype(jnp.bfloat16)
    time_weights, time_rounded, time_out = attend(time_query, time_key, time_value)
    grad_time = arrange(grad_attn_time.reshape(token_count, model_width))
    grad_time_query, grad_time_key, grad_time_value = attend_back(
        time_query, time_key, time_value, time_weights, time_rounded, time_out, grad_time
    )
    grad_projected = jnp.concatenate(
        [
            restore(rotate(grad_time_query, frame_places, -1.0)),
            restore(rotate(grad_time_key, frame_places, -1.0)),
            restore(grad_time_value),
        ],
        axis=-1,
    ).astype(jnp.bfloat16)
    grad_modulated = cut_columns(place_columns(grad_projected, qkv_full))
    sums = jnp.stack([jnp.sum(grad_modulated, axis=0), jnp.sum(grad_modulated * normed, axis=0)])
    grad_normed = grad_modulated * (1.0 + scale_time)
    resid_back = (
        (
            grad_normed
            - jnp.mean(grad_normed, axis=-1, keepdims=True)
            - normed * jnp.mean(grad_normed * normed, axis=-1, keepdims=True)
        )
        * inverse
    ).astype(jnp.bfloat16)
    back_frames, sums = back(resid_back, sums.reshape(8, -1))
    sums = sums.reshape(2, model_width)
    grad_shift, grad_scale = sums[:1], sums[1:]
    grad_hidden = (
        grad_resid.astype(jnp.float32) + back_frames.reshape(grad_resid.shape).astype(jnp.float32)
    ).astype(jnp.bfloat16)
    grad_flat = grad_hidden.reshape(-1, model_width)
    grad_space_out = cut_columns(
        place_columns(grad_flat, proj_full).astype(jnp.bfloat16)
    ).reshape(per_frame)
    grad_space_query, grad_space_key, grad_space_value = attend_back(
        space_query, space_key, space_value, space_weights, space_rounded, space_out, grad_space_out
    )
    full_shape = hidden.shape
    grad_query = (
        rotate_space(grad_space_query, row_places, col_places, -1.0)
        .astype(jnp.bfloat16)
        .reshape(full_shape)
    )
    grad_key = (
        rotate_space(grad_space_key, row_places, col_places, -1.0)
        .astype(jnp.bfloat16)
        .reshape(full_shape)
    )
    grad_value = grad_space_value.astype(jnp.bfloat16).reshape(full_shape)
    grad_proj_space, grad_qkv_time = weight_gradients(
        grad_projected, modulated, grad_flat, space_mixed
    )
    return (
        grad_hidden,
        grad_query,
        grad_key,
        grad_value,
        grad_proj_space,
        grad_qkv_time,
        grad_shift,
        grad_scale,
    )


def solution(mesh):
    in_specs = (
        P("dp", "seq", None, None),
        P("dp", "seq", None, None),
        P("dp", "seq", None, None),
        P("dp", "seq", None, None),
        P(None, "dp", None, None),
        P("dp", None),
        P("dp", None),
        P("dp", None),
        P("dp", None),
        P("dp", None, "seq", None),
        P("dp", "seq", None, None),
    )
    out_specs = (
        P("dp", "seq", None, None),
        P("dp", "seq", None, None),
        P("dp", "seq", None, None),
        P("dp", "seq", None, None),
        P("dp", "seq"),
        P("dp", "seq"),
        P("dp", None),
        P("dp", None),
    )
    return jax.shard_map(body, mesh=mesh, in_specs=in_specs, out_specs=out_specs, check_vma=False)
```

```python
import math

import jax
import jax.numpy as jnp
from jax import lax
from jax.experimental import pallas as pl
from jax.experimental.pallas import tpu as pltpu
from jax.sharding import PartitionSpec as P

HEADS = 16


epsilon = 1e-06


MESH = pl.DeviceIdType.MESH

PIECE_ROWS = 80
HALF_LANES = 640
KEEP_LANES = 384
ORDER = ("x_near", "y_near", "x_far", "z_near")


def place():
    dp, seq = lax.axis_index("dp"), lax.axis_index("seq")
    hi, core = dp // 2, dp % 2
    z, lo, x = seq // 8, (seq // 4) % 2, seq % 4
    return hi, core, z, lo, x


def device(hi, core, z, lo, x):
    return (hi * 2 + core, z * 8 + lo * 4 + x)


def send(source, target, sends, recvs, at, peer):
    copy = pltpu.make_async_remote_copy(
        src_ref=source, dst_ref=target, send_sem=sends.at[at], recv_sem=recvs.at[at],
        device_id=peer, device_id_type=MESH,
    )
    copy.start()
    return copy


def meet(peers):
    barrier = pltpu.get_barrier_semaphore()
    for peer in peers:
        pl.semaphore_signal(barrier, inc=1, device_id=peer, device_id_type=MESH)
    pl.semaphore_wait(barrier, len(peers))


def order_of(group):
    return [ORDER[(group + step) % 4] for step in range(4)]


def piece_of(group, block):
    bits = {name: (block // (8 >> step)) % 2 for step, name in enumerate(order_of(group))}
    x = bits["x_far"] * 2 + (bits["x_near"] + bits["x_far"]) % 2
    return (group * 2 + bits["z_near"]) * 8 + bits["y_near"] * 4 + x


def sum_kernel(
    left_ref, right_ref, out_ref, twin_left, twin_right, work, got0, got1, got2, got3, last, final,
    twin_send, twin_recv, step_send, step_recv, final_send, final_recv,
):
    hi, core, z, lo, x = place()
    near, pair = z % 2, z // 2
    bits = {"x_near": (x % 2 + x // 2) % 2, "x_far": x // 2, "y_near": lo, "z_near": near}
    partners = {
        "x_near": device(hi, core, z, lo, x + 1 - 2 * (x % 2)),
        "x_far": device(hi, core, z, lo, 3 - x),
        "y_near": device(hi, core, z, 1 - lo, x),
        "z_near": device(hi, core, z + 1 - 2 * near, lo, x),
    }
    twin = device(hi, 1 - core, z, lo, x)
    others = []
    for step_hi in range(2):
        for step_pair in range(4):
            if step_hi + step_pair > 0:
                to_hi, to_pair = (hi + step_hi) % 2, (pair + step_pair) % 4
                others.append(
                    (step_hi * 4 + step_pair, to_hi, to_pair,
                     device(to_hi, core, to_pair * 2 + near, lo, x))
                )

    meet([twin] + list(partners.values()) + [other[3] for other in others])
    twin_copies = [
        send(right_ref.at[1 - core], twin_right, twin_send, twin_recv, 0, twin),
        send(left_ref, twin_left, twin_send, twin_recv, 1, twin),
    ]
    for copy in twin_copies:
        copy.wait_recv()

    got = [got0, got1, got2, got3]
    copies = {}

    def fill(group, start):
        def quarter(at, _):
            first = start + at * 4
            pieces = [piece_of(group, first + j) for j in range(4)]
            own = jnp.concatenate([left_ref[piece] for piece in pieces], axis=0)
            other = jnp.concatenate([twin_left[piece] for piece in pieces], axis=0)
            total = jnp.dot(own, right_ref[core], preferred_element_type=jnp.float32)
            total += jnp.dot(other, twin_right[...], preferred_element_type=jnp.float32)
            work[group, pl.ds(first, 4)] = total.astype(jnp.bfloat16).reshape(
                4, PIECE_ROWS, HALF_LANES
            )
            return 0

        lax.fori_loop(0, 2, quarter, 0)

    def take(group, step, start, count, offset):
        def one(at, _):
            total = work[group, start + at].astype(jnp.float32)
            total += got[step][group, offset + at].astype(jnp.float32)
            work[group, start + at] = total.astype(jnp.bfloat16)
            return 0

        lax.fori_loop(0, count, one, 0)

    base = [0, 0, 0, 0]
    for group in range(4):
        name = order_of(group)[0]
        away = (1 - bits[name]) * 8
        fill(group, away)
        copies[group, 0] = send(
            work.at[group, pl.ds(away, 8)], got[0].at[group],
            step_send, step_recv, (group, 0), partners[name],
        )
    for group in range(4):
        base[group] = bits[order_of(group)[0]] * 8
        fill(group, base[group])
    for step in range(1, 4):
        half = 8 >> step
        for group in range(4):
            name = order_of(group)[step]
            away = (1 - bits[name]) * half
            copies[group, step - 1].wait_recv()
            take(group, step - 1, base[group] + away, half, away)
            copies[group, step] = send(
                work.at[group, pl.ds(base[group] + away, half)], got[step].at[group],
                step_send, step_recv, (group, step), partners[name],
            )
            mine = bits[name] * half
            take(group, step - 1, base[group] + mine, half, mine)
            base[group] = base[group] + mine
    for group in range(4):
        copies[group, 3].wait_recv()
        total = work[group, base[group]].astype(jnp.float32) + got3[group, 0].astype(jnp.float32)
        total = total.astype(jnp.bfloat16)
        last[group, 0] = total[:, :KEEP_LANES]
        last[group, 1] = total[:, HALF_LANES - KEEP_LANES :]
    ends = []
    for slot, to_hi, to_pair, peer in others:
        ends.append(
            send(
                last.at[to_pair, to_hi], final.at[slot], final_send, final_recv, slot, peer
            )
        )
    total = last[pair, hi].astype(jnp.float32)
    for (slot, _, _, _), copy in zip(others, ends):
        copy.wait_recv()
        total += final[slot].astype(jnp.float32)
    out_ref[...] = total
    for copy in twin_copies + list(copies.values()) + ends:
        copy.wait_send()


def sum_products(left, right):
    depth = left.shape[2]
    block = (PIECE_ROWS, HALF_LANES)
    return pl.pallas_call(
        sum_kernel,
        out_shape=jax.ShapeDtypeStruct((PIECE_ROWS, KEEP_LANES), jnp.float32),
        in_specs=[pl.BlockSpec(memory_space=pltpu.VMEM)] * 2,
        out_specs=pl.BlockSpec(memory_space=pltpu.VMEM),
        scratch_shapes=[
            pltpu.VMEM(left.shape, jnp.bfloat16),
            pltpu.VMEM((depth, HALF_LANES), jnp.bfloat16),
            pltpu.VMEM((4, 16) + block, jnp.bfloat16),
            pltpu.VMEM((4, 8) + block, jnp.bfloat16),
            pltpu.VMEM((4, 4) + block, jnp.bfloat16),
            pltpu.VMEM((4, 2) + block, jnp.bfloat16),
            pltpu.VMEM((4, 1) + block, jnp.bfloat16),
            pltpu.VMEM((4, 2, PIECE_ROWS, KEEP_LANES), jnp.bfloat16),
            pltpu.VMEM((8, PIECE_ROWS, KEEP_LANES), jnp.bfloat16),
            pltpu.SemaphoreType.DMA((2,)),
            pltpu.SemaphoreType.DMA((2,)),
            pltpu.SemaphoreType.DMA((4, 4)),
            pltpu.SemaphoreType.DMA((4, 4)),
            pltpu.SemaphoreType.DMA((8,)),
            pltpu.SemaphoreType.DMA((8,)),
        ],
        compiler_params=pltpu.CompilerParams(
            collective_id=3, has_side_effects=True, vmem_limit_bytes=40 * 1024 * 1024
        ),
    )(left, right)


def weight_gradients(grad_projected, modulated, grad_flat, space_mixed):
    tokens, width = modulated.shape
    qkv_rows = grad_projected.T.reshape(64, -1, tokens)
    proj_rows = grad_flat.T.reshape(64, -1, tokens)
    n_qkv, n_proj = qkv_rows.shape[1], proj_rows.shape[1]
    left = jnp.concatenate(
        [
            jnp.pad(qkv_rows, ((0, 0), (0, PIECE_ROWS - n_qkv), (0, 0))),
            jnp.pad(proj_rows, ((0, 0), (n_qkv, PIECE_ROWS - n_qkv - n_proj), (0, 0))),
        ],
        axis=2,
    )
    part = width // 4
    right = jnp.concatenate([modulated, space_mixed], axis=0).reshape(2 * tokens, 2, 2, part)
    right = jnp.transpose(right, (2, 0, 1, 3)).reshape(2, 2 * tokens, 2 * part)
    right = jnp.pad(right, ((0, 0), (0, 0), (0, HALF_LANES - 2 * part)))
    summed = sum_products(left, right)
    hi = lax.axis_index("dp") // 2
    start = hi * (part + KEEP_LANES - HALF_LANES)
    kept = lax.dynamic_slice(summed, (0, start), (n_qkv + n_proj, part)).T
    return kept[:, n_qkv:], kept[:, :n_qkv]


def near_peers():
    hi, core, z, lo, x = place()
    group = lo * 4 + x
    plane = [(hi * 2 + core, z * 8 + (group + step) % 8) for step in range(1, 8)]
    line = [(hi * 2 + core, ((z + step) % 8) * 8 + group) for step in range(1, 8)]
    return plane, line


def swap_eights(rows):
    count = rows.shape[0]
    at = lax.broadcasted_iota(jnp.int32, (count, count), 0)
    origin = lax.broadcasted_iota(jnp.int32, (count, count), 1)
    wanted = (at // 2 % 8) * 16 + at // 16 * 2 + at % 2
    chosen = jnp.where(origin == wanted, 1.0, 0.0).astype(jnp.bfloat16)
    moved = jnp.dot(chosen, rows, preferred_element_type=jnp.float32)
    return moved.astype(jnp.bfloat16)


class Exchange:
    def __init__(self, first, got_first, second, got_second, sends, recvs):
        self.first, self.got_first = first, got_first
        self.second, self.got_second = second, got_second
        self.sends, self.recvs = sends, recvs
        self.plane, self.line = near_peers()
        _, _, self.z, lo, x = place()
        self.group = lo * 4 + x

    def start_plane(self, rows):
        self.first[...] = swap_eights(rows).reshape(self.first.shape)
        self.copies = [
            send(
                self.first.at[(self.group + step) % 8], self.got_first.at[self.group],
                self.sends, self.recvs, step, self.plane[step - 1],
            )
            for step in range(1, 8)
        ]
        self.got_first[self.group] = self.first[self.group]

    def start_line(self):
        for copy in self.copies:
            copy.wait_recv()
        rows = self.got_first[...].reshape(128, -1)
        self.second[...] = swap_eights(rows).reshape(self.second.shape)
        more = [
            send(
                self.second.at[(self.z + step) % 8], self.got_second.at[self.z],
                self.sends, self.recvs, 8 + step, self.line[step - 1],
            )
            for step in range(1, 8)
        ]
        self.got_second[self.z] = self.second[self.z]
        self.copies = self.copies + more
        return more

    def finish(self):
        for copy in self.copies[7:]:
            copy.wait_recv()
        for copy in self.copies:
            copy.wait_send()
        return self.got_second[...].reshape(128, -1)


EXCHANGE_SCRATCH = [pltpu.VMEM((8, 16, 1152), jnp.bfloat16)] * 4 + [
    pltpu.SemaphoreType.DMA((16,)),
    pltpu.SemaphoreType.DMA((16,)),
]


class Gather:
    def __init__(self, own, full, cut, sends, recvs, local):
        self.own, self.full, self.cut = own, full, cut
        self.sends, self.recvs, self.local = sends, recvs, local
        self.hi, self.core, z, lo, self.x = place()
        hi, core, x = self.hi, self.core, self.x
        self.mine, self.far = hi * 2 + core, (1 - hi) * 2 + core
        self.twin = device(hi, 1 - core, z, lo, x)
        self.across = device(1 - hi, core, z, 1 - lo, x)
        self.right = device(hi, core, z, lo, (x + 1) % 4)
        self.left = device(hi, core, z, lo, (x + 3) % 4)
        self.copies = {}

    def go(self, at, source, target, peer):
        self.copies[at] = send(source, target, self.sends, self.recvs, at, peer)

    def same(self, at, ref, peer):
        self.go(at, ref, ref, peer)

    def start(self):
        start = pl.multiple_of(self.x * 64 + self.x // 2 * 16, 16)
        self.go(0, self.own.at[pl.ds(start, 80)], self.full.at[self.mine, self.x], self.across)
        self.locals = []
        for quarter, first in enumerate(STARTS):
            source, target = self.own.at[pl.ds(first, 80)], self.full.at[self.mine, quarter]
            self.go(10 + quarter, source, target, self.twin)
            copy = pltpu.make_async_copy(source, target, self.local.at[quarter])
            copy.start()
            self.locals.append(copy)

    def spread(self):
        self.copies[0].wait_recv()
        piece = self.full.at[self.far, self.x]
        self.same(2, piece, self.right)
        self.same(3, piece, self.left)
        self.same(4, piece, self.twin)

    def pass_on(self):
        cut, width = self.cut, self.full.shape[3]
        self.copies[2].wait_recv()
        from_left = (self.far, (self.x + 3) % 4)
        self.same(5, self.full.at[from_left + (slice(None), pl.ds(0, cut))], self.right)
        self.same(6, self.full.at[from_left], self.twin)
        self.copies[3].wait_recv()
        from_right = (self.far, (self.x + 1) % 4)
        self.same(7, self.full.at[from_right + (slice(None), pl.ds(cut, width - cut))], self.left)
        self.same(8, self.full.at[from_right], self.twin)

    def last(self):
        self.copies[5].wait_recv()
        self.copies[7].wait_recv()
        self.same(9, self.full.at[self.far, (self.x + 2) % 4], self.twin)

    def arrive(self):
        for copy in self.locals:
            copy.wait()
        for at in (4, 6, 8, 9, 10, 11, 12, 13):
            self.copies[at].wait_recv()

    def finish(self):
        for copy in self.copies.values():
            copy.wait_send()


STARTS = (0, 64, 144, 208)
GATHER_SCRATCH = [
    pltpu.SemaphoreType.DMA((14,)), pltpu.SemaphoreType.DMA((14,)), pltpu.SemaphoreType.DMA((4,))
]


def weight_rows(full, columns):
    return jnp.concatenate(
        [
            full[block, quarter, 16 * (quarter % 2) : 80, columns]
            for block in range(4)
            for quarter in range(4)
        ],
        axis=0,
    )


WIDTH = 1152
HEAD = WIDTH // HEADS
FACTOR = 1.0 / math.sqrt(HEAD)


def across_rows(left, right):
    return lax.dot_general(
        left, right, (((1,), (1,)), ((), ())), preferred_element_type=jnp.float32
    )


def down_rows(left, right):
    return lax.dot_general(
        left, right, (((0,), (0,)), ((), ())), preferred_element_type=jnp.float32
    )


def turn_tables(angles, half):
    lane = lax.broadcasted_iota(jnp.int32, (1, WIDTH), 1) % HEAD
    first = lane % (2 * half) < half
    origin = lane // (2 * half) * half + lane % half
    row = lax.broadcasted_iota(jnp.int32, (128, WIDTH), 0)
    cosine_at = jnp.where(row == origin, 1.0, 0.0).astype(jnp.bfloat16)
    sine_at = jnp.where(row == origin + 36, 1.0, 0.0) * jnp.where(first, -1.0, 1.0)
    sine_at = sine_at.astype(jnp.bfloat16)
    cosine = jnp.zeros((128, WIDTH), jnp.float32)
    sine = jnp.zeros((128, WIDTH), jnp.float32)
    rest = angles
    for _ in range(3):
        part = rest.astype(jnp.bfloat16)
        rest = rest - part.astype(jnp.float32)
        cosine += jnp.dot(part, cosine_at, preferred_element_type=jnp.float32)
        sine += jnp.dot(part, sine_at, preferred_element_type=jnp.float32)
    return cosine, sine


def turn(values, cosine, sine, half, direction):
    lane = lax.broadcasted_iota(jnp.int32, (1, WIDTH), 1) % (2 * half)
    partner = jnp.where(
        lane < half, pltpu.roll(values, WIDTH - half, 1), pltpu.roll(values, half, 1)
    )
    return values * cosine + partner * (sine * direction)


def head_window(head):
    start = min(head * HEAD // 128 * 128, WIDTH - 256)
    lane = lax.broadcasted_iota(jnp.int32, (1, 256), 1) + start
    mask = jnp.where((lane >= head * HEAD) & (lane < (head + 1) * HEAD), 1.0, 0.0)
    return slice(start, start + 256), mask.astype(jnp.bfloat16)


def softmax_rows(scores):
    exponent = jnp.exp(scores - jnp.max(scores, axis=-1, keepdims=True))
    return exponent / jnp.sum(exponent, axis=-1, keepdims=True)


def head_back(weights, query, key, value, grad, mask):
    grad = grad * mask
    rounded = weights.astype(jnp.bfloat16)
    grad_weights = across_rows(grad, value)
    delta = jnp.sum(rounded.astype(jnp.float32) * grad_weights, axis=-1, keepdims=True)
    scores = (weights * (grad_weights - delta) * FACTOR).astype(jnp.bfloat16)
    return (
        jnp.dot(scores, key * mask, preferred_element_type=jnp.float32),
        down_rows(scores, query * mask),
        down_rows(rounded, grad),
    )


def space_forward(query_ref, key_ref, value_ref, angles_ref, turned_query, turned_key, weights_ref, mixed):
    cosine, sine = turn_tables(angles_ref[...], HEAD // 4)
    for source, target in ((query_ref, turned_query), (key_ref, turned_key)):
        values = source[...].astype(jnp.float32)
        target[...] = turn(values, cosine, sine, HEAD // 4, 1.0).astype(jnp.bfloat16)
    mixed[...] = jnp.zeros_like(mixed)
    for head in range(HEADS):
        window, mask = head_window(head)
        scores = across_rows(turned_query[:, window] * mask, turned_key[:, window]) * FACTOR
        weights = softmax_rows(scores)
        weights_ref[head] = weights
        mixed[:, window] += jnp.dot(
            weights.astype(jnp.bfloat16), value_ref[:, window] * mask,
            preferred_element_type=jnp.float32,
        )


def space_back_kernel(
    back_ref, resid_ref, proj_full, query_ref, key_ref, value_ref, weights_ref, angles_ref,
    hidden_out, query_out, key_out, value_out, total_query, total_key, total_value, grad,
):
    hidden = resid_ref[...].astype(jnp.float32) + back_ref[...].astype(jnp.float32)
    hidden = hidden.astype(jnp.bfloat16)
    hidden_out[...] = hidden
    for block in range(3):
        columns = slice(block * 384, block * 384 + 384)
        part = across_rows(hidden[:, columns], weight_rows(proj_full, columns))
        if block == 0:
            total_query[...] = part
        else:
            total_query[...] += part
    grad[...] = total_query[...].astype(jnp.bfloat16)
    totals = (total_query, total_key, total_value)
    for total in totals:
        total[...] = jnp.zeros_like(total)
    for head in range(HEADS):
        window, mask = head_window(head)
        parts = head_back(
            weights_ref[head], query_ref[:, window], key_ref[:, window], value_ref[:, window],
            grad[:, window], mask,
        )
        for total, part in zip(totals, parts):
            total[:, window] += part
    cosine, sine = turn_tables(angles_ref[...], HEAD // 4)
    for total, out in ((total_query, query_out), (total_key, key_out)):
        out[...] = turn(total[...], cosine, sine, HEAD // 4, -1.0).astype(jnp.bfloat16)
    value_out[...] = total_value[...].astype(jnp.bfloat16)


def local_call(kernel, outs, scratch, megabytes, *args):
    return pl.pallas_call(
        kernel,
        out_shape=tuple(jax.ShapeDtypeStruct(shape, kind) for shape, kind in outs),
        in_specs=[pl.BlockSpec(memory_space=pltpu.VMEM)] * len(args),
        out_specs=tuple(pl.BlockSpec(memory_space=pltpu.VMEM) for _ in outs),
        scratch_shapes=[pltpu.VMEM(shape, kind) for shape, kind in scratch],
        compiler_params=pltpu.CompilerParams(vmem_limit_bytes=megabytes * 1024 * 1024),
    )(*args)


ROWS = ((128, WIDTH), jnp.bfloat16)
WIDE_ROWS = ((128, WIDTH), jnp.float32)


def space_back(*args):
    return local_call(
        space_back_kernel, [ROWS] * 4, [WIDE_ROWS] * 3 + [ROWS], 24, *args
    )


def time_kernel(
    rows_ref, qkv_full, scale_ref, shift_ref, grad_ref, angles_ref,
    modulated_ref, projected_ref, back_ref, sums_ref,
    normed_ref, wide, turned, total_back,
):
    rows = rows_ref[...].astype(jnp.float32)
    centered = rows - jnp.mean(rows, axis=-1, keepdims=True)
    inverse = lax.rsqrt(jnp.mean(centered * centered, axis=-1, keepdims=True) + epsilon)
    normed = centered * inverse
    normed_ref[...] = normed
    scale = 1.0 + scale_ref[...]
    modulated_ref[...] = (normed * scale + shift_ref[...]).astype(jnp.bfloat16)
    for block in range(9):
        columns = slice(block * 384, block * 384 + 384)
        wide[:, columns] = jnp.dot(
            modulated_ref[...], weight_rows(qkv_full, columns), preferred_element_type=jnp.float32
        )
    cosine, sine = turn_tables(angles_ref[...], HEAD // 2)
    for block in range(2):
        columns = slice(block * WIDTH, block * WIDTH + WIDTH)
        turned[:, columns] = turn(wide[:, columns], cosine, sine, HEAD // 2, 1.0).astype(jnp.bfloat16)
    turned[:, 2 * WIDTH :] = wide[:, 2 * WIDTH :].astype(jnp.bfloat16)
    wide[...] = jnp.zeros_like(wide)
    spot_row = lax.broadcasted_iota(jnp.int32, (128, 128), 0) % 2
    spot_column = lax.broadcasted_iota(jnp.int32, (128, 128), 1) % 2
    together = spot_row == spot_column
    for head in range(HEADS):
        window, mask = head_window(head)
        windows = [slice(window.start + WIDTH * j, window.stop + WIDTH * j) for j in range(3)]
        query, key, value = [turned[:, columns] for columns in windows]
        scores = across_rows(query * mask, key) * FACTOR
        weights = softmax_rows(jnp.where(together, scores, -jnp.inf))
        parts = head_back(weights, query, key, value, grad_ref[:, window], mask)
        for columns, part in zip(windows, parts):
            wide[:, columns] += part
    for block in range(2):
        columns = slice(block * WIDTH, block * WIDTH + WIDTH)
        projected_ref[:, columns] = turn(wide[:, columns], cosine, sine, HEAD // 2, -1.0).astype(
            jnp.bfloat16
        )
    projected_ref[:, 2 * WIDTH :] = wide[:, 2 * WIDTH :].astype(jnp.bfloat16)
    for block in range(9):
        columns = slice(block * 384, block * 384 + 384)
        part = across_rows(projected_ref[:, columns], weight_rows(qkv_full, columns))
        if block == 0:
            total_back[...] = part
        else:
            total_back[...] += part
    grad = total_back[...]
    normed = normed_ref[...]
    sums_ref[...] = jnp.concatenate(
        [
            jnp.sum(grad, axis=0, keepdims=True),
            jnp.sum(grad * normed, axis=0, keepdims=True),
            jnp.zeros((6, WIDTH), jnp.float32),
        ],
        axis=0,
    )
    grad = grad * scale
    back_ref[...] = (
        (
            grad
            - jnp.mean(grad, axis=-1, keepdims=True)
            - normed * jnp.mean(grad * normed, axis=-1, keepdims=True)
        )
        * inverse
    ).astype(jnp.bfloat16)


def time_sublayer(*args):
    wide = (128, 3 * WIDTH)
    return local_call(
        time_kernel,
        [ROWS, (wide, jnp.bfloat16), ROWS, ((8, WIDTH), jnp.float32)],
        [WIDE_ROWS, (wide, jnp.float32), (wide, jnp.bfloat16), WIDE_ROWS],
        40,
        *args,
    )


def front_kernel(
    query_ref, key_ref, value_ref, hidden_ref, angles_ref, proj_ref, qkv_ref,
    rows_ref, mixed_ref, turned_query, turned_key, weights_ref, proj_full, qkv_full,
    wide, *scratch,
):
    proj = Gather(proj_ref, proj_full, 640, *scratch[:3])
    qkv = Gather(qkv_ref, qkv_full, 1792, *scratch[3:6])
    exchange = Exchange(*scratch[6:])
    meet([proj.twin, proj.across] + exchange.plane + exchange.line)
    proj.start()
    qkv.start()
    proj.spread()
    space_forward(
        query_ref, key_ref, value_ref, angles_ref, turned_query, turned_key, weights_ref, wide
    )
    mixed_ref[...] = wide[...].astype(jnp.bfloat16)
    proj.pass_on()
    proj.last()
    proj.arrive()
    for block in range(3):
        columns = slice(block * 384, block * 384 + 384)
        wide[:, columns] = hidden_ref[:, columns].astype(jnp.float32) + jnp.dot(
            mixed_ref[...], weight_rows(proj_full, columns), preferred_element_type=jnp.float32
        )
    exchange.start_plane(wide[...].astype(jnp.bfloat16))
    qkv.spread()
    exchange.start_line()
    qkv.pass_on()
    qkv.last()
    rows_ref[...] = exchange.finish()
    qkv.arrive()
    proj.finish()
    qkv.finish()


def front(query, key, value, hidden, angles, proj, qkv):
    def whole(weight):
        return jax.ShapeDtypeStruct((4, 4, 80, weight.shape[1]), weight.dtype)

    vmem, anywhere = pl.BlockSpec(memory_space=pltpu.VMEM), pl.BlockSpec(memory_space=pl.ANY)
    rows = jax.ShapeDtypeStruct(*ROWS)
    return pl.pallas_call(
        front_kernel,
        out_shape=(
            rows, rows, rows, rows, jax.ShapeDtypeStruct((HEADS, 128, 128), jnp.float32),
            whole(proj), whole(qkv),
        ),
        in_specs=[vmem] * 5 + [anywhere] * 2,
        out_specs=(vmem,) * 7,
        scratch_shapes=[pltpu.VMEM(*WIDE_ROWS)] + GATHER_SCRATCH * 2 + EXCHANGE_SCRATCH,
        compiler_params=pltpu.CompilerParams(
            collective_id=1, has_side_effects=True, vmem_limit_bytes=32 * 1024 * 1024
        ),
    )(query, key, value, hidden, angles, proj, qkv)


def back_kernel(rows_ref, sums_ref, out_ref, total_ref, plane_sums, line_sums, *scratch):
    sum_sends, sum_recvs = scratch[:2]
    exchange = Exchange(*scratch[2:])
    z, group = exchange.z, exchange.group
    meet(exchange.plane + exchange.line)
    exchange.start_plane(rows_ref[...])
    copies = [
        send(sums_ref, plane_sums.at[group], sum_sends, sum_recvs, step, exchange.plane[step - 1])
        for step in range(1, 8)
    ]
    plane_sums[group] = sums_ref[...]
    exchange.start_line()
    for copy in copies:
        copy.wait_recv()
    line_sums[z] = jnp.sum(plane_sums[...], axis=0)
    more = [
        send(
            line_sums.at[z], line_sums.at[z], sum_sends, sum_recvs, 8 + step,
            exchange.line[step - 1],
        )
        for step in range(1, 8)
    ]
    out_ref[...] = exchange.finish()
    for copy in more:
        copy.wait_recv()
    total_ref[...] = jnp.sum(line_sums[...], axis=0)
    for copy in copies + more:
        copy.wait_send()


def back(rows, sums):
    vmem = pl.BlockSpec(memory_space=pltpu.VMEM)
    return pl.pallas_call(
        back_kernel,
        out_shape=(
            jax.ShapeDtypeStruct(rows.shape, rows.dtype),
            jax.ShapeDtypeStruct(sums.shape, sums.dtype),
        ),
        in_specs=[vmem] * 2,
        out_specs=(vmem, vmem),
        scratch_shapes=[
            pltpu.VMEM((8,) + sums.shape, sums.dtype),
            pltpu.VMEM((8,) + sums.shape, sums.dtype),
            pltpu.SemaphoreType.DMA((16,)),
            pltpu.SemaphoreType.DMA((16,)),
        ] + EXCHANGE_SCRATCH,
        compiler_params=pltpu.CompilerParams(
            collective_id=2, has_side_effects=True, vmem_limit_bytes=16 * 1024 * 1024
        ),
    )(rows, sums)


def turn_angles(places, half):
    frequency = 10000.0 ** (-jnp.arange(half, dtype=jnp.float32) / half)
    angles = (places.astype(jnp.float32)[:, :, None] * frequency).reshape(128, 36)
    return jnp.pad(jnp.concatenate([jnp.cos(angles), jnp.sin(angles)], axis=1), ((0, 0), (0, 56)))


def body(
    hidden,
    query_space,
    key_space,
    value_space,
    positions,
    proj_space,
    shift_time,
    scale_time,
    qkv_time,
    grad_attn_time,
    grad_resid,
):
    seq_place = lax.axis_index("seq")
    frame_places = lax.dynamic_slice_in_dim(positions[0, 0], seq_place * 2, 2, 1).reshape(128, 1)
    spot_places = lax.dynamic_slice_in_dim(positions[1:, 0], seq_place, 1, 1).reshape(2, 128).T
    space_angles = turn_angles(spot_places, HEAD // 4)
    time_angles = turn_angles(frame_places, HEAD // 2)

    def flat(values):
        return values.reshape(128, WIDTH)

    rows, space_mixed, space_query, space_key, space_weights, proj_full, qkv_full = front(
        flat(query_space), flat(key_space), flat(value_space), flat(hidden), space_angles,
        proj_space, qkv_time,
    )
    modulated, grad_projected, resid_back, sums = time_sublayer(
        rows, qkv_full, scale_time, shift_time, flat(grad_attn_time), time_angles
    )
    back_frames, sums = back(resid_back, sums[:2].reshape(8, -1))
    sums = sums.reshape(2, WIDTH)
    grad_hidden, grad_query, grad_key, grad_value = space_back(
        back_frames, flat(grad_resid), proj_full, space_query, space_key, flat(value_space),
        space_weights, space_angles,
    )
    grad_proj_space, grad_qkv_time = weight_gradients(
        grad_projected, modulated, grad_hidden, space_mixed
    )
    shape = hidden.shape
    return (
        grad_hidden.reshape(shape),
        grad_query.reshape(shape),
        grad_key.reshape(shape),
        grad_value.reshape(shape),
        grad_proj_space,
        grad_qkv_time,
        sums[:1],
        sums[1:],
    )


def solution(mesh):
    in_specs = (
        P("dp", "seq", None, None),
        P("dp", "seq", None, None),
        P("dp", "seq", None, None),
        P("dp", "seq", None, None),
        P(None, "dp", None, None),
        P("dp", None),
        P("dp", None),
        P("dp", None),
        P("dp", None),
        P("dp", None, "seq", None),
        P("dp", "seq", None, None),
    )
    out_specs = (
        P("dp", "seq", None, None),
        P("dp", "seq", None, None),
        P("dp", "seq", None, None),
        P("dp", "seq", None, None),
        P("dp", "seq"),
        P("dp", "seq"),
        P("dp", None),
        P("dp", None),
    )
    return jax.shard_map(body, mesh=mesh, in_specs=in_specs, out_specs=out_specs, check_vma=False)
```

```python
import math

import jax
import jax.numpy as jnp
from jax import lax
from jax.experimental import pallas as pl
from jax.experimental.pallas import tpu as pltpu
from jax.sharding import PartitionSpec as P

HEADS = 16


epsilon = 1e-06


MESH = pl.DeviceIdType.MESH

HALF_LANES = 640
KEEP_LANES = 384
ORDER = ("x_near", "y_near", "x_far", "z_near")
GROUPS = (
    (0, 0, 64, 0), (0, 64, 128, 1), (0, 128, 176, 2), (0, 176, 224, 3), (1, 0, 48, 2), (1, 48, 80, 3)
)
QKV_ROWS, PROJ_ROWS = 224, 80
QKV_WINDOW, PROJ_WINDOW = 80, 32


def place():
    dp, seq = lax.axis_index("dp"), lax.axis_index("seq")
    hi, core = dp // 2, dp % 2
    z, lo, x = seq // 8, (seq // 4) % 2, seq % 4
    return hi, core, z, lo, x


def device(hi, core, z, lo, x):
    return (hi * 2 + core, z * 8 + lo * 4 + x)


def send(source, target, sends, recvs, at, peer):
    copy = pltpu.make_async_remote_copy(
        src_ref=source, dst_ref=target, send_sem=sends.at[at], recv_sem=recvs.at[at],
        device_id=peer, device_id_type=MESH,
    )
    copy.start()
    return copy


def meet(peers):
    barrier = pltpu.get_barrier_semaphore()
    for peer in peers:
        pl.semaphore_signal(barrier, inc=1, device_id=peer, device_id_type=MESH)
    pl.semaphore_wait(barrier, len(peers))


def order_of(group):
    return [ORDER[(GROUPS[group][3] + step) % 4] for step in range(4)]


def combination(group, block):
    bits = {name: (block // (8 >> step)) % 2 for step, name in enumerate(order_of(group))}
    x = bits["x_far"] * 2 + (bits["x_near"] + bits["x_far"]) % 2
    return bits["z_near"] * 8 + bits["y_near"] * 4 + x


class Halving:
    def __init__(self, right, left, twin_left, work, got, sends, recvs):
        self.right, self.left, self.twin_left = right, left, twin_left
        self.work, self.got, self.sends, self.recvs = work, got, sends, recvs
        hi, core, z, lo, x = place()
        near = z % 2
        self.bits = {"x_near": (x % 2 + x // 2) % 2, "x_far": x // 2, "y_near": lo, "z_near": near}
        self.partners = {
            "x_near": device(hi, core, z, lo, x + 1 - 2 * (x % 2)),
            "x_far": device(hi, core, z, lo, 3 - x),
            "y_near": device(hi, core, z, 1 - lo, x),
            "z_near": device(hi, core, z + 1 - 2 * near, lo, x),
        }
        self.base = [0] * len(GROUPS)
        self.copies = {}

    def fill(self, group, start):
        kind, first_row, last_row, _ = GROUPS[group]
        count, rows = last_row - first_row, slice(first_row, last_row)
        left, other = self.left[kind], self.twin_left[kind]
        work, right = self.work[group], self.right[kind]

        def four(at, _):
            first = start + at * 4
            parts = []
            for j in range(4):
                block = combination(group, first + j)
                parts.append(jnp.concatenate([left[block, rows], other[block, rows]], axis=1))
            total = jnp.dot(
                jnp.concatenate(parts, axis=0), right[...], preferred_element_type=jnp.float32
            )
            work[pl.ds(first, 4)] = total.astype(jnp.bfloat16).reshape(4, count, HALF_LANES)
            return 0

        lax.fori_loop(0, 2, four, 0)

    def send(self, group, step, first):
        name = order_of(group)[step]
        self.copies[group, step] = send(
            self.work[group].at[pl.ds(first, 8 >> step)], self.got[group][step],
            self.sends, self.recvs, (group, step), self.partners[name],
        )

    def begin(self, group):
        bit = self.bits[order_of(group)[0]]
        self.fill(group, (1 - bit) * 8)
        self.send(group, 0, (1 - bit) * 8)

    def keep(self, group):
        self.base[group] = self.bits[order_of(group)[0]] * 8
        self.fill(group, self.base[group])

    def take(self, group, step, start, count, offset):
        work, got = self.work[group], self.got[group][step]

        def one(at, _):
            total = work[start + at].astype(jnp.float32) + got[offset + at].astype(jnp.float32)
            work[start + at] = total.astype(jnp.bfloat16)
            return 0

        lax.fori_loop(0, count, one, 0)

    def advance(self, group, step):
        half, bit = 8 >> step, self.bits[order_of(group)[step]]
        away, mine = (1 - bit) * half, bit * half
        self.copies[group, step - 1].wait_recv()
        self.take(group, step - 1, self.base[group] + away, half, away)
        self.send(group, step, self.base[group] + away)
        self.take(group, step - 1, self.base[group] + mine, half, mine)
        self.base[group] = self.base[group] + mine

    def last(self, group, target):
        _, first_row, last_row, _ = GROUPS[group]
        self.copies[group, 3].wait_recv()
        total = self.work[group][self.base[group]].astype(jnp.float32)
        total = (total + self.got[group][3][0].astype(jnp.float32)).astype(jnp.bfloat16)
        target[0, first_row:last_row] = total[:, :KEEP_LANES]
        target[1, first_row:last_row] = total[:, HALF_LANES - KEEP_LANES :]


def near_peers():
    hi, core, z, lo, x = place()
    group = lo * 4 + x
    plane = [(hi * 2 + core, z * 8 + (group + step) % 8) for step in range(1, 8)]
    line = [(hi * 2 + core, ((z + step) % 8) * 8 + group) for step in range(1, 8)]
    return plane, line


def swap_eights(rows):
    count = rows.shape[0]
    at = lax.broadcasted_iota(jnp.int32, (count, count), 0)
    origin = lax.broadcasted_iota(jnp.int32, (count, count), 1)
    wanted = (at // 2 % 8) * 16 + at // 16 * 2 + at % 2
    chosen = jnp.where(origin == wanted, 1.0, 0.0).astype(jnp.bfloat16)
    moved = jnp.dot(chosen, rows, preferred_element_type=jnp.float32)
    return moved.astype(jnp.bfloat16)


class Exchange:
    def __init__(self, first, got_first, second, got_second, sends, recvs):
        self.first, self.got_first = first, got_first
        self.second, self.got_second = second, got_second
        self.sends, self.recvs = sends, recvs
        self.plane, self.line = near_peers()
        _, _, self.z, lo, x = place()
        self.group = lo * 4 + x

    def start_plane(self, rows):
        self.first[...] = swap_eights(rows).reshape(self.first.shape)
        self.copies = [
            send(
                self.first.at[(self.group + step) % 8], self.got_first.at[self.group],
                self.sends, self.recvs, step, self.plane[step - 1],
            )
            for step in range(1, 8)
        ]
        self.got_first[self.group] = self.first[self.group]

    def start_line(self):
        for copy in self.copies:
            copy.wait_recv()
        rows = self.got_first[...].reshape(128, -1)
        self.second[...] = swap_eights(rows).reshape(self.second.shape)
        more = [
            send(
                self.second.at[(self.z + step) % 8], self.got_second.at[self.z],
                self.sends, self.recvs, 8 + step, self.line[step - 1],
            )
            for step in range(1, 8)
        ]
        self.got_second[self.z] = self.second[self.z]
        self.copies = self.copies + more
        return more

    def finish(self):
        for copy in self.copies[7:]:
            copy.wait_recv()
        for copy in self.copies:
            copy.wait_send()
        return self.got_second[...].reshape(128, -1)


EXCHANGE_SCRATCH = [pltpu.VMEM((8, 16, 1152), jnp.bfloat16)] * 4 + [
    pltpu.SemaphoreType.DMA((16,)),
    pltpu.SemaphoreType.DMA((16,)),
]


class Gather:
    def __init__(self, own, full, cut, sends, recvs, local):
        self.own, self.full, self.cut = own, full, cut
        self.sends, self.recvs, self.local = sends, recvs, local
        self.hi, self.core, z, lo, self.x = place()
        hi, core, x = self.hi, self.core, self.x
        self.mine, self.far = hi * 2 + core, (1 - hi) * 2 + core
        self.twin = device(hi, 1 - core, z, lo, x)
        self.across = device(1 - hi, core, z, 1 - lo, x)
        self.right = device(hi, core, z, lo, (x + 1) % 4)
        self.left = device(hi, core, z, lo, (x + 3) % 4)
        self.copies = {}

    def go(self, at, source, target, peer):
        self.copies[at] = send(source, target, self.sends, self.recvs, at, peer)

    def same(self, at, ref, peer):
        self.go(at, ref, ref, peer)

    def start(self):
        start = pl.multiple_of(self.x * 64 + self.x // 2 * 16, 16)
        self.go(0, self.own.at[pl.ds(start, 80)], self.full.at[self.mine, self.x], self.across)
        self.locals = []
        for quarter, first in enumerate(STARTS):
            source, target = self.own.at[pl.ds(first, 80)], self.full.at[self.mine, quarter]
            self.go(10 + quarter, source, target, self.twin)
            copy = pltpu.make_async_copy(source, target, self.local.at[quarter])
            copy.start()
            self.locals.append(copy)

    def spread(self):
        self.copies[0].wait_recv()
        piece = self.full.at[self.far, self.x]
        self.same(2, piece, self.right)
        self.same(3, piece, self.left)
        self.same(4, piece, self.twin)

    def pass_on(self):
        cut, width = self.cut, self.full.shape[3]
        self.copies[2].wait_recv()
        from_left = (self.far, (self.x + 3) % 4)
        self.same(5, self.full.at[from_left + (slice(None), pl.ds(0, cut))], self.right)
        self.same(6, self.full.at[from_left], self.twin)
        self.copies[3].wait_recv()
        from_right = (self.far, (self.x + 1) % 4)
        self.same(7, self.full.at[from_right + (slice(None), pl.ds(cut, width - cut))], self.left)
        self.same(8, self.full.at[from_right], self.twin)

    def last(self):
        self.copies[5].wait_recv()
        self.copies[7].wait_recv()
        self.same(9, self.full.at[self.far, (self.x + 2) % 4], self.twin)

    def arrive(self):
        for copy in self.locals:
            copy.wait()
        for at in (4, 6, 8, 9, 10, 11, 12, 13):
            self.copies[at].wait_recv()

    def finish(self):
        for copy in self.copies.values():
            copy.wait_send()


STARTS = (0, 64, 144, 208)
GATHER_SCRATCH = [
    pltpu.SemaphoreType.DMA((14,)), pltpu.SemaphoreType.DMA((14,)), pltpu.SemaphoreType.DMA((4,))
]


def weight_rows(full, columns):
    return jnp.concatenate(
        [
            full[block, quarter, 16 * (quarter % 2) : 80, columns]
            for block in range(4)
            for quarter in range(4)
        ],
        axis=0,
    )


WIDTH = 1152
HEAD = WIDTH // HEADS
FACTOR = 1.0 / math.sqrt(HEAD)


def across_rows(left, right):
    return lax.dot_general(
        left, right, (((1,), (1,)), ((), ())), preferred_element_type=jnp.float32
    )


def down_rows(left, right):
    return lax.dot_general(
        left, right, (((0,), (0,)), ((), ())), preferred_element_type=jnp.float32
    )


def turn_tables(angles, half):
    lane = lax.broadcasted_iota(jnp.int32, (1, WIDTH), 1) % HEAD
    first = lane % (2 * half) < half
    origin = lane // (2 * half) * half + lane % half
    row = lax.broadcasted_iota(jnp.int32, (128, WIDTH), 0)
    cosine_at = jnp.where(row == origin, 1.0, 0.0).astype(jnp.bfloat16)
    sine_at = jnp.where(row == origin + 36, 1.0, 0.0) * jnp.where(first, -1.0, 1.0)
    sine_at = sine_at.astype(jnp.bfloat16)
    cosine = jnp.zeros((128, WIDTH), jnp.float32)
    sine = jnp.zeros((128, WIDTH), jnp.float32)
    rest = angles
    for _ in range(3):
        part = rest.astype(jnp.bfloat16)
        rest = rest - part.astype(jnp.float32)
        cosine += jnp.dot(part, cosine_at, preferred_element_type=jnp.float32)
        sine += jnp.dot(part, sine_at, preferred_element_type=jnp.float32)
    return cosine, sine


def turn(values, cosine, sine, half, direction):
    lane = lax.broadcasted_iota(jnp.int32, (1, WIDTH), 1) % (2 * half)
    partner = jnp.where(
        lane < half, pltpu.roll(values, WIDTH - half, 1), pltpu.roll(values, half, 1)
    )
    return values * cosine + partner * (sine * direction)


def head_window(head):
    start = min(head * HEAD // 128 * 128, WIDTH - 256)
    lane = lax.broadcasted_iota(jnp.int32, (1, 256), 1) + start
    mask = jnp.where((lane >= head * HEAD) & (lane < (head + 1) * HEAD), 1.0, 0.0)
    return slice(start, start + 256), mask.astype(jnp.bfloat16)


def softmax_rows(scores):
    exponent = jnp.exp(scores - jnp.max(scores, axis=-1, keepdims=True))
    return exponent / jnp.sum(exponent, axis=-1, keepdims=True)


def head_back(weights, query, key, value, grad, mask):
    grad = grad * mask
    rounded = weights.astype(jnp.bfloat16)
    grad_weights = across_rows(grad, value)
    delta = jnp.sum(rounded.astype(jnp.float32) * grad_weights, axis=-1, keepdims=True)
    scores = (weights * (grad_weights - delta) * FACTOR).astype(jnp.bfloat16)
    return (
        jnp.dot(scores, key * mask, preferred_element_type=jnp.float32),
        down_rows(scores, query * mask),
        down_rows(rounded, grad),
    )


def space_forward(heads, turned_query, turned_key, value, weights_ref, mixed):
    for head in heads:
        window, mask = head_window(head)
        scores = across_rows(turned_query[:, window] * mask, turned_key[:, window]) * FACTOR
        weights = softmax_rows(scores)
        weights_ref[head] = weights
        mixed[:, window] += jnp.dot(
            weights.astype(jnp.bfloat16), value[:, window] * mask,
            preferred_element_type=jnp.float32,
        )


def space_back_heads(heads, weights, turned_query, turned_key, value, grad, totals):
    for head in heads:
        window, mask = head_window(head)
        parts = head_back(
            weights[head], turned_query[:, window], turned_key[:, window], value[:, window],
            grad[:, window], mask,
        )
        for total, part in zip(totals, parts):
            total[:, window] += part


def core_columns(rows, core):
    part = WIDTH // 4
    pieces = [rows[:, (hi * 2 + core) * part : (hi * 2 + core + 1) * part] for hi in range(2)]
    rest = jnp.zeros((rows.shape[0], HALF_LANES - 2 * part), rows.dtype)
    return jnp.concatenate(pieces + [rest], axis=1)


def stage(pairs, sems):
    copies = [
        pltpu.make_async_copy(source, target, sems.at[at]) for at, (source, target) in enumerate(pairs)
    ]
    for copy in copies:
        copy.start()
    return copies


def local_call(kernel, outs, scratch, megabytes, *args):
    return pl.pallas_call(
        kernel,
        out_shape=tuple(jax.ShapeDtypeStruct(shape, kind) for shape, kind in outs),
        in_specs=[pl.BlockSpec(memory_space=pltpu.VMEM)] * len(args),
        out_specs=tuple(pl.BlockSpec(memory_space=pltpu.VMEM) for _ in outs),
        scratch_shapes=[pltpu.VMEM(shape, kind) for shape, kind in scratch],
        compiler_params=pltpu.CompilerParams(vmem_limit_bytes=megabytes * 1024 * 1024),
    )(*args)


ROWS = ((128, WIDTH), jnp.bfloat16)
WIDE_ROWS = ((128, WIDTH), jnp.float32)
RIGHT = ((2, 128, HALF_LANES), jnp.bfloat16)


def time_kernel(
    rows_ref, qkv_full, scale_ref, shift_ref, grad_ref, angles_ref,
    right_ref, projected_ref, back_ref, sums_ref,
    normed_ref, wide, turned, total_back, modulated_ref,
):
    rows = rows_ref[...].astype(jnp.float32)
    centered = rows - jnp.mean(rows, axis=-1, keepdims=True)
    inverse = lax.rsqrt(jnp.mean(centered * centered, axis=-1, keepdims=True) + epsilon)
    normed = centered * inverse
    normed_ref[...] = normed
    scale = 1.0 + scale_ref[...]
    modulated = (normed * scale + shift_ref[...]).astype(jnp.bfloat16)
    modulated_ref[...] = modulated
    for core in range(2):
        right_ref[core] = core_columns(modulated, core)
    for block in range(9):
        columns = slice(block * 384, block * 384 + 384)
        wide[:, columns] = jnp.dot(
            modulated_ref[...], weight_rows(qkv_full, columns), preferred_element_type=jnp.float32
        )
    cosine, sine = turn_tables(angles_ref[...], HEAD // 2)
    for block in range(2):
        columns = slice(block * WIDTH, block * WIDTH + WIDTH)
        turned[:, columns] = turn(wide[:, columns], cosine, sine, HEAD // 2, 1.0).astype(jnp.bfloat16)
    turned[:, 2 * WIDTH :] = wide[:, 2 * WIDTH :].astype(jnp.bfloat16)
    wide[...] = jnp.zeros_like(wide)
    spot_row = lax.broadcasted_iota(jnp.int32, (128, 128), 0) % 2
    spot_column = lax.broadcasted_iota(jnp.int32, (128, 128), 1) % 2
    together = spot_row == spot_column
    for head in range(HEADS):
        window, mask = head_window(head)
        windows = [slice(window.start + WIDTH * j, window.stop + WIDTH * j) for j in range(3)]
        query, key, value = [turned[:, columns] for columns in windows]
        scores = across_rows(query * mask, key) * FACTOR
        weights = softmax_rows(jnp.where(together, scores, -jnp.inf))
        parts = head_back(weights, query, key, value, grad_ref[:, window], mask)
        for columns, part in zip(windows, parts):
            wide[:, columns] += part
    for block in range(2):
        columns = slice(block * WIDTH, block * WIDTH + WIDTH)
        projected_ref[:, columns] = turn(wide[:, columns], cosine, sine, HEAD // 2, -1.0).astype(
            jnp.bfloat16
        )
    projected_ref[:, 2 * WIDTH :] = wide[:, 2 * WIDTH :].astype(jnp.bfloat16)
    for block in range(9):
        columns = slice(block * 384, block * 384 + 384)
        part = across_rows(projected_ref[:, columns], weight_rows(qkv_full, columns))
        if block == 0:
            total_back[...] = part
        else:
            total_back[...] += part
    grad = total_back[...]
    normed = normed_ref[...]
    sums_ref[...] = jnp.concatenate(
        [
            jnp.sum(grad, axis=0, keepdims=True),
            jnp.sum(grad * normed, axis=0, keepdims=True),
            jnp.zeros((6, WIDTH), jnp.float32),
        ],
        axis=0,
    )
    grad = grad * scale
    back_ref[...] = (
        (
            grad
            - jnp.mean(grad, axis=-1, keepdims=True)
            - normed * jnp.mean(grad * normed, axis=-1, keepdims=True)
        )
        * inverse
    ).astype(jnp.bfloat16)


def time_sublayer(*args):
    wide = (128, 3 * WIDTH)
    return local_call(
        time_kernel,
        [RIGHT, (wide, jnp.bfloat16), ROWS, ((8, WIDTH), jnp.float32)],
        [WIDE_ROWS, (wide, jnp.float32), (wide, jnp.bfloat16), WIDE_ROWS, ROWS],
        40,
        *args,
    )


def front_kernel(
    query_in, key_in, value_in, hidden_in, angles_ref, proj_ref, qkv_ref,
    rows_ref, right_ref, turned_query, turned_key, weights_ref, proj_full, qkv_full,
    query_ref, key_ref, value_ref, hidden_ref, wide, mixed_ref, stage_sems, *scratch,
):
    staged = stage(
        [(query_in, query_ref), (key_in, key_ref), (value_in, value_ref), (hidden_in, hidden_ref)],
        stage_sems,
    )
    proj = Gather(proj_ref, proj_full, 640, *scratch[:3])
    thirds = []
    for third in range(3):
        columns = pl.ds(third * WIDTH, WIDTH)
        thirds.append(
            Gather(
                qkv_ref.at[:, columns], qkv_full.at[:, :, :, columns], 640,
                *scratch[3 * third + 3 : 3 * third + 6],
            )
        )
    one, two, three = thirds
    exchange = Exchange(*scratch[12:])
    meet([proj.twin, proj.across] + exchange.plane + exchange.line)
    for gather in (proj, one, two, three):
        gather.start()
    for copy in staged:
        copy.wait()
    cosine, sine = turn_tables(angles_ref[...], HEAD // 4)
    for source, target in ((query_ref, turned_query), (key_ref, turned_key)):
        values = source[...].astype(jnp.float32)
        target[...] = turn(values, cosine, sine, HEAD // 4, 1.0).astype(jnp.bfloat16)
    wide[...] = jnp.zeros_like(wide)

    def heads(first):
        space_forward(
            range(first, first + 4), turned_query, turned_key, value_ref, weights_ref, wide
        )

    proj.spread()
    heads(0)
    one.spread()
    heads(4)
    proj.pass_on()
    heads(8)
    two.spread()
    proj.last()
    heads(12)
    one.pass_on()
    mixed = wide[...].astype(jnp.bfloat16)
    mixed_ref[...] = mixed
    proj.arrive()
    for block in range(3):
        columns = slice(block * 384, block * 384 + 384)
        wide[:, columns] = hidden_ref[:, columns].astype(jnp.float32) + jnp.dot(
            mixed_ref[...], weight_rows(proj_full, columns), preferred_element_type=jnp.float32
        )
    exchange.start_plane(wide[...].astype(jnp.bfloat16))
    three.spread()
    one.last()
    for core in range(2):
        right_ref[core] = core_columns(mixed_ref[...], core)
    exchange.start_line()
    two.pass_on()
    two.last()
    three.pass_on()
    three.last()
    rows_ref[...] = exchange.finish()
    for gather in thirds:
        gather.arrive()
    for gather in (proj, one, two, three):
        gather.finish()


def front(query, key, value, hidden, angles, proj, qkv):
    def whole(weight):
        return jax.ShapeDtypeStruct((4, 4, 80, weight.shape[1]), weight.dtype)

    vmem, away = pl.BlockSpec(memory_space=pltpu.VMEM), pl.BlockSpec(memory_space=pltpu.HBM)
    rows = jax.ShapeDtypeStruct(*ROWS)
    return pl.pallas_call(
        front_kernel,
        out_shape=(
            rows, jax.ShapeDtypeStruct(*RIGHT), rows, rows,
            jax.ShapeDtypeStruct((HEADS, 128, 128), jnp.float32), whole(proj), whole(qkv),
        ),
        in_specs=[away] * 4 + [vmem] + [away] * 2,
        out_specs=(vmem,) * 7,
        scratch_shapes=[pltpu.VMEM(*ROWS)] * 4
        + [pltpu.VMEM(*WIDE_ROWS), pltpu.VMEM(*ROWS), pltpu.SemaphoreType.DMA((4,))]
        + GATHER_SCRATCH * 4
        + EXCHANGE_SCRATCH,
        compiler_params=pltpu.CompilerParams(
            collective_id=1, has_side_effects=True, vmem_limit_bytes=32 * 1024 * 1024
        ),
    )(query, key, value, hidden, angles, proj, qkv)


def tail_kernel(
    left_qkv, right_qkv, back_rows, sums_ref, angles_ref,
    right_proj, resid_in, query_in, key_in, value_in, weights_in, proj_in,
    hidden_out, query_out, key_out, value_out, total_ref, qkv_out, proj_out,
    resid_ref, query_ref, key_ref, value_ref, weights_ref, proj_full, stage_sems,
    left_proj, both_qkv, both_proj, twin_qkv, twin_proj, twin_send, twin_recv,
    total_query, total_key, total_value, grad,
    plane_sums, line_sums, sum_sends, sum_recvs,
    step_send, step_recv, qkv_last, proj_last, qkv_final, proj_final, final_send, final_recv,
    *scratch,
):
    count = len(GROUPS)
    exchange = Exchange(*scratch[:6])
    work, got = scratch[6 : 6 + count], scratch[6 + count :]
    got = [got[4 * group : 4 * group + 4] for group in range(count)]
    hi, core, z, lo, x = place()
    near, pair, group_at = z % 2, z // 2, exchange.group
    twin = device(hi, 1 - core, z, lo, x)
    halving = Halving(
        (both_qkv, both_proj), (left_qkv, left_proj), (twin_qkv, twin_proj), work, got,
        step_send, step_recv,
    )
    others = []
    for step_hi in range(2):
        for step_pair in range(4):
            if step_hi + step_pair > 0:
                to_hi, to_pair = (hi + step_hi) % 2, (pair + step_pair) % 4
                others.append(
                    (step_hi * 4 + step_pair, to_hi, to_pair,
                     device(to_hi, core, to_pair * 2 + near, lo, x))
                )
    staged = stage(
        [
            (resid_in, resid_ref), (proj_in, proj_full), (query_in, query_ref), (key_in, key_ref),
            (value_in, value_ref), (weights_in, weights_ref),
            (right_proj.at[core], both_proj.at[pl.ds(0, 128)]),
        ],
        stage_sems,
    )
    meet([twin] + [other[3] for other in others[3:]] + exchange.plane + exchange.line)
    own, other = pl.ds(0, 128), pl.ds(128, 128)
    twins = [
        send(right_qkv.at[1 - core], both_qkv.at[other], twin_send, twin_recv, 0, twin),
        send(left_qkv, twin_qkv, twin_send, twin_recv, 1, twin),
        send(right_proj.at[1 - core], both_proj.at[other], twin_send, twin_recv, 2, twin),
    ]
    exchange.start_plane(back_rows[...])
    sums = [
        send(sums_ref, plane_sums.at[group_at], sum_sends, sum_recvs, step, exchange.plane[step - 1])
        for step in range(1, 8)
    ]
    plane_sums[group_at] = sums_ref[...]
    both_qkv[own] = right_qkv[core]
    twins[0].wait_recv()
    twins[1].wait_recv()
    for group in range(2):
        halving.begin(group)
    exchange.start_line()
    for copy in sums:
        copy.wait_recv()
    line_sums[z] = jnp.sum(plane_sums[...], axis=0)
    more = [
        send(
            line_sums.at[z], line_sums.at[z], sum_sends, sum_recvs, 8 + step,
            exchange.line[step - 1],
        )
        for step in range(1, 8)
    ]
    for group in range(2, 4):
        halving.begin(group)
    for group in range(4):
        halving.keep(group)
    row = lax.broadcasted_iota(jnp.int32, (PROJ_ROWS, WIDTH), 0)
    column = lax.broadcasted_iota(jnp.int32, (PROJ_ROWS, WIDTH), 1)
    piece = WIDTH // 64
    wanted = jnp.where(row < 4 * piece, row // piece * (16 * piece) + row % piece, -WIDTH)
    ahead = column - wanted
    for copy in staged:
        copy.wait()
    frames = exchange.finish()
    hidden = resid_ref[...].astype(jnp.float32) + frames.astype(jnp.float32)
    hidden_out[...] = hidden.astype(jnp.bfloat16)
    for block in range(16):
        chosen = jnp.where(ahead == block * piece, 1.0, 0.0).astype(jnp.bfloat16)
        left_proj[block] = across_rows(chosen, hidden_out[...]).astype(jnp.bfloat16)
    twins.append(send(left_proj, twin_proj, twin_send, twin_recv, 3, twin))
    for block in range(3):
        columns = slice(block * 384, block * 384 + 384)
        part = across_rows(hidden_out[:, columns], weight_rows(proj_full, columns))
        if block == 0:
            total_query[...] = part
        else:
            total_query[...] += part
    grad[...] = total_query[...].astype(jnp.bfloat16)
    twins[2].wait_recv()
    twins[3].wait_recv()
    for group in range(4, 6):
        halving.begin(group)
    for group in range(4, 6):
        halving.keep(group)
    for group in range(4):
        halving.advance(group, 1)
    totals = (total_query, total_key, total_value)
    for total in totals:
        total[...] = jnp.zeros_like(total)

    def heads(first, end):
        space_back_heads(
            range(first, end), weights_ref, query_ref, key_ref, value_ref, grad, totals
        )

    heads(0, 10)
    for group in range(4):
        halving.advance(group, 2)
    heads(10, 16)
    for group in range(4, 6):
        halving.advance(group, 1)
    for group in range(4):
        halving.advance(group, 3)
    cosine, sine = turn_tables(angles_ref[...], HEAD // 4)
    for total, out in ((total_query, query_out), (total_key, key_out)):
        out[...] = turn(total[...], cosine, sine, HEAD // 4, -1.0).astype(jnp.bfloat16)
    value_out[...] = total_value[...].astype(jnp.bfloat16)
    for copy in more:
        copy.wait_recv()
    total_ref[...] = jnp.sum(line_sums[...], axis=0)
    for group in range(4, 6):
        halving.advance(group, 2)
    for group in range(4):
        halving.last(group, qkv_last)
    ends = []
    for slot, to_hi, to_pair, peer in others:
        rows = pl.ds(pl.multiple_of(to_pair * 48, 16), QKV_WINDOW)
        ends.append(
            send(qkv_last.at[to_hi, rows], qkv_final.at[slot], final_send, final_recv, slot, peer)
        )
    for group in range(4, 6):
        halving.advance(group, 3)
    for group in range(4, 6):
        halving.last(group, proj_last)
    for slot, to_hi, to_pair, peer in others:
        rows = pl.ds(pl.multiple_of(to_pair * 16, 16), PROJ_WINDOW)
        ends.append(
            send(
                proj_last.at[to_hi, rows], proj_final.at[slot], final_send, final_recv, 8 + slot,
                peer,
            )
        )
    total = qkv_last[hi, pl.ds(pl.multiple_of(pair * 48, 16), QKV_WINDOW)].astype(jnp.float32)
    for (slot, _, _, _), copy in zip(others, ends[:7]):
        copy.wait_recv()
        total += qkv_final[slot].astype(jnp.float32)
    qkv_out[...] = total
    total = proj_last[hi, pl.ds(pl.multiple_of(pair * 16, 16), PROJ_WINDOW)].astype(jnp.float32)
    for (slot, _, _, _), copy in zip(others, ends[7:]):
        copy.wait_recv()
        total += proj_final[slot].astype(jnp.float32)
    proj_out[...] = total
    for copy in twins + sums + more + list(halving.copies.values()) + ends:
        copy.wait_send()


def tail(left, right, back_rows, sums, angles, right_proj, resid, query, key, value, weights, proj):
    vmem, away = pl.BlockSpec(memory_space=pltpu.VMEM), pl.BlockSpec(memory_space=pltpu.HBM)
    b16, f32 = jnp.bfloat16, jnp.float32
    shape, dma = pltpu.VMEM, pltpu.SemaphoreType.DMA
    outs = [ROWS] * 4 + [
        (sums.shape, f32), ((QKV_WINDOW, KEEP_LANES), f32), ((PROJ_WINDOW, KEEP_LANES), f32)
    ]
    counts = [last - first for _, first, last, _ in GROUPS]
    scratch = [
        shape(*ROWS), shape(*ROWS), shape(*ROWS), shape(*ROWS),
        shape(weights.shape, f32), shape(proj.shape, b16), dma((7,)),
        shape((16, PROJ_ROWS, 128), b16), shape((256, HALF_LANES), b16), shape((256, HALF_LANES), b16),
        shape((16, QKV_ROWS, 128), b16), shape((16, PROJ_ROWS, 128), b16), dma((4,)), dma((4,)),
        shape(*WIDE_ROWS), shape(*WIDE_ROWS), shape(*WIDE_ROWS), shape(*ROWS),
        shape((8,) + sums.shape, f32), shape((8,) + sums.shape, f32), dma((16,)), dma((16,)),
        dma((6, 4)), dma((6, 4)),
        shape((2, QKV_ROWS, KEEP_LANES), b16), shape((2, PROJ_ROWS, KEEP_LANES), b16),
        shape((8, QKV_WINDOW, KEEP_LANES), b16), shape((8, PROJ_WINDOW, KEEP_LANES), b16),
        dma((16,)), dma((16,)),
    ] + EXCHANGE_SCRATCH
    scratch += [shape((16, count, HALF_LANES), b16) for count in counts]
    scratch += [
        shape((8 >> step, count, HALF_LANES), b16) for count in counts for step in range(4)
    ]
    return pl.pallas_call(
        tail_kernel,
        out_shape=tuple(jax.ShapeDtypeStruct(*out) for out in outs),
        in_specs=[vmem] * 5 + [away] * 7,
        out_specs=(vmem,) * len(outs),
        scratch_shapes=scratch,
        compiler_params=pltpu.CompilerParams(
            collective_id=2, has_side_effects=True, vmem_limit_bytes=44 * 1024 * 1024
        ),
    )(left, right, back_rows, sums, angles, right_proj, resid, query, key, value, weights, proj)


def turn_angles(places, half):
    frequency = 10000.0 ** (-jnp.arange(half, dtype=jnp.float32) / half)
    angles = (places.astype(jnp.float32)[:, :, None] * frequency).reshape(128, 36)
    return jnp.pad(jnp.concatenate([jnp.cos(angles), jnp.sin(angles)], axis=1), ((0, 0), (0, 56)))


def body(
    hidden,
    query_space,
    key_space,
    value_space,
    positions,
    proj_space,
    shift_time,
    scale_time,
    qkv_time,
    grad_attn_time,
    grad_resid,
):
    seq_place = lax.axis_index("seq")
    frame_places = lax.dynamic_slice_in_dim(positions[0, 0], seq_place * 2, 2, 1).reshape(128, 1)
    spot_places = lax.dynamic_slice_in_dim(positions[1:, 0], seq_place, 1, 1).reshape(2, 128).T
    space_angles = turn_angles(spot_places, HEAD // 4)
    time_angles = turn_angles(frame_places, HEAD // 2)

    def flat(values):
        return values.reshape(128, WIDTH)

    rows, right_proj, space_query, space_key, space_weights, proj_full, qkv_full = front(
        flat(query_space), flat(key_space), flat(value_space), flat(hidden), space_angles,
        proj_space, qkv_time,
    )
    right_qkv, grad_projected, resid_back, sums = time_sublayer(
        rows, qkv_full, scale_time, shift_time, flat(grad_attn_time), time_angles
    )
    left = jnp.transpose(grad_projected.T.reshape(4, 16, 54, 128), (1, 0, 2, 3)).reshape(16, 216, 128)
    left = jnp.pad(left, ((0, 0), (0, QKV_ROWS - 216), (0, 0)))
    grad_hidden, grad_query, grad_key, grad_value, sums, qkv_block, proj_block = tail(
        left, right_qkv, resid_back, sums[:2].reshape(8, -1), space_angles, right_proj,
        flat(grad_resid), space_query, space_key, flat(value_space), space_weights, proj_full,
    )
    sums = sums.reshape(2, WIDTH)
    hi, pair = lax.axis_index("dp") // 2, seq_place // 16
    column = hi * (WIDTH // 4 + KEEP_LANES - HALF_LANES)
    grad_qkv_time = lax.dynamic_slice(qkv_block, (pair * 6, column), (54, WIDTH // 4)).T
    grad_proj_space = lax.dynamic_slice(proj_block, (pair * 2, column), (18, WIDTH // 4)).T
    shape = hidden.shape
    return (
        grad_hidden.reshape(shape),
        grad_query.reshape(shape),
        grad_key.reshape(shape),
        grad_value.reshape(shape),
        grad_proj_space,
        grad_qkv_time,
        sums[:1],
        sums[1:],
    )


def solution(mesh):
    in_specs = (
        P("dp", "seq", None, None),
        P("dp", "seq", None, None),
        P("dp", "seq", None, None),
        P("dp", "seq", None, None),
        P(None, "dp", None, None),
        P("dp", None),
        P("dp", None),
        P("dp", None),
        P("dp", None),
        P("dp", None, "seq", None),
        P("dp", "seq", None, None),
    )
    out_specs = (
        P("dp", "seq", None, None),
        P("dp", "seq", None, None),
        P("dp", "seq", None, None),
        P("dp", "seq", None, None),
        P("dp", "seq"),
        P("dp", "seq"),
        P("dp", None),
        P("dp", None),
    )
    return jax.shard_map(body, mesh=mesh, in_specs=in_specs, out_specs=out_specs, check_vma=False)
```

```python
import math

import jax
import jax.numpy as jnp
from jax import lax
from jax.experimental import pallas as pl
from jax.experimental.pallas import tpu as pltpu
from jax.sharding import PartitionSpec as P

HEADS = 16


epsilon = 1e-06


MESH = pl.DeviceIdType.MESH

HALF_LANES = 640
KEEP_LANES = 384
ORDER = ("x_near", "y_near", "x_far", "z_near")
GROUPS = (
    (0, 0, 64, 0), (0, 64, 128, 1), (0, 128, 176, 2), (0, 176, 224, 3), (1, 0, 48, 2), (1, 48, 80, 3)
)
QKV_ROWS, PROJ_ROWS = 224, 80
QKV_WINDOW, PROJ_WINDOW = 80, 32


def place():
    dp, seq = lax.axis_index("dp"), lax.axis_index("seq")
    hi, core = dp // 2, dp % 2
    z, lo, x = seq // 8, (seq // 4) % 2, seq % 4
    return hi, core, z, lo, x


def device(hi, core, z, lo, x):
    return (hi * 2 + core, z * 8 + lo * 4 + x)


def send(source, target, sends, recvs, at, peer):
    copy = pltpu.make_async_remote_copy(
        src_ref=source, dst_ref=target, send_sem=sends.at[at], recv_sem=recvs.at[at],
        device_id=peer, device_id_type=MESH,
    )
    copy.start()
    return copy


def meet(peers):
    barrier = pltpu.get_barrier_semaphore()
    for peer in peers:
        pl.semaphore_signal(barrier, inc=1, device_id=peer, device_id_type=MESH)
    pl.semaphore_wait(barrier, len(peers))


def order_of(group):
    return [ORDER[(GROUPS[group][3] + step) % 4] for step in range(4)]


def combination(group, block):
    bits = {name: (block // (8 >> step)) % 2 for step, name in enumerate(order_of(group))}
    x = bits["x_far"] * 2 + (bits["x_near"] + bits["x_far"]) % 2
    return bits["z_near"] * 8 + bits["y_near"] * 4 + x


class Halving:
    def __init__(self, right, left, twin_left, work, got, sends, recvs):
        self.right, self.left, self.twin_left = right, left, twin_left
        self.work, self.got, self.sends, self.recvs = work, got, sends, recvs
        hi, core, z, lo, x = place()
        near = z % 2
        self.bits = {"x_near": (x % 2 + x // 2) % 2, "x_far": x // 2, "y_near": lo, "z_near": near}
        self.partners = {
            "x_near": device(hi, core, z, lo, x + 1 - 2 * (x % 2)),
            "x_far": device(hi, core, z, lo, 3 - x),
            "y_near": device(hi, core, z, 1 - lo, x),
            "z_near": device(hi, core, z + 1 - 2 * near, lo, x),
        }
        self.base = [0] * len(GROUPS)
        self.copies = {}

    def fill(self, group, start):
        kind, first_row, last_row, _ = GROUPS[group]
        count, rows = last_row - first_row, slice(first_row, last_row)
        left, other = self.left[kind], self.twin_left[kind]
        work, right = self.work[group], self.right[kind]

        def four(at, _):
            first = start + at * 4
            parts = []
            for j in range(4):
                block = combination(group, first + j)
                parts.append(jnp.concatenate([left[block, rows], other[block, rows]], axis=1))
            total = jnp.dot(
                jnp.concatenate(parts, axis=0), right[...], preferred_element_type=jnp.float32
            )
            work[pl.ds(first, 4)] = total.astype(jnp.bfloat16).reshape(4, count, HALF_LANES)
            return 0

        lax.fori_loop(0, 2, four, 0)

    def send(self, group, step, first):
        name = order_of(group)[step]
        self.copies[group, step] = send(
            self.work[group].at[pl.ds(first, 8 >> step)], self.got[group][step],
            self.sends, self.recvs, (group, step), self.partners[name],
        )

    def begin(self, group):
        bit = self.bits[order_of(group)[0]]
        self.fill(group, (1 - bit) * 8)
        self.send(group, 0, (1 - bit) * 8)

    def keep(self, group):
        self.base[group] = self.bits[order_of(group)[0]] * 8
        self.fill(group, self.base[group])

    def take(self, group, step, start, count, offset):
        work, got = self.work[group], self.got[group][step]

        def one(at, _):
            total = work[start + at].astype(jnp.float32) + got[offset + at].astype(jnp.float32)
            work[start + at] = total.astype(jnp.bfloat16)
            return 0

        lax.fori_loop(0, count, one, 0)

    def advance(self, group, step):
        half, bit = 8 >> step, self.bits[order_of(group)[step]]
        away, mine = (1 - bit) * half, bit * half
        self.copies[group, step - 1].wait_recv()
        self.take(group, step - 1, self.base[group] + away, half, away)
        self.send(group, step, self.base[group] + away)
        self.take(group, step - 1, self.base[group] + mine, half, mine)
        self.base[group] = self.base[group] + mine

    def last(self, group, target):
        _, first_row, last_row, _ = GROUPS[group]
        self.copies[group, 3].wait_recv()
        total = self.work[group][self.base[group]].astype(jnp.float32)
        total = (total + self.got[group][3][0].astype(jnp.float32)).astype(jnp.bfloat16)
        target[0, first_row:last_row] = total[:, :KEEP_LANES]
        target[1, first_row:last_row] = total[:, HALF_LANES - KEEP_LANES :]


def near_peers():
    hi, core, z, lo, x = place()
    group = lo * 4 + x
    plane = [(hi * 2 + core, z * 8 + (group + step) % 8) for step in range(1, 8)]
    line = [(hi * 2 + core, ((z + step) % 8) * 8 + group) for step in range(1, 8)]
    return plane, line


def swap_eights(rows):
    count = rows.shape[0]
    at = lax.broadcasted_iota(jnp.int32, (count, count), 0)
    origin = lax.broadcasted_iota(jnp.int32, (count, count), 1)
    wanted = (at // 2 % 8) * 16 + at // 16 * 2 + at % 2
    chosen = jnp.where(origin == wanted, 1.0, 0.0).astype(jnp.bfloat16)
    moved = jnp.dot(chosen, rows, preferred_element_type=jnp.float32)
    return moved.astype(jnp.bfloat16)


class Exchange:
    def __init__(self, first, got_first, second, got_second, sends, recvs):
        self.first, self.got_first = first, got_first
        self.second, self.got_second = second, got_second
        self.sends, self.recvs = sends, recvs
        self.plane, self.line = near_peers()
        _, _, self.z, lo, x = place()
        self.group = lo * 4 + x

    def start_plane(self, rows):
        self.first[...] = swap_eights(rows).reshape(self.first.shape)
        self.copies = [
            send(
                self.first.at[(self.group + step) % 8], self.got_first.at[self.group],
                self.sends, self.recvs, step, self.plane[step - 1],
            )
            for step in range(1, 8)
        ]
        self.got_first[self.group] = self.first[self.group]

    def start_line(self):
        for copy in self.copies:
            copy.wait_recv()
        rows = self.got_first[...].reshape(128, -1)
        self.second[...] = swap_eights(rows).reshape(self.second.shape)
        more = [
            send(
                self.second.at[(self.z + step) % 8], self.got_second.at[self.z],
                self.sends, self.recvs, 8 + step, self.line[step - 1],
            )
            for step in range(1, 8)
        ]
        self.got_second[self.z] = self.second[self.z]
        self.copies = self.copies + more
        return more

    def finish(self):
        for copy in self.copies[7:]:
            copy.wait_recv()
        for copy in self.copies:
            copy.wait_send()
        return self.got_second[...].reshape(128, -1)


EXCHANGE_SCRATCH = [pltpu.VMEM((8, 16, 1152), jnp.bfloat16)] * 4 + [
    pltpu.SemaphoreType.DMA((16,)),
    pltpu.SemaphoreType.DMA((16,)),
]


class Gather:
    def __init__(self, own, full, cut, sends, recvs, local):
        self.own, self.full, self.cut = own, full, cut
        self.sends, self.recvs, self.local = sends, recvs, local
        self.hi, self.core, z, lo, self.x = place()
        hi, core, x = self.hi, self.core, self.x
        self.mine, self.far = hi * 2 + core, (1 - hi) * 2 + core
        self.twin = device(hi, 1 - core, z, lo, x)
        self.across = device(1 - hi, core, z, 1 - lo, x)
        self.right = device(hi, core, z, lo, (x + 1) % 4)
        self.left = device(hi, core, z, lo, (x + 3) % 4)
        self.copies = {}

    def go(self, at, source, target, peer):
        self.copies[at] = send(source, target, self.sends, self.recvs, at, peer)

    def same(self, at, ref, peer):
        self.go(at, ref, ref, peer)

    def start(self):
        start = pl.multiple_of(self.x * 64 + self.x // 2 * 16, 16)
        self.go(0, self.own.at[pl.ds(start, 80)], self.full.at[self.mine, self.x], self.across)
        self.locals = []
        for quarter, first in enumerate(STARTS):
            source, target = self.own.at[pl.ds(first, 80)], self.full.at[self.mine, quarter]
            self.go(10 + quarter, source, target, self.twin)
            copy = pltpu.make_async_copy(source, target, self.local.at[quarter])
            copy.start()
            self.locals.append(copy)

    def spread(self):
        self.copies[0].wait_recv()
        piece = self.full.at[self.far, self.x]
        self.same(2, piece, self.right)
        self.same(3, piece, self.left)
        self.same(4, piece, self.twin)

    def pass_on(self):
        cut, width = self.cut, self.full.shape[3]
        self.copies[2].wait_recv()
        from_left = (self.far, (self.x + 3) % 4)
        self.same(5, self.full.at[from_left + (slice(None), pl.ds(0, cut))], self.right)
        self.same(6, self.full.at[from_left], self.twin)
        self.copies[3].wait_recv()
        from_right = (self.far, (self.x + 1) % 4)
        self.same(7, self.full.at[from_right + (slice(None), pl.ds(cut, width - cut))], self.left)
        self.same(8, self.full.at[from_right], self.twin)

    def last(self):
        self.copies[5].wait_recv()
        self.copies[7].wait_recv()
        self.same(9, self.full.at[self.far, (self.x + 2) % 4], self.twin)

    def arrive(self):
        for copy in self.locals:
            copy.wait()
        for at in (4, 6, 8, 9, 10, 11, 12, 13):
            self.copies[at].wait_recv()

    def finish(self):
        for copy in self.copies.values():
            copy.wait_send()


STARTS = (0, 64, 144, 208)
GATHER_SCRATCH = [
    pltpu.SemaphoreType.DMA((14,)), pltpu.SemaphoreType.DMA((14,)), pltpu.SemaphoreType.DMA((4,))
]


def weight_rows(full, columns):
    return jnp.concatenate(
        [
            full[block, quarter, 16 * (quarter % 2) : 80, columns]
            for block in range(4)
            for quarter in range(4)
        ],
        axis=0,
    )


WIDTH = 1152
HEAD = WIDTH // HEADS
FACTOR = 1.0 / math.sqrt(HEAD)


def across_rows(left, right):
    return lax.dot_general(
        left, right, (((1,), (1,)), ((), ())), preferred_element_type=jnp.float32
    )


def down_rows(left, right):
    return lax.dot_general(
        left, right, (((0,), (0,)), ((), ())), preferred_element_type=jnp.float32
    )


def turn_tables(angles, half):
    lane = lax.broadcasted_iota(jnp.int32, (1, WIDTH), 1) % HEAD
    first = lane % (2 * half) < half
    origin = lane // (2 * half) * half + lane % half
    row = lax.broadcasted_iota(jnp.int32, (128, WIDTH), 0)
    cosine_at = jnp.where(row == origin, 1.0, 0.0).astype(jnp.bfloat16)
    sine_at = jnp.where(row == origin + 36, 1.0, 0.0) * jnp.where(first, -1.0, 1.0)
    sine_at = sine_at.astype(jnp.bfloat16)
    cosine = jnp.zeros((128, WIDTH), jnp.float32)
    sine = jnp.zeros((128, WIDTH), jnp.float32)
    rest = angles
    for _ in range(3):
        part = rest.astype(jnp.bfloat16)
        rest = rest - part.astype(jnp.float32)
        cosine += jnp.dot(part, cosine_at, preferred_element_type=jnp.float32)
        sine += jnp.dot(part, sine_at, preferred_element_type=jnp.float32)
    return cosine, sine


def turn(values, cosine, sine, half, direction):
    lane = lax.broadcasted_iota(jnp.int32, (1, WIDTH), 1) % (2 * half)
    partner = jnp.where(
        lane < half, pltpu.roll(values, WIDTH - half, 1), pltpu.roll(values, half, 1)
    )
    return values * cosine + partner * (sine * direction)


def head_window(head):
    start = min(head * HEAD // 128 * 128, WIDTH - 256)
    lane = lax.broadcasted_iota(jnp.int32, (1, 256), 1) + start
    mask = jnp.where((lane >= head * HEAD) & (lane < (head + 1) * HEAD), 1.0, 0.0)
    return slice(start, start + 256), mask.astype(jnp.bfloat16)


def softmax_rows(scores):
    exponent = jnp.exp(scores - jnp.max(scores, axis=-1, keepdims=True))
    return exponent / jnp.sum(exponent, axis=-1, keepdims=True)


def head_back(weights, query, key, value, grad, mask):
    grad = grad * mask
    rounded = weights.astype(jnp.bfloat16)
    grad_weights = across_rows(grad, value)
    delta = jnp.sum(rounded.astype(jnp.float32) * grad_weights, axis=-1, keepdims=True)
    scores = (weights * (grad_weights - delta) * FACTOR).astype(jnp.bfloat16)
    return (
        jnp.dot(scores, key * mask, preferred_element_type=jnp.float32),
        down_rows(scores, query * mask),
        down_rows(rounded, grad),
    )


def space_forward(heads, turned_query, turned_key, value, weights_ref, mixed):
    for head in heads:
        window, mask = head_window(head)
        scores = across_rows(turned_query[:, window] * mask, turned_key[:, window]) * FACTOR
        weights = softmax_rows(scores)
        weights_ref[head] = weights
        mixed[:, window] += jnp.dot(
            weights.astype(jnp.bfloat16), value[:, window] * mask,
            preferred_element_type=jnp.float32,
        )


def space_back_heads(heads, weights, turned_query, turned_key, value, grad, totals):
    for head in heads:
        window, mask = head_window(head)
        parts = head_back(
            weights[head], turned_query[:, window], turned_key[:, window], value[:, window],
            grad[:, window], mask,
        )
        for total, part in zip(totals, parts):
            total[:, window] += part


def core_columns(rows, core):
    part = WIDTH // 4
    pieces = [rows[:, (hi * 2 + core) * part : (hi * 2 + core + 1) * part] for hi in range(2)]
    rest = jnp.zeros((rows.shape[0], HALF_LANES - 2 * part), rows.dtype)
    return jnp.concatenate(pieces + [rest], axis=1)


def stage(pairs, sems):
    copies = [
        pltpu.make_async_copy(source, target, sems.at[at]) for at, (source, target) in enumerate(pairs)
    ]
    for copy in copies:
        copy.start()
    return copies


def local_call(kernel, outs, scratch, megabytes, *args):
    return pl.pallas_call(
        kernel,
        out_shape=tuple(jax.ShapeDtypeStruct(shape, kind) for shape, kind in outs),
        in_specs=[pl.BlockSpec(memory_space=pltpu.VMEM)] * len(args),
        out_specs=tuple(pl.BlockSpec(memory_space=pltpu.VMEM) for _ in outs),
        scratch_shapes=[pltpu.VMEM(shape, kind) for shape, kind in scratch],
        compiler_params=pltpu.CompilerParams(vmem_limit_bytes=megabytes * 1024 * 1024),
    )(*args)


ROWS = ((128, WIDTH), jnp.bfloat16)
WIDE_ROWS = ((128, WIDTH), jnp.float32)
RIGHT = ((2, 128, HALF_LANES), jnp.bfloat16)


def time_sublayer(
    rows, qkv_full, scale_ref, shift_ref, grad_ref, angles_ref,
    right_ref, projected_ref, sums_ref,
    normed_ref, wide, turned, total_back, modulated_ref,
):
    rows = rows.astype(jnp.float32)
    centered = rows - jnp.mean(rows, axis=-1, keepdims=True)
    inverse = lax.rsqrt(jnp.mean(centered * centered, axis=-1, keepdims=True) + epsilon)
    normed = centered * inverse
    normed_ref[...] = normed
    scale = 1.0 + scale_ref[...]
    modulated = (normed * scale + shift_ref[...]).astype(jnp.bfloat16)
    modulated_ref[...] = modulated
    for core in range(2):
        right_ref[core] = core_columns(modulated, core)
    for block in range(9):
        columns = slice(block * 384, block * 384 + 384)
        wide[:, columns] = jnp.dot(
            modulated_ref[...], weight_rows(qkv_full, columns), preferred_element_type=jnp.float32
        )
    cosine, sine = turn_tables(angles_ref[...], HEAD // 2)
    for block in range(2):
        columns = slice(block * WIDTH, block * WIDTH + WIDTH)
        turned[:, columns] = turn(wide[:, columns], cosine, sine, HEAD // 2, 1.0).astype(jnp.bfloat16)
    turned[:, 2 * WIDTH :] = wide[:, 2 * WIDTH :].astype(jnp.bfloat16)
    wide[...] = jnp.zeros_like(wide)
    spot_row = lax.broadcasted_iota(jnp.int32, (128, 128), 0) % 2
    spot_column = lax.broadcasted_iota(jnp.int32, (128, 128), 1) % 2
    together = spot_row == spot_column
    for head in range(HEADS):
        window, mask = head_window(head)
        windows = [slice(window.start + WIDTH * j, window.stop + WIDTH * j) for j in range(3)]
        query, key, value = [turned[:, columns] for columns in windows]
        scores = across_rows(query * mask, key) * FACTOR
        weights = softmax_rows(jnp.where(together, scores, -jnp.inf))
        parts = head_back(weights, query, key, value, grad_ref[:, window], mask)
        for columns, part in zip(windows, parts):
            wide[:, columns] += part
    for block in range(2):
        columns = slice(block * WIDTH, block * WIDTH + WIDTH)
        projected_ref[:, columns] = turn(wide[:, columns], cosine, sine, HEAD // 2, -1.0).astype(
            jnp.bfloat16
        )
    projected_ref[:, 2 * WIDTH :] = wide[:, 2 * WIDTH :].astype(jnp.bfloat16)
    for block in range(9):
        columns = slice(block * 384, block * 384 + 384)
        part = across_rows(projected_ref[:, columns], weight_rows(qkv_full, columns))
        if block == 0:
            total_back[...] = part
        else:
            total_back[...] += part
    grad = total_back[...]
    normed = normed_ref[...]
    sums_ref[0:1] = jnp.sum(grad, axis=0, keepdims=True)
    sums_ref[1:2] = jnp.sum(grad * normed, axis=0, keepdims=True)
    grad = grad * scale
    return (
        (
            grad
            - jnp.mean(grad, axis=-1, keepdims=True)
            - normed * jnp.mean(grad * normed, axis=-1, keepdims=True)
        )
        * inverse
    ).astype(jnp.bfloat16)


def piece_rows(values_ref, turned_rows, tall):
    for block in range(27):
        rows = slice(block * 128, block * 128 + 128)
        tall[rows] = values_ref[:, rows].astype(jnp.float32).T
    piece = 3 * WIDTH // 64
    for at in range(16):
        parts = [tall[(16 * k + at) * piece : (16 * k + at + 1) * piece] for k in range(4)]
        parts.append(jnp.zeros((QKV_ROWS - 4 * piece, 128), jnp.float32))
        turned_rows[at] = jnp.concatenate(parts, axis=0).astype(jnp.bfloat16)


def whole_kernel(
    angles_ref, time_angles, scale_ref, shift_ref,
    query_in, key_in, value_in, hidden_in, grad_time_in, resid_in, proj_ref, qkv_ref,
    hidden_out, query_out, key_out, value_out, total_ref, qkv_out, proj_out,
    query_ref, key_ref, value_ref, hidden_ref, grad_time, resid_ref, stage_sems,
    turned_query, turned_key, weights_ref, proj_full, qkv_full,
    wide, mixed_ref, right_qkv, right_proj, projected, sums_ref, normed, time_wide, turned,
    total_back, modulated, tall,
    left_qkv, left_proj, both_qkv, both_proj, twin_qkv, twin_proj, twin_send, twin_recv,
    total_query, total_key, total_value, grad,
    plane_sums, line_sums, sum_sends, sum_recvs,
    step_send, step_recv, qkv_last, proj_last, qkv_final, proj_final, final_send, final_recv,
    *scratch,
):
    staged = stage(
        [
            (query_in, query_ref), (key_in, key_ref), (value_in, value_ref),
            (hidden_in, hidden_ref), (grad_time_in, grad_time), (resid_in, resid_ref),
        ],
        stage_sems,
    )
    hi, core, z, lo, x = place()
    near, pair = z % 2, z // 2
    twin = device(hi, 1 - core, z, lo, x)
    count = len(GROUPS)
    proj = Gather(proj_ref, proj_full, 640, *scratch[:3])
    thirds = []
    for third in range(3):
        columns = pl.ds(third * WIDTH, WIDTH)
        thirds.append(
            Gather(
                qkv_ref.at[:, columns], qkv_full.at[:, :, :, columns], 640,
                *scratch[3 * third + 3 : 3 * third + 6],
            )
        )
    one, two, three = thirds
    exchange = Exchange(*scratch[12:18])
    exchange_back = Exchange(*scratch[18:24])
    group_at = exchange.group
    work, got = scratch[24 : 24 + count], scratch[24 + count :]
    got = [got[4 * group : 4 * group + 4] for group in range(count)]
    halving = Halving(
        (both_qkv, both_proj), (left_qkv, left_proj), (twin_qkv, twin_proj), work, got,
        step_send, step_recv,
    )
    others = []
    for step_hi in range(2):
        for step_pair in range(4):
            if step_hi + step_pair > 0:
                to_hi, to_pair = (hi + step_hi) % 2, (pair + step_pair) % 4
                others.append(
                    (step_hi * 4 + step_pair, to_hi, to_pair,
                     device(to_hi, core, to_pair * 2 + near, lo, x))
                )
    meet(
        [twin, proj.across] + [other[3] for other in others[3:]] + exchange.plane + exchange.line
    )
    for gather in (proj, one, two, three):
        gather.start()
    for copy in staged:
        copy.wait()
    cosine, sine = turn_tables(angles_ref[...], HEAD // 4)
    for source, target in ((query_ref, turned_query), (key_ref, turned_key)):
        values = source[...].astype(jnp.float32)
        target[...] = turn(values, cosine, sine, HEAD // 4, 1.0).astype(jnp.bfloat16)
    wide[...] = jnp.zeros_like(wide)

    def heads(first):
        space_forward(
            range(first, first + 4), turned_query, turned_key, value_ref, weights_ref, wide
        )

    proj.spread()
    heads(0)
    one.spread()
    heads(4)
    proj.pass_on()
    heads(8)
    two.spread()
    proj.last()
    heads(12)
    one.pass_on()
    mixed = wide[...].astype(jnp.bfloat16)
    mixed_ref[...] = mixed
    proj.arrive()
    for block in range(3):
        columns = slice(block * 384, block * 384 + 384)
        wide[:, columns] = hidden_ref[:, columns].astype(jnp.float32) + jnp.dot(
            mixed_ref[...], weight_rows(proj_full, columns), preferred_element_type=jnp.float32
        )
    exchange.start_plane(wide[...].astype(jnp.bfloat16))
    three.spread()
    one.last()
    for side in range(2):
        right_proj[side] = core_columns(mixed_ref[...], side)
    exchange.start_line()
    two.pass_on()
    two.last()
    three.pass_on()
    three.last()
    for gather in thirds:
        gather.arrive()
    back_rows = time_sublayer(
        exchange.finish(), qkv_full, scale_ref, shift_ref, grad_time, time_angles,
        right_qkv, projected, sums_ref, normed, time_wide, turned, total_back, modulated,
    )
    own, other = pl.ds(0, 128), pl.ds(128, 128)
    exchange_back.start_plane(back_rows)
    sums = [
        send(sums_ref, plane_sums.at[group_at], sum_sends, sum_recvs, step, exchange.plane[step - 1])
        for step in range(1, 8)
    ]
    plane_sums[group_at] = sums_ref[...]
    piece_rows(projected, left_qkv, tall)
    twins = [
        send(right_qkv.at[1 - core], both_qkv.at[other], twin_send, twin_recv, 0, twin),
        send(left_qkv, twin_qkv, twin_send, twin_recv, 1, twin),
        send(right_proj.at[1 - core], both_proj.at[other], twin_send, twin_recv, 2, twin),
    ]
    both_qkv[own] = right_qkv[core]
    both_proj[own] = right_proj[core]
    twins[0].wait_recv()
    twins[1].wait_recv()
    for group in range(2):
        halving.begin(group)
    exchange_back.start_line()
    for copy in sums:
        copy.wait_recv()
    line_sums[z] = jnp.sum(plane_sums[...], axis=0)
    more = [
        send(
            line_sums.at[z], line_sums.at[z], sum_sends, sum_recvs, 8 + step,
            exchange.line[step - 1],
        )
        for step in range(1, 8)
    ]
    for group in range(2, 4):
        halving.begin(group)
    for group in range(4):
        halving.keep(group)
    row = lax.broadcasted_iota(jnp.int32, (PROJ_ROWS, WIDTH), 0)
    column = lax.broadcasted_iota(jnp.int32, (PROJ_ROWS, WIDTH), 1)
    piece = WIDTH // 64
    wanted = jnp.where(row < 4 * piece, row // piece * (16 * piece) + row % piece, -WIDTH)
    ahead = column - wanted
    frames = exchange_back.finish()
    hidden = resid_ref[...].astype(jnp.float32) + frames.astype(jnp.float32)
    hidden_out[...] = hidden.astype(jnp.bfloat16)
    for block in range(16):
        chosen = jnp.where(ahead == block * piece, 1.0, 0.0).astype(jnp.bfloat16)
        left_proj[block] = across_rows(chosen, hidden_out[...]).astype(jnp.bfloat16)
    twins.append(send(left_proj, twin_proj, twin_send, twin_recv, 3, twin))
    for block in range(3):
        columns = slice(block * 384, block * 384 + 384)
        part = across_rows(hidden_out[:, columns], weight_rows(proj_full, columns))
        if block == 0:
            total_query[...] = part
        else:
            total_query[...] += part
    grad[...] = total_query[...].astype(jnp.bfloat16)
    twins[2].wait_recv()
    twins[3].wait_recv()
    for group in range(4, 6):
        halving.begin(group)
    for group in range(4, 6):
        halving.keep(group)
    for group in range(4):
        halving.advance(group, 1)
    totals = (total_query, total_key, total_value)
    for total in totals:
        total[...] = jnp.zeros_like(total)

    def heads(first, end):
        space_back_heads(
            range(first, end), weights_ref, turned_query, turned_key, value_ref, grad, totals
        )

    heads(0, 10)
    for group in range(4):
        halving.advance(group, 2)
    heads(10, 16)
    for group in range(4, 6):
        halving.advance(group, 1)
    for group in range(4):
        halving.advance(group, 3)
    cosine, sine = turn_tables(angles_ref[...], HEAD // 4)
    for total, out in ((total_query, query_out), (total_key, key_out)):
        out[...] = turn(total[...], cosine, sine, HEAD // 4, -1.0).astype(jnp.bfloat16)
    value_out[...] = total_value[...].astype(jnp.bfloat16)
    for copy in more:
        copy.wait_recv()
    total_ref[...] = jnp.sum(line_sums[...], axis=0)
    for group in range(4, 6):
        halving.advance(group, 2)
    for group in range(4):
        halving.last(group, qkv_last)
    ends = []
    for slot, to_hi, to_pair, peer in others:
        rows = pl.ds(pl.multiple_of(to_pair * 48, 16), QKV_WINDOW)
        ends.append(
            send(qkv_last.at[to_hi, rows], qkv_final.at[slot], final_send, final_recv, slot, peer)
        )
    for group in range(4, 6):
        halving.advance(group, 3)
    for group in range(4, 6):
        halving.last(group, proj_last)
    for slot, to_hi, to_pair, peer in others:
        rows = pl.ds(pl.multiple_of(to_pair * 16, 16), PROJ_WINDOW)
        ends.append(
            send(
                proj_last.at[to_hi, rows], proj_final.at[slot], final_send, final_recv, 8 + slot,
                peer,
            )
        )
    total = qkv_last[hi, pl.ds(pl.multiple_of(pair * 48, 16), QKV_WINDOW)].astype(jnp.float32)
    for (slot, _, _, _), copy in zip(others, ends[:7]):
        copy.wait_recv()
        total += qkv_final[slot].astype(jnp.float32)
    total = pltpu.roll(pltpu.roll(total, (QKV_WINDOW - pair * 6) % QKV_WINDOW, 0), (KEEP_LANES - hi * 32) % KEEP_LANES, 1)
    qkv_out[...] = total
    total = proj_last[hi, pl.ds(pl.multiple_of(pair * 16, 16), PROJ_WINDOW)].astype(jnp.float32)
    for (slot, _, _, _), copy in zip(others, ends[7:]):
        copy.wait_recv()
        total += proj_final[slot].astype(jnp.float32)
    total = pltpu.roll(pltpu.roll(total, (PROJ_WINDOW - pair * 2) % PROJ_WINDOW, 0), (KEEP_LANES - hi * 32) % KEEP_LANES, 1)
    proj_out[...] = total
    for copy in twins + sums + more + list(halving.copies.values()) + ends:
        copy.wait_send()
    for gather in (proj, one, two, three):
        gather.finish()


def whole(angles, time_angles, scale, shift, query, key, value, hidden, grad_time, resid, proj, qkv):
    vmem, away = pl.BlockSpec(memory_space=pltpu.VMEM), pl.BlockSpec(memory_space=pltpu.HBM)
    b16, f32 = jnp.bfloat16, jnp.float32
    shape, dma = pltpu.VMEM, pltpu.SemaphoreType.DMA
    wide, sums = (128, 3 * WIDTH), (2, WIDTH)
    outs = [ROWS] * 4 + [
        (sums, f32), ((QKV_WINDOW, KEEP_LANES), f32), ((PROJ_WINDOW, KEEP_LANES), f32)
    ]
    counts = [last - first for _, first, last, _ in GROUPS]
    scratch = [shape(*ROWS)] * 6 + [
        dma((6,)),
        shape(*ROWS), shape(*ROWS), shape((HEADS, 128, 128), f32),
        shape((4, 4, 80, WIDTH), b16), shape((4, 4, 80, 3 * WIDTH), b16),
        shape(*WIDE_ROWS), shape(*ROWS), shape(*RIGHT), shape(*RIGHT), shape(wide, b16),
        shape(sums, f32), shape(*WIDE_ROWS), shape(wide, f32), shape(wide, b16),
        shape(*WIDE_ROWS), shape(*ROWS), shape((3 * WIDTH, 128), f32),
        shape((16, QKV_ROWS, 128), b16), shape((16, PROJ_ROWS, 128), b16),
        shape((256, HALF_LANES), b16), shape((256, HALF_LANES), b16),
        shape((16, QKV_ROWS, 128), b16), shape((16, PROJ_ROWS, 128), b16), dma((4,)), dma((4,)),
        shape(*WIDE_ROWS), shape(*WIDE_ROWS), shape(*WIDE_ROWS), shape(*ROWS),
        shape((8,) + sums, f32), shape((8,) + sums, f32), dma((16,)), dma((16,)),
        dma((6, 4)), dma((6, 4)),
        shape((2, QKV_ROWS, KEEP_LANES), b16), shape((2, PROJ_ROWS, KEEP_LANES), b16),
        shape((8, QKV_WINDOW, KEEP_LANES), b16), shape((8, PROJ_WINDOW, KEEP_LANES), b16),
        dma((16,)), dma((16,)),
    ] + GATHER_SCRATCH * 4 + EXCHANGE_SCRATCH * 2
    scratch += [shape((16, count, HALF_LANES), b16) for count in counts]
    scratch += [
        shape((8 >> step, count, HALF_LANES), b16) for count in counts for step in range(4)
    ]
    return pl.pallas_call(
        whole_kernel,
        out_shape=tuple(jax.ShapeDtypeStruct(*out) for out in outs),
        in_specs=[vmem] * 4 + [away] * 8,
        out_specs=(vmem,) * len(outs),
        scratch_shapes=scratch,
        compiler_params=pltpu.CompilerParams(
            collective_id=1, has_side_effects=True, vmem_limit_bytes=58 * 1024 * 1024
        ),
    )(angles, time_angles, scale, shift, query, key, value, hidden, grad_time, resid, proj, qkv)


def results_kernel(*refs):
    given, outs = refs[:7], refs[7:]
    for source, target in zip(given[:4], outs[:4]):
        target[...] = source[...]
    sums_ref, qkv_ref, proj_ref = given[4:]
    part = WIDTH // 4
    outs[4][...] = proj_ref[...].T[:part, : WIDTH // 64]
    outs[5][...] = qkv_ref[...].T[:part, : 3 * WIDTH // 64]
    outs[6][...] = sums_ref[0:1]
    outs[7][...] = sums_ref[1:2]


def results(*args):
    f32, part = jnp.float32, WIDTH // 4
    outs = [ROWS] * 4 + [
        ((part, WIDTH // 64), f32), ((part, 3 * WIDTH // 64), f32), ((1, WIDTH), f32), ((1, WIDTH), f32)
    ]
    return local_call(results_kernel, outs, [], 16, *args)


def turn_angles(places, half):
    frequency = 10000.0 ** (-jnp.arange(half, dtype=jnp.float32) / half)
    angles = (places.astype(jnp.float32)[:, :, None] * frequency).reshape(128, 36)
    return jnp.pad(jnp.concatenate([jnp.cos(angles), jnp.sin(angles)], axis=1), ((0, 0), (0, 56)))


def body(
    hidden,
    query_space,
    key_space,
    value_space,
    positions,
    proj_space,
    shift_time,
    scale_time,
    qkv_time,
    grad_attn_time,
    grad_resid,
):
    seq_place = lax.axis_index("seq")
    frame_places = lax.dynamic_slice_in_dim(positions[0, 0], seq_place * 2, 2, 1).reshape(128, 1)
    spot_places = lax.dynamic_slice_in_dim(positions[1:, 0], seq_place, 1, 1).reshape(2, 128).T
    space_angles = turn_angles(spot_places, HEAD // 4)
    time_angles = turn_angles(frame_places, HEAD // 2)

    def flat(values):
        return values.reshape(128, WIDTH)

    sums_and_grads = whole(
        space_angles, time_angles, scale_time, shift_time, flat(query_space), flat(key_space),
        flat(value_space), flat(hidden), flat(grad_attn_time), flat(grad_resid), proj_space, qkv_time,
    )
    outs = results(*sums_and_grads)
    return tuple(out.reshape(hidden.shape) for out in outs[:4]) + tuple(outs[4:])


def solution(mesh):
    in_specs = (
        P("dp", "seq", None, None),
        P("dp", "seq", None, None),
        P("dp", "seq", None, None),
        P("dp", "seq", None, None),
        P(None, "dp", None, None),
        P("dp", None),
        P("dp", None),
        P("dp", None),
        P("dp", None),
        P("dp", None, "seq", None),
        P("dp", "seq", None, None),
    )
    out_specs = (
        P("dp", "seq", None, None),
        P("dp", "seq", None, None),
        P("dp", "seq", None, None),
        P("dp", "seq", None, None),
        P("dp", "seq"),
        P("dp", "seq"),
        P("dp", None),
        P("dp", None),
    )
    return jax.shard_map(body, mesh=mesh, in_specs=in_specs, out_specs=out_specs, check_vma=False)
```

```python
import math

import jax
import jax.numpy as jnp
import numpy as np
from jax import lax
from jax.experimental import pallas as pl
from jax.experimental.pallas import tpu as pltpu
from jax.sharding import PartitionSpec as P

HEADS = 16


epsilon = 1e-06


MESH = pl.DeviceIdType.MESH

HALF_LANES = 640
KEEP_LANES = 384
ORDER = ("x_near", "y_near", "x_far", "z_near")
GROUPS = (
    (0, 0, 64, 0), (0, 64, 128, 1), (0, 128, 176, 2), (0, 176, 224, 3), (1, 0, 16, 0), (1, 16, 32, 1),
    (1, 32, 48, 2), (1, 48, 80, 3),
)
QKV_ROWS, PROJ_ROWS = 224, 80
QKV_WINDOW, PROJ_WINDOW = 80, 32


def place():
    dp, seq = lax.axis_index("dp"), lax.axis_index("seq")
    hi, core = dp // 2, dp % 2
    z, lo, x = seq // 8, (seq // 4) % 2, seq % 4
    return hi, core, z, lo, x


def device(hi, core, z, lo, x):
    return (hi * 2 + core, z * 8 + lo * 4 + x)


def send(source, target, sends, recvs, at, peer):
    copy = pltpu.make_async_remote_copy(
        src_ref=source, dst_ref=target, send_sem=sends.at[at], recv_sem=recvs.at[at],
        device_id=peer, device_id_type=MESH,
    )
    copy.start()
    return copy


def greet(peers):
    barrier = pltpu.get_barrier_semaphore()
    for peer in peers:
        pl.semaphore_signal(barrier, inc=1, device_id=peer, device_id_type=MESH)


def order_of(group):
    return [ORDER[(GROUPS[group][3] + step) % 4] for step in range(4)]


def combination(group, block):
    bits = {name: (block // (8 >> step)) % 2 for step, name in enumerate(order_of(group))}
    x = bits["x_far"] * 2 + (bits["x_near"] + bits["x_far"]) % 2
    return bits["z_near"] * 8 + bits["y_near"] * 4 + x


class Halving:
    def __init__(self, right, left, twin_left, work, got, sends, recvs):
        self.right, self.left, self.twin_left = right, left, twin_left
        self.work, self.got, self.sends, self.recvs = work, got, sends, recvs
        hi, core, z, lo, x = place()
        near = z % 2
        self.bits = {"x_near": (x % 2 + x // 2) % 2, "x_far": x // 2, "y_near": lo, "z_near": near}
        self.partners = {
            "x_near": device(hi, core, z, lo, x + 1 - 2 * (x % 2)),
            "x_far": device(hi, core, z, lo, 3 - x),
            "y_near": device(hi, core, z, 1 - lo, x),
            "z_near": device(hi, core, z + 1 - 2 * near, lo, x),
        }
        self.base = [0] * len(GROUPS)
        self.copies = {}

    def fill(self, group, start):
        kind, first_row, last_row, _ = GROUPS[group]
        count, rows = last_row - first_row, slice(first_row, last_row)
        left, other = self.left[kind], self.twin_left[kind]
        work, right = self.work[group], self.right[kind]

        def four(at, _):
            first = start + at * 4
            parts = []
            for j in range(4):
                block = combination(group, first + j)
                parts.append(jnp.concatenate([left[block, rows], other[block, rows]], axis=1))
            total = jnp.dot(
                jnp.concatenate(parts, axis=0), right[...], preferred_element_type=jnp.float32
            )
            work[pl.ds(first, 4)] = total.astype(jnp.bfloat16).reshape(4, count, HALF_LANES)
            return 0

        lax.fori_loop(0, 2, four, 0)

    def send(self, group, step, first):
        name = order_of(group)[step]
        self.copies[group, step] = send(
            self.work[group].at[pl.ds(first, 8 >> step)], self.got[group][step],
            self.sends, self.recvs, (group, step), self.partners[name],
        )

    def begin(self, group):
        bit = self.bits[order_of(group)[0]]
        self.fill(group, (1 - bit) * 8)
        self.send(group, 0, (1 - bit) * 8)

    def keep(self, group):
        self.base[group] = self.bits[order_of(group)[0]] * 8
        self.fill(group, self.base[group])

    def take(self, group, step, start, count, offset):
        work, got = self.work[group], self.got[group][step]

        def one(at, _):
            total = work[start + at].astype(jnp.float32) + got[offset + at].astype(jnp.float32)
            work[start + at] = total.astype(jnp.bfloat16)
            return 0

        lax.fori_loop(0, count, one, 0)

    def advance(self, group, step):
        half, bit = 8 >> step, self.bits[order_of(group)[step]]
        away, mine = (1 - bit) * half, bit * half
        self.copies[group, step - 1].wait_recv()
        self.take(group, step - 1, self.base[group] + away, half, away)
        self.send(group, step, self.base[group] + away)
        self.take(group, step - 1, self.base[group] + mine, half, mine)
        self.base[group] = self.base[group] + mine

    def last(self, group, target):
        _, first_row, last_row, _ = GROUPS[group]
        self.copies[group, 3].wait_recv()
        total = self.work[group][self.base[group]].astype(jnp.float32)
        total = (total + self.got[group][3][0].astype(jnp.float32)).astype(jnp.bfloat16)
        target[0, first_row:last_row] = total[:, :KEEP_LANES]
        target[1, first_row:last_row] = total[:, HALF_LANES - KEEP_LANES :]


def near_peers():
    hi, core, z, lo, x = place()
    group = lo * 4 + x
    plane = [(hi * 2 + core, z * 8 + (group + step) % 8) for step in range(1, 8)]
    line = [(hi * 2 + core, ((z + step) % 8) * 8 + group) for step in range(1, 8)]
    return plane, line


def swap_eights(rows):
    count = rows.shape[0]
    at = lax.broadcasted_iota(jnp.int32, (count, count), 0)
    origin = lax.broadcasted_iota(jnp.int32, (count, count), 1)
    wanted = (at // 2 % 8) * 16 + at // 16 * 2 + at % 2
    chosen = jnp.where(origin == wanted, 1.0, 0.0).astype(jnp.bfloat16)
    moved = jnp.dot(chosen, rows, preferred_element_type=jnp.float32)
    return moved.astype(jnp.bfloat16)


class Exchange:
    def __init__(self, first, got_first, second, got_second, sends, recvs):
        self.first, self.got_first = first, got_first
        self.second, self.got_second = second, got_second
        self.sends, self.recvs = sends, recvs
        self.plane, self.line = near_peers()
        _, _, self.z, lo, x = place()
        self.group = lo * 4 + x

    def start_plane(self, rows):
        self.first[...] = swap_eights(rows).reshape(self.first.shape)
        self.copies = [
            send(
                self.first.at[(self.group + step) % 8], self.got_first.at[self.group],
                self.sends, self.recvs, step, self.plane[step - 1],
            )
            for step in range(1, 8)
        ]
        self.got_first[self.group] = self.first[self.group]

    def start_line(self):
        for copy in self.copies:
            copy.wait_recv()
        rows = self.got_first[...].reshape(128, -1)
        self.second[...] = swap_eights(rows).reshape(self.second.shape)
        more = [
            send(
                self.second.at[(self.z + step) % 8], self.got_second.at[self.z],
                self.sends, self.recvs, 8 + step, self.line[step - 1],
            )
            for step in range(1, 8)
        ]
        self.got_second[self.z] = self.second[self.z]
        self.copies = self.copies + more
        return more

    def finish(self):
        for copy in self.copies[7:]:
            copy.wait_recv()
        for copy in self.copies:
            copy.wait_send()
        return self.got_second[...].reshape(128, -1)


EXCHANGE_SCRATCH = [pltpu.VMEM((8, 16, 1152), jnp.bfloat16)] * 4 + [
    pltpu.SemaphoreType.DMA((16,)),
    pltpu.SemaphoreType.DMA((16,)),
]


class Gather:
    def __init__(self, own, full, cut, along_x, sends, recvs, local):
        self.own, self.full, self.cut = own, full, cut
        self.sends, self.recvs, self.local = sends, recvs, local
        hi, core, z, lo, x = place()
        self.mine, self.far = hi * 2 + core, (1 - hi) * 2 + core
        self.twin = device(hi, 1 - core, z, lo, x)
        self.across = device(1 - hi, core, z, 1 - lo, x)
        if along_x:
            self.spot, self.there = x, x
            self.right = device(hi, core, z, lo, (x + 1) % 4)
            self.left = device(hi, core, z, lo, (x + 3) % 4)
        else:
            self.spot = lo * 2 + (lo + z) % 2
            self.there = 3 - self.spot
            self.right, self.left = [
                device(hi, core, z // 2 * 2 + (at % 2 + at // 2) % 2, at // 2, x)
                for at in ((self.spot + 1) % 4, (self.spot + 3) % 4)
            ]
        self.copies = {}

    def go(self, at, source, target, peer):
        self.copies[at] = send(source, target, self.sends, self.recvs, at, peer)

    def same(self, at, ref, peer):
        self.go(at, ref, ref, peer)

    def start(self):
        start = pl.multiple_of(self.there * 64 + self.there // 2 * 16, 16)
        self.go(0, self.own.at[pl.ds(start, 80)], self.full.at[self.mine, self.there], self.across)
        self.locals = []
        for quarter, first in enumerate(STARTS):
            source, target = self.own.at[pl.ds(first, 80)], self.full.at[self.mine, quarter]
            self.go(10 + quarter, source, target, self.twin)
            copy = pltpu.make_async_copy(source, target, self.local.at[quarter])
            copy.start()
            self.locals.append(copy)

    def spread(self):
        self.copies[0].wait_recv()
        piece = self.full.at[self.far, self.spot]
        self.same(2, piece, self.right)
        self.same(3, piece, self.left)
        self.same(4, piece, self.twin)

    def pass_on(self):
        cut, width = self.cut, self.full.shape[3]
        self.copies[2].wait_recv()
        from_left = (self.far, (self.spot + 3) % 4)
        self.same(5, self.full.at[from_left + (slice(None), pl.ds(0, cut))], self.right)
        self.same(6, self.full.at[from_left], self.twin)
        self.copies[3].wait_recv()
        from_right = (self.far, (self.spot + 1) % 4)
        self.same(7, self.full.at[from_right + (slice(None), pl.ds(cut, width - cut))], self.left)
        self.same(8, self.full.at[from_right], self.twin)

    def last(self):
        self.copies[5].wait_recv()
        self.copies[7].wait_recv()
        self.same(9, self.full.at[self.far, (self.spot + 2) % 4], self.twin)

    def arrive(self):
        for copy in self.locals:
            copy.wait()
        for at in (4, 6, 8, 9, 10, 11, 12, 13):
            self.copies[at].wait_recv()

    def finish(self):
        for copy in self.copies.values():
            copy.wait_send()


STARTS = (0, 64, 144, 208)
GATHER_SCRATCH = [
    pltpu.SemaphoreType.DMA((14,)), pltpu.SemaphoreType.DMA((14,)), pltpu.SemaphoreType.DMA((4,))
]


def weight_rows(full, columns):
    return jnp.concatenate(
        [
            full[block, quarter, 16 * (quarter % 2) : 80, columns]
            for block in range(4)
            for quarter in range(4)
        ],
        axis=0,
    )


WIDTH = 1152
HEAD = WIDTH // HEADS
FACTOR = 1.0 / math.sqrt(HEAD)


def across_rows(left, right):
    return lax.dot_general(
        left, right, (((1,), (1,)), ((), ())), preferred_element_type=jnp.float32
    )


def down_rows(left, right):
    return lax.dot_general(
        left, right, (((0,), (0,)), ((), ())), preferred_element_type=jnp.float32
    )


def turn_tables(angles, half):
    lane = lax.broadcasted_iota(jnp.int32, (1, WIDTH), 1) % HEAD
    first = lane % (2 * half) < half
    origin = lane // (2 * half) * half + lane % half
    row = lax.broadcasted_iota(jnp.int32, (128, WIDTH), 0)
    cosine_at = jnp.where(row == origin, 1.0, 0.0).astype(jnp.bfloat16)
    sine_at = jnp.where(row == origin + 36, 1.0, 0.0) * jnp.where(first, -1.0, 1.0)
    sine_at = sine_at.astype(jnp.bfloat16)
    cosine = jnp.zeros((128, WIDTH), jnp.float32)
    sine = jnp.zeros((128, WIDTH), jnp.float32)
    rest = angles
    for _ in range(3):
        part = rest.astype(jnp.bfloat16)
        rest = rest - part.astype(jnp.float32)
        cosine += jnp.dot(part, cosine_at, preferred_element_type=jnp.float32)
        sine += jnp.dot(part, sine_at, preferred_element_type=jnp.float32)
    return cosine, sine


def make_angles(positions, rates, space_angles, time_angles):
    lane = lax.broadcasted_iota(jnp.int32, (128, 128), 1)
    token = lax.broadcasted_iota(jnp.int32, (128, 128), 0)
    frame = pl.ds(lax.axis_index("seq"), 1)

    def spots(axis):
        places = positions[axis, 0, frame, :].astype(jnp.float32)
        return jnp.broadcast_to(places, (128, 128)).T

    stride = positions[0, 0, 1:2, 0:1].astype(jnp.float32)
    frames = jnp.broadcast_to(stride, (128, 128)) * (token // 2).astype(jnp.float32)
    by_row = lane % (HEAD // 2) < HEAD // 4
    for at, places, out in (
        (0, jnp.where(by_row, spots(1), spots(2)), space_angles), (1, frames, time_angles)
    ):
        angles = places * rates[at : at + 1]
        turned = jnp.where(lane < HEAD // 2, jnp.cos(angles), jnp.sin(angles))
        out[...] = jnp.where(lane < HEAD, turned, 0.0)


def turn(values, cosine, sine, half, direction):
    lane = lax.broadcasted_iota(jnp.int32, (1, WIDTH), 1) % (2 * half)
    partner = jnp.where(
        lane < half, pltpu.roll(values, WIDTH - half, 1), pltpu.roll(values, half, 1)
    )
    return values * cosine + partner * (sine * direction)


def head_window(head):
    start = min(head * HEAD // 128 * 128, WIDTH - 256)
    lane = lax.broadcasted_iota(jnp.int32, (1, 256), 1) + start
    mask = jnp.where((lane >= head * HEAD) & (lane < (head + 1) * HEAD), 1.0, 0.0)
    return slice(start, start + 256), mask.astype(jnp.bfloat16)


def softmax_rows(scores):
    exponent = jnp.exp(scores - jnp.max(scores, axis=-1, keepdims=True))
    return exponent / jnp.sum(exponent, axis=-1, keepdims=True)


def head_back(weights, query, key, value, grad, mask):
    grad = grad * mask
    rounded = weights.astype(jnp.bfloat16)
    grad_weights = across_rows(grad, value)
    delta = jnp.sum(rounded.astype(jnp.float32) * grad_weights, axis=-1, keepdims=True)
    scores = (weights * (grad_weights - delta) * FACTOR).astype(jnp.bfloat16)
    return (
        jnp.dot(scores, key * mask, preferred_element_type=jnp.float32),
        down_rows(scores, query * mask),
        down_rows(rounded, grad),
    )


def space_forward(heads, turned_query, turned_key, value, weights_ref, mixed):
    for head in heads:
        window, mask = head_window(head)
        scores = across_rows(turned_query[:, window] * mask, turned_key[:, window]) * FACTOR
        weights = softmax_rows(scores)
        weights_ref[head] = weights
        mixed[:, window] += jnp.dot(
            weights.astype(jnp.bfloat16), value[:, window] * mask,
            preferred_element_type=jnp.float32,
        )


def space_back_heads(heads, weights, turned_query, turned_key, value, grad, totals):
    for head in heads:
        window, mask = head_window(head)
        parts = head_back(
            weights[head], turned_query[:, window], turned_key[:, window], value[:, window],
            grad[:, window], mask,
        )
        for total, part in zip(totals, parts):
            total[:, window] += part


def core_columns(rows, core):
    part = WIDTH // 4
    pieces = [rows[:, (hi * 2 + core) * part : (hi * 2 + core + 1) * part] for hi in range(2)]
    rest = jnp.zeros((rows.shape[0], HALF_LANES - 2 * part), rows.dtype)
    return jnp.concatenate(pieces + [rest], axis=1)


def stage(pairs, sems):
    copies = [
        pltpu.make_async_copy(source, target, sems.at[at]) for at, (source, target) in enumerate(pairs)
    ]
    for copy in copies:
        copy.start()
    return copies


ROWS = ((128, WIDTH), jnp.bfloat16)
WIDE_ROWS = ((128, WIDTH), jnp.float32)
RIGHT = ((2, 128, HALF_LANES), jnp.bfloat16)


def time_sublayer(
    rows, qkv_full, scale_ref, shift_ref, grad_ref, angles_ref,
    right_ref, projected_ref, sums_ref,
    normed_ref, wide, turned, total_back, modulated_ref,
):
    rows = rows.astype(jnp.float32)
    centered = rows - jnp.mean(rows, axis=-1, keepdims=True)
    inverse = lax.rsqrt(jnp.mean(centered * centered, axis=-1, keepdims=True) + epsilon)
    normed = centered * inverse
    normed_ref[...] = normed
    scale = 1.0 + scale_ref[...]
    modulated = (normed * scale + shift_ref[...]).astype(jnp.bfloat16)
    modulated_ref[...] = modulated
    for core in range(2):
        right_ref[core] = core_columns(modulated, core)
    for block in range(9):
        columns = slice(block * 384, block * 384 + 384)
        wide[:, columns] = jnp.dot(
            modulated_ref[...], weight_rows(qkv_full, columns), preferred_element_type=jnp.float32
        )
    cosine, sine = turn_tables(angles_ref[...], HEAD // 2)
    for block in range(2):
        columns = slice(block * WIDTH, block * WIDTH + WIDTH)
        turned[:, columns] = turn(wide[:, columns], cosine, sine, HEAD // 2, 1.0).astype(jnp.bfloat16)
    turned[:, 2 * WIDTH :] = wide[:, 2 * WIDTH :].astype(jnp.bfloat16)
    wide[...] = jnp.zeros_like(wide)
    spot_row = lax.broadcasted_iota(jnp.int32, (128, 128), 0) % 2
    spot_column = lax.broadcasted_iota(jnp.int32, (128, 128), 1) % 2
    together = spot_row == spot_column
    for head in range(HEADS):
        window, mask = head_window(head)
        windows = [slice(window.start + WIDTH * j, window.stop + WIDTH * j) for j in range(3)]
        query, key, value = [turned[:, columns] for columns in windows]
        scores = across_rows(query * mask, key) * FACTOR
        weights = softmax_rows(jnp.where(together, scores, -jnp.inf))
        parts = head_back(weights, query, key, value, grad_ref[:, window], mask)
        for columns, part in zip(windows, parts):
            wide[:, columns] += part
    for block in range(2):
        columns = slice(block * WIDTH, block * WIDTH + WIDTH)
        projected_ref[:, columns] = turn(wide[:, columns], cosine, sine, HEAD // 2, -1.0).astype(
            jnp.bfloat16
        )
    projected_ref[:, 2 * WIDTH :] = wide[:, 2 * WIDTH :].astype(jnp.bfloat16)
    for block in range(9):
        columns = slice(block * 384, block * 384 + 384)
        part = across_rows(projected_ref[:, columns], weight_rows(qkv_full, columns))
        if block == 0:
            total_back[...] = part
        else:
            total_back[...] += part
    grad = total_back[...]
    normed = normed_ref[...]
    sums_ref[0:1] = jnp.sum(grad, axis=0, keepdims=True)
    sums_ref[1:2] = jnp.sum(grad * normed, axis=0, keepdims=True)
    grad = grad * scale
    return (
        (
            grad
            - jnp.mean(grad, axis=-1, keepdims=True)
            - normed * jnp.mean(grad * normed, axis=-1, keepdims=True)
        )
        * inverse
    ).astype(jnp.bfloat16)


def piece_rows(values_ref, turned_rows, tall):
    for block in range(27):
        rows = slice(block * 128, block * 128 + 128)
        tall[rows] = values_ref[:, rows].astype(jnp.float32).T
    piece = 3 * WIDTH // 64
    for at in range(16):
        parts = [tall[(16 * k + at) * piece : (16 * k + at + 1) * piece] for k in range(4)]
        parts.append(jnp.zeros((QKV_ROWS - 4 * piece, 128), jnp.float32))
        turned_rows[at] = jnp.concatenate(parts, axis=0).astype(jnp.bfloat16)


def whole_kernel(
    scale_in, shift_in, positions_in, rates_in,
    query_in, key_in, value_in, hidden_in, grad_time_in, resid_in, proj_ref, qkv_ref,
    hidden_out, query_out, key_out, value_out, total_ref, qkv_out, proj_out,
    query_ref, key_ref, value_ref, hidden_ref, grad_time, resid_ref,
    scale_ref, shift_ref, positions, rates, angles_ref, time_angles, stage_sems,
    turned_query, turned_key, weights_ref, proj_full, qkv_full,
    wide, mixed_ref, right_qkv, right_proj, projected, sums_ref, normed, time_wide, turned,
    total_back, modulated, tall,
    left_qkv, left_proj, both_qkv, both_proj, twin_qkv, twin_proj, twin_send, twin_recv,
    total_query, total_key, total_value, grad,
    plane_sums, line_sums, sum_sends, sum_recvs,
    step_send, step_recv, qkv_last, proj_last, qkv_final, proj_final, final_send, final_recv,
    *scratch,
):
    staged = stage(
        [
            (query_in, query_ref), (key_in, key_ref), (value_in, value_ref),
            (hidden_in, hidden_ref), (grad_time_in, grad_time), (resid_in, resid_ref),
            (scale_in, scale_ref), (shift_in, shift_ref), (positions_in, positions), (rates_in, rates),
        ],
        stage_sems,
    )
    hi, core, z, lo, x = place()
    near, pair = z % 2, z // 2
    twin = device(hi, 1 - core, z, lo, x)
    count = len(GROUPS)
    proj = Gather(proj_ref, proj_full, 640, True, *scratch[:3])
    thirds = []
    for third in range(3):
        columns = pl.ds(third * WIDTH, WIDTH)
        thirds.append(
            Gather(
                qkv_ref.at[:, columns], qkv_full.at[:, :, :, columns], 640, third == 1,
                *scratch[3 * third + 3 : 3 * third + 6],
            )
        )
    one, two, three = thirds
    exchange = Exchange(*scratch[12:18])
    exchange_back = Exchange(*scratch[18:24])
    group_at = exchange.group
    work, got = scratch[24 : 24 + count], scratch[24 + count :]
    got = [got[4 * group : 4 * group + 4] for group in range(count)]
    halving = Halving(
        (both_qkv, both_proj), (left_qkv, left_proj), (twin_qkv, twin_proj), work, got,
        step_send, step_recv,
    )
    others = []
    for step_hi in range(2):
        for step_pair in range(4):
            if step_hi + step_pair > 0:
                to_hi, to_pair = (hi + step_hi) % 2, (pair + step_pair) % 4
                others.append(
                    (step_hi * 4 + step_pair, to_hi, to_pair,
                     device(to_hi, core, to_pair * 2 + near, lo, x))
                )
    peers = [twin, proj.across] + [other[3] for other in others[3:]] + exchange.plane + exchange.line
    greet(peers)
    for copy in staged:
        copy.wait()
    make_angles(positions, rates, angles_ref, time_angles)
    cosine, sine = turn_tables(angles_ref[...], HEAD // 4)
    for source, target in ((query_ref, turned_query), (key_ref, turned_key)):
        values = source[...].astype(jnp.float32)
        target[...] = turn(values, cosine, sine, HEAD // 4, 1.0).astype(jnp.bfloat16)
    wide[...] = jnp.zeros_like(wide)
    pl.semaphore_wait(pltpu.get_barrier_semaphore(), len(peers))
    for gather in (proj, one, two, three):
        gather.start()

    def heads(first):
        space_forward(
            range(first, first + 4), turned_query, turned_key, value_ref, weights_ref, wide
        )

    proj.spread()
    heads(0)
    one.spread()
    heads(4)
    proj.pass_on()
    heads(8)
    two.spread()
    proj.last()
    heads(12)
    one.pass_on()
    mixed = wide[...].astype(jnp.bfloat16)
    mixed_ref[...] = mixed
    proj.arrive()
    for block in range(3):
        columns = slice(block * 384, block * 384 + 384)
        wide[:, columns] = hidden_ref[:, columns].astype(jnp.float32) + jnp.dot(
            mixed_ref[...], weight_rows(proj_full, columns), preferred_element_type=jnp.float32
        )
    exchange.start_plane(wide[...].astype(jnp.bfloat16))
    three.spread()
    one.last()
    for side in range(2):
        right_proj[side] = core_columns(mixed_ref[...], side)
    exchange.start_line()
    two.pass_on()
    two.last()
    three.pass_on()
    three.last()
    for gather in thirds:
        gather.arrive()
    back_rows = time_sublayer(
        exchange.finish(), qkv_full, scale_ref, shift_ref, grad_time, time_angles,
        right_qkv, projected, sums_ref, normed, time_wide, turned, total_back, modulated,
    )
    own, other = pl.ds(0, 128), pl.ds(128, 128)
    exchange_back.start_plane(back_rows)
    sums = [
        send(sums_ref, plane_sums.at[group_at], sum_sends, sum_recvs, step, exchange.plane[step - 1])
        for step in range(1, 8)
    ]
    plane_sums[group_at] = sums_ref[...]
    piece_rows(projected, left_qkv, tall)
    twins = [
        send(right_qkv.at[1 - core], both_qkv.at[other], twin_send, twin_recv, 0, twin),
        send(left_qkv, twin_qkv, twin_send, twin_recv, 1, twin),
        send(right_proj.at[1 - core], both_proj.at[other], twin_send, twin_recv, 2, twin),
    ]
    both_qkv[own] = right_qkv[core]
    both_proj[own] = right_proj[core]
    twins[0].wait_recv()
    twins[1].wait_recv()
    for group in range(2):
        halving.begin(group)
    exchange_back.start_line()
    for copy in sums:
        copy.wait_recv()
    line_sums[z] = jnp.sum(plane_sums[...], axis=0)
    more = [
        send(
            line_sums.at[z], line_sums.at[z], sum_sends, sum_recvs, 8 + step,
            exchange.line[step - 1],
        )
        for step in range(1, 8)
    ]
    for group in range(2, 4):
        halving.begin(group)
    for group in range(4):
        halving.keep(group)
    row = lax.broadcasted_iota(jnp.int32, (PROJ_ROWS, WIDTH), 0)
    column = lax.broadcasted_iota(jnp.int32, (PROJ_ROWS, WIDTH), 1)
    piece = WIDTH // 64
    wanted = jnp.where(row < 4 * piece, row // piece * (16 * piece) + row % piece, -WIDTH)
    ahead = column - wanted
    frames = exchange_back.finish()
    hidden = resid_ref[...].astype(jnp.float32) + frames.astype(jnp.float32)
    hidden_out[...] = hidden.astype(jnp.bfloat16)
    for block in range(16):
        chosen = jnp.where(ahead == block * piece, 1.0, 0.0).astype(jnp.bfloat16)
        left_proj[block] = across_rows(chosen, hidden_out[...]).astype(jnp.bfloat16)
    twins.append(send(left_proj, twin_proj, twin_send, twin_recv, 3, twin))
    for block in range(3):
        columns = slice(block * 384, block * 384 + 384)
        part = across_rows(hidden_out[:, columns], weight_rows(proj_full, columns))
        if block == 0:
            total_query[...] = part
        else:
            total_query[...] += part
    grad[...] = total_query[...].astype(jnp.bfloat16)
    twins[2].wait_recv()
    twins[3].wait_recv()
    for group in range(4, 8):
        halving.begin(group)
    for group in range(4, 8):
        halving.keep(group)
    for group in range(4):
        halving.advance(group, 1)
    totals = (total_query, total_key, total_value)
    for total in totals:
        total[...] = jnp.zeros_like(total)

    def heads(first, end):
        space_back_heads(
            range(first, end), weights_ref, turned_query, turned_key, value_ref, grad, totals
        )

    heads(0, 10)
    for group in range(4):
        halving.advance(group, 2)
    heads(10, 16)
    for group in range(4, 8):
        halving.advance(group, 1)
    for group in range(4):
        halving.advance(group, 3)
    cosine, sine = turn_tables(angles_ref[...], HEAD // 4)
    for total, out in ((total_query, query_out), (total_key, key_out)):
        out[...] = turn(total[...], cosine, sine, HEAD // 4, -1.0).astype(jnp.bfloat16)
    value_out[...] = total_value[...].astype(jnp.bfloat16)
    for copy in more:
        copy.wait_recv()
    total_ref[...] = jnp.sum(line_sums[...], axis=0)
    for group in range(4, 8):
        halving.advance(group, 2)
    for group in range(4):
        halving.last(group, qkv_last)
    ends = []
    for slot, to_hi, to_pair, peer in others:
        rows = pl.ds(pl.multiple_of(to_pair * 48, 16), QKV_WINDOW)
        ends.append(
            send(qkv_last.at[to_hi, rows], qkv_final.at[slot], final_send, final_recv, slot, peer)
        )
    for group in range(4, 8):
        halving.advance(group, 3)
    for group in range(4, 8):
        halving.last(group, proj_last)
    for slot, to_hi, to_pair, peer in others:
        rows = pl.ds(pl.multiple_of(to_pair * 16, 16), PROJ_WINDOW)
        ends.append(
            send(
                proj_last.at[to_hi, rows], proj_final.at[slot], final_send, final_recv, 8 + slot,
                peer,
            )
        )
    total = qkv_last[hi, pl.ds(pl.multiple_of(pair * 48, 16), QKV_WINDOW)].astype(jnp.float32)
    for (slot, _, _, _), copy in zip(others, ends[:7]):
        copy.wait_recv()
        total += qkv_final[slot].astype(jnp.float32)
    total = pltpu.roll(pltpu.roll(total, (QKV_WINDOW - pair * 6) % QKV_WINDOW, 0), (KEEP_LANES - hi * 32) % KEEP_LANES, 1)
    qkv_out[...] = total
    total = proj_last[hi, pl.ds(pl.multiple_of(pair * 16, 16), PROJ_WINDOW)].astype(jnp.float32)
    for (slot, _, _, _), copy in zip(others, ends[7:]):
        copy.wait_recv()
        total += proj_final[slot].astype(jnp.float32)
    total = pltpu.roll(pltpu.roll(total, (PROJ_WINDOW - pair * 2) % PROJ_WINDOW, 0), (KEEP_LANES - hi * 32) % KEEP_LANES, 1)
    proj_out[...] = total
    for copy in twins + sums + more + list(halving.copies.values()) + ends:
        copy.wait_send()
    for gather in (proj, one, two, three):
        gather.finish()


def whole(scale, shift, positions, rates, query, key, value, hidden, grad_time, resid, proj, qkv):
    vmem, away = pl.BlockSpec(memory_space=pltpu.VMEM), pl.BlockSpec(memory_space=pltpu.HBM)
    b16, f32 = jnp.bfloat16, jnp.float32
    shape, dma = pltpu.VMEM, pltpu.SemaphoreType.DMA
    wide, sums = (128, 3 * WIDTH), (2, WIDTH)
    outs = [ROWS] * 4 + [
        (sums, f32), ((QKV_WINDOW, KEEP_LANES), f32), ((PROJ_WINDOW, KEEP_LANES), f32)
    ]
    counts = [last - first for _, first, last, _ in GROUPS]
    scratch = [shape(*ROWS)] * 6 + [
        shape(scale.shape, f32), shape(scale.shape, f32), shape(positions.shape, positions.dtype),
        shape(rates.shape, f32), shape((128, 128), f32), shape((128, 128), f32), dma((10,)),
        shape(*ROWS), shape(*ROWS), shape((HEADS, 128, 128), f32),
        shape((4, 4, 80, WIDTH), b16), shape((4, 4, 80, 3 * WIDTH), b16),
        shape(*WIDE_ROWS), shape(*ROWS), shape(*RIGHT), shape(*RIGHT), shape(wide, b16),
        shape(sums, f32), shape(*WIDE_ROWS), shape(wide, f32), shape(wide, b16),
        shape(*WIDE_ROWS), shape(*ROWS), shape((3 * WIDTH, 128), f32),
        shape((16, QKV_ROWS, 128), b16), shape((16, PROJ_ROWS, 128), b16),
        shape((256, HALF_LANES), b16), shape((256, HALF_LANES), b16),
        shape((16, QKV_ROWS, 128), b16), shape((16, PROJ_ROWS, 128), b16), dma((4,)), dma((4,)),
        shape(*WIDE_ROWS), shape(*WIDE_ROWS), shape(*WIDE_ROWS), shape(*ROWS),
        shape((8,) + sums, f32), shape((8,) + sums, f32), dma((16,)), dma((16,)),
        dma((8, 4)), dma((8, 4)),
        shape((2, QKV_ROWS, KEEP_LANES), b16), shape((2, PROJ_ROWS, KEEP_LANES), b16),
        shape((8, QKV_WINDOW, KEEP_LANES), b16), shape((8, PROJ_WINDOW, KEEP_LANES), b16),
        dma((16,)), dma((16,)),
    ] + GATHER_SCRATCH * 4 + EXCHANGE_SCRATCH * 2
    scratch += [shape((16, count, HALF_LANES), b16) for count in counts]
    scratch += [
        shape((8 >> step, count, HALF_LANES), b16) for count in counts for step in range(4)
    ]
    return pl.pallas_call(
        whole_kernel,
        out_shape=tuple(jax.ShapeDtypeStruct(*out) for out in outs),
        in_specs=[away] * 12,
        out_specs=(vmem,) * len(outs),
        scratch_shapes=scratch,
        compiler_params=pltpu.CompilerParams(
            collective_id=1, has_side_effects=True, vmem_limit_bytes=58 * 1024 * 1024
        ),
    )(scale, shift, positions, rates, query, key, value, hidden, grad_time, resid, proj, qkv)


def results_kernel(*refs):
    given, outs, (sums_ref, qkv_ref, proj_ref, sems) = refs[:7], refs[7:15], refs[15:]
    copies = stage(
        list(zip(given[4:], (sums_ref, qkv_ref, proj_ref))) + list(zip(given[:4], outs[:4])), sems
    )
    for copy in copies[:3]:
        copy.wait()
    part = WIDTH // 4
    outs[4][...] = proj_ref[: WIDTH // 64, :part]
    outs[5][...] = qkv_ref[: 3 * WIDTH // 64, :part]
    outs[6][...] = sums_ref[0:1]
    outs[7][...] = sums_ref[1:2]
    for copy in copies[3:]:
        copy.wait()


def results(*args):
    f32, part = jnp.float32, WIDTH // 4
    outs = [ROWS] * 4 + [
        ((WIDTH // 64, part), f32), ((3 * WIDTH // 64, part), f32), ((1, WIDTH), f32), ((1, WIDTH), f32)
    ]
    vmem, away = pl.BlockSpec(memory_space=pltpu.VMEM), pl.BlockSpec(memory_space=pltpu.HBM)
    return pl.pallas_call(
        results_kernel,
        out_shape=tuple(jax.ShapeDtypeStruct(shape, kind) for shape, kind in outs),
        in_specs=[away] * 7,
        out_specs=(away,) * 4 + (vmem,) * 4,
        scratch_shapes=[pltpu.VMEM(arg.shape, arg.dtype) for arg in args[4:]]
        + [pltpu.SemaphoreType.DMA((7,))],
        compiler_params=pltpu.CompilerParams(vmem_limit_bytes=58 * 1024 * 1024),
    )(*args)


def turn_rates():
    rows = []
    for half in (HEAD // 4, HEAD // 2):
        frequency = np.float32(10000.0) ** (-np.arange(half, dtype=np.float32) / np.float32(half))
        rows.append(np.pad(np.tile(frequency, HEAD // half), (0, 56)))
    return np.stack(rows + [np.zeros(128)] * 6).astype(np.float32)


def body(
    hidden,
    query_space,
    key_space,
    value_space,
    positions,
    proj_space,
    shift_time,
    scale_time,
    qkv_time,
    grad_attn_time,
    grad_resid,
):
    def flat(values):
        return values.reshape(128, WIDTH)

    outs = results(
        *whole(
            scale_time, shift_time, positions, turn_rates(), flat(query_space), flat(key_space),
            flat(value_space), flat(hidden), flat(grad_attn_time), flat(grad_resid), proj_space,
            qkv_time,
        )
    )
    grads = tuple(out.reshape(hidden.shape) for out in outs[:4])
    return grads + (outs[4].T, outs[5].T, outs[6], outs[7])


def solution(mesh):
    in_specs = (
        P("dp", "seq", None, None),
        P("dp", "seq", None, None),
        P("dp", "seq", None, None),
        P("dp", "seq", None, None),
        P(None, "dp", None, None),
        P("dp", None),
        P("dp", None),
        P("dp", None),
        P("dp", None),
        P("dp", None, "seq", None),
        P("dp", "seq", None, None),
    )
    out_specs = (
        P("dp", "seq", None, None),
        P("dp", "seq", None, None),
        P("dp", "seq", None, None),
        P("dp", "seq", None, None),
        P("dp", "seq"),
        P("dp", "seq"),
        P("dp", None),
        P("dp", None),
    )
    return jax.shard_map(body, mesh=mesh, in_specs=in_specs, out_specs=out_specs, check_vma=False)
```

```python
import math

import jax
import jax.numpy as jnp
import numpy as np
from jax import lax
from jax.experimental import pallas as pl
from jax.experimental.pallas import tpu as pltpu
from jax.sharding import PartitionSpec as P

HEADS = 16


epsilon = 1e-06


MESH = pl.DeviceIdType.MESH

HALF_LANES = 640
KEEP_LANES = 384
ORDER = ("x_near", "y_near", "x_far", "z_near")
GROUPS = (
    (0, 0, 64, 0), (0, 64, 128, 1), (0, 128, 176, 2), (0, 176, 224, 3), (1, 0, 16, 0), (1, 16, 32, 1),
    (1, 32, 48, 2), (1, 48, 80, 3),
)
QKV_ROWS, PROJ_ROWS = 224, 80
QKV_WINDOW, PROJ_WINDOW = 80, 32


def place():
    dp, seq = lax.axis_index("dp"), lax.axis_index("seq")
    hi, core = dp // 2, dp % 2
    z, lo, x = seq // 8, (seq // 4) % 2, seq % 4
    return hi, core, z, lo, x


def device(hi, core, z, lo, x):
    return (hi * 2 + core, z * 8 + lo * 4 + x)


def send(source, target, sends, recvs, at, peer):
    copy = pltpu.make_async_remote_copy(
        src_ref=source, dst_ref=target, send_sem=sends.at[at], recv_sem=recvs.at[at],
        device_id=peer, device_id_type=MESH,
    )
    copy.start()
    return copy


def greet(peers):
    barrier = pltpu.get_barrier_semaphore()
    for peer in peers:
        pl.semaphore_signal(barrier, inc=1, device_id=peer, device_id_type=MESH)


def order_of(group):
    return [ORDER[(GROUPS[group][3] + step) % 4] for step in range(4)]


def combination(group, block):
    bits = {name: (block // (8 >> step)) % 2 for step, name in enumerate(order_of(group))}
    x = bits["x_far"] * 2 + (bits["x_near"] + bits["x_far"]) % 2
    return bits["z_near"] * 8 + bits["y_near"] * 4 + x


class Halving:
    def __init__(self, right, left, twin_left, work, got, sends, recvs):
        self.right, self.left, self.twin_left = right, left, twin_left
        self.work, self.got, self.sends, self.recvs = work, got, sends, recvs
        hi, core, z, lo, x = place()
        near = z % 2
        self.bits = {"x_near": (x % 2 + x // 2) % 2, "x_far": x // 2, "y_near": lo, "z_near": near}
        self.partners = {
            "x_near": device(hi, core, z, lo, x + 1 - 2 * (x % 2)),
            "x_far": device(hi, core, z, lo, 3 - x),
            "y_near": device(hi, core, z, 1 - lo, x),
            "z_near": device(hi, core, z + 1 - 2 * near, lo, x),
        }
        self.base = [0] * len(GROUPS)
        self.copies = {}

    def fill(self, group, start):
        kind, first_row, last_row, _ = GROUPS[group]
        count, rows = last_row - first_row, slice(first_row, last_row)
        left, other = self.left[kind], self.twin_left[kind]
        work, right = self.work[group], self.right[kind]

        def four(at, _):
            first = start + at * 4
            parts = []
            for j in range(4):
                block = combination(group, first + j)
                parts.append(jnp.concatenate([left[block, rows], other[block, rows]], axis=1))
            total = jnp.dot(
                jnp.concatenate(parts, axis=0), right[...], preferred_element_type=jnp.float32
            )
            work[pl.ds(first, 4)] = total.astype(jnp.bfloat16).reshape(4, count, HALF_LANES)
            return 0

        lax.fori_loop(0, 2, four, 0)

    def send(self, group, step, first):
        name = order_of(group)[step]
        self.copies[group, step] = send(
            self.work[group].at[pl.ds(first, 8 >> step)], self.got[group][step],
            self.sends, self.recvs, (group, step), self.partners[name],
        )

    def begin(self, group):
        bit = self.bits[order_of(group)[0]]
        self.fill(group, (1 - bit) * 8)
        self.send(group, 0, (1 - bit) * 8)

    def keep(self, group):
        self.base[group] = self.bits[order_of(group)[0]] * 8
        self.fill(group, self.base[group])

    def take(self, group, step, start, count, offset):
        work, got = self.work[group], self.got[group][step]

        def one(at, _):
            total = work[start + at].astype(jnp.float32) + got[offset + at].astype(jnp.float32)
            work[start + at] = total.astype(jnp.bfloat16)
            return 0

        lax.fori_loop(0, count, one, 0)

    def advance(self, group, step):
        half, bit = 8 >> step, self.bits[order_of(group)[step]]
        away, mine = (1 - bit) * half, bit * half
        self.copies[group, step - 1].wait_recv()
        self.take(group, step - 1, self.base[group] + away, half, away)
        self.send(group, step, self.base[group] + away)
        self.take(group, step - 1, self.base[group] + mine, half, mine)
        self.base[group] = self.base[group] + mine

    def last(self, group, target):
        _, first_row, last_row, _ = GROUPS[group]
        self.copies[group, 3].wait_recv()
        total = self.work[group][self.base[group]].astype(jnp.float32)
        total = (total + self.got[group][3][0].astype(jnp.float32)).astype(jnp.bfloat16)
        target[0, first_row:last_row] = total[:, :KEEP_LANES]
        target[1, first_row:last_row] = total[:, HALF_LANES - KEEP_LANES :]


def near_peers():
    hi, core, z, lo, x = place()
    group = lo * 4 + x
    plane = [(hi * 2 + core, z * 8 + (group + step) % 8) for step in range(1, 8)]
    line = [(hi * 2 + core, ((z + step) % 8) * 8 + group) for step in range(1, 8)]
    return plane, line


def swap_eights(rows):
    count = rows.shape[0]
    at = lax.broadcasted_iota(jnp.int32, (count, count), 0)
    origin = lax.broadcasted_iota(jnp.int32, (count, count), 1)
    wanted = (at // 2 % 8) * 16 + at // 16 * 2 + at % 2
    chosen = jnp.where(origin == wanted, 1.0, 0.0).astype(jnp.bfloat16)
    moved = jnp.dot(chosen, rows, preferred_element_type=jnp.float32)
    return moved.astype(jnp.bfloat16)


class Exchange:
    def __init__(self, first, got_first, second, got_second, sends, recvs):
        self.first, self.got_first = first, got_first
        self.second, self.got_second = second, got_second
        self.sends, self.recvs = sends, recvs
        self.plane, self.line = near_peers()
        _, _, self.z, lo, x = place()
        self.group = lo * 4 + x

    def start_plane(self, rows):
        self.first[...] = swap_eights(rows).reshape(self.first.shape)
        self.copies = [
            send(
                self.first.at[(self.group + step) % 8], self.got_first.at[self.group],
                self.sends, self.recvs, step, self.plane[step - 1],
            )
            for step in range(1, 8)
        ]
        self.got_first[self.group] = self.first[self.group]

    def start_line(self):
        for copy in self.copies:
            copy.wait_recv()
        rows = self.got_first[...].reshape(128, -1)
        self.second[...] = swap_eights(rows).reshape(self.second.shape)
        more = [
            send(
                self.second.at[(self.z + step) % 8], self.got_second.at[self.z],
                self.sends, self.recvs, 8 + step, self.line[step - 1],
            )
            for step in range(1, 8)
        ]
        self.got_second[self.z] = self.second[self.z]
        self.copies = self.copies + more
        return more

    def finish(self):
        for copy in self.copies[7:]:
            copy.wait_recv()
        for copy in self.copies:
            copy.wait_send()
        return self.got_second[...].reshape(128, -1)


EXCHANGE_SCRATCH = [pltpu.VMEM((8, 16, 1152), jnp.bfloat16)] * 4 + [
    pltpu.SemaphoreType.DMA((16,)),
    pltpu.SemaphoreType.DMA((16,)),
]


class Gather:
    def __init__(self, own, full, cut, along_x, sends, recvs, local):
        self.own, self.full, self.cut = own, full, cut
        self.sends, self.recvs, self.local = sends, recvs, local
        hi, core, z, lo, x = place()
        self.mine, self.far = hi * 2 + core, (1 - hi) * 2 + core
        self.twin = device(hi, 1 - core, z, lo, x)
        self.across = device(1 - hi, core, z, 1 - lo, x)
        if along_x:
            self.spot, self.there = x, x
            self.right = device(hi, core, z, lo, (x + 1) % 4)
            self.left = device(hi, core, z, lo, (x + 3) % 4)
        else:
            self.spot = lo * 2 + (lo + z) % 2
            self.there = 3 - self.spot
            self.right, self.left = [
                device(hi, core, z // 2 * 2 + (at % 2 + at // 2) % 2, at // 2, x)
                for at in ((self.spot + 1) % 4, (self.spot + 3) % 4)
            ]
        self.copies = {}

    def go(self, at, source, target, peer):
        self.copies[at] = send(source, target, self.sends, self.recvs, at, peer)

    def same(self, at, ref, peer):
        self.go(at, ref, ref, peer)

    def start(self):
        start = pl.multiple_of(self.there * 64 + self.there // 2 * 16, 16)
        self.go(0, self.own.at[pl.ds(start, 80)], self.full.at[self.mine, self.there], self.across)
        self.locals = []
        for quarter, first in enumerate(STARTS):
            source, target = self.own.at[pl.ds(first, 80)], self.full.at[self.mine, quarter]
            self.go(10 + quarter, source, target, self.twin)
            copy = pltpu.make_async_copy(source, target, self.local.at[quarter])
            copy.start()
            self.locals.append(copy)

    def spread(self):
        self.copies[0].wait_recv()
        piece = self.full.at[self.far, self.spot]
        self.same(2, piece, self.right)
        self.same(3, piece, self.left)
        self.same(4, piece, self.twin)

    def pass_on(self):
        cut, width = self.cut, self.full.shape[3]
        self.copies[2].wait_recv()
        from_left = (self.far, (self.spot + 3) % 4)
        self.same(5, self.full.at[from_left + (slice(None), pl.ds(0, cut))], self.right)
        self.same(6, self.full.at[from_left], self.twin)
        self.copies[3].wait_recv()
        from_right = (self.far, (self.spot + 1) % 4)
        self.same(7, self.full.at[from_right + (slice(None), pl.ds(cut, width - cut))], self.left)
        self.same(8, self.full.at[from_right], self.twin)

    def last(self):
        self.copies[5].wait_recv()
        self.copies[7].wait_recv()
        self.same(9, self.full.at[self.far, (self.spot + 2) % 4], self.twin)

    def arrive(self):
        for copy in self.locals:
            copy.wait()
        for at in (4, 6, 8, 9, 10, 11, 12, 13):
            self.copies[at].wait_recv()

    def finish(self):
        for copy in self.copies.values():
            copy.wait_send()


STARTS = (0, 64, 144, 208)
GATHER_SCRATCH = [
    pltpu.SemaphoreType.DMA((14,)), pltpu.SemaphoreType.DMA((14,)), pltpu.SemaphoreType.DMA((4,))
]


def weight_rows(full, columns):
    return jnp.concatenate(
        [
            full[block, quarter, 16 * (quarter % 2) : 80, columns]
            for block in range(4)
            for quarter in range(4)
        ],
        axis=0,
    )


WIDTH = 1152
HEAD = WIDTH // HEADS
FACTOR = 1.0 / math.sqrt(HEAD)


def across_rows(left, right):
    return lax.dot_general(
        left, right, (((1,), (1,)), ((), ())), preferred_element_type=jnp.float32
    )


def down_rows(left, right):
    return lax.dot_general(
        left, right, (((0,), (0,)), ((), ())), preferred_element_type=jnp.float32
    )


def turn_tables(angles, half):
    lane = lax.broadcasted_iota(jnp.int32, (1, WIDTH), 1) % HEAD
    first = lane % (2 * half) < half
    origin = lane // (2 * half) * half + lane % half
    row = lax.broadcasted_iota(jnp.int32, (128, WIDTH), 0)
    cosine_at = jnp.where(row == origin, 1.0, 0.0).astype(jnp.bfloat16)
    sine_at = jnp.where(row == origin + 36, 1.0, 0.0) * jnp.where(first, -1.0, 1.0)
    sine_at = sine_at.astype(jnp.bfloat16)
    cosine = jnp.zeros((128, WIDTH), jnp.float32)
    sine = jnp.zeros((128, WIDTH), jnp.float32)
    rest = angles
    for _ in range(3):
        part = rest.astype(jnp.bfloat16)
        rest = rest - part.astype(jnp.float32)
        cosine += jnp.dot(part, cosine_at, preferred_element_type=jnp.float32)
        sine += jnp.dot(part, sine_at, preferred_element_type=jnp.float32)
    return cosine, sine


def make_angles(positions, rates, space_angles, time_angles):
    lane = lax.broadcasted_iota(jnp.int32, (128, 128), 1)
    token = lax.broadcasted_iota(jnp.int32, (128, 128), 0)
    frame = pl.ds(lax.axis_index("seq"), 1)

    def spots(axis):
        places = positions[axis, 0, frame, :].astype(jnp.float32)
        return jnp.broadcast_to(places, (128, 128)).T

    stride = positions[0, 0, 1:2, 0:1].astype(jnp.float32)
    frames = jnp.broadcast_to(stride, (128, 128)) * (token // 2).astype(jnp.float32)
    by_row = lane % (HEAD // 2) < HEAD // 4
    for at, places, out in (
        (0, jnp.where(by_row, spots(1), spots(2)), space_angles), (1, frames, time_angles)
    ):
        angles = places * rates[at : at + 1]
        turned = jnp.where(lane < HEAD // 2, jnp.cos(angles), jnp.sin(angles))
        out[...] = jnp.where(lane < HEAD, turned, 0.0)


def turn(values, cosine, sine, half, direction):
    lane = lax.broadcasted_iota(jnp.int32, (1, WIDTH), 1) % (2 * half)
    partner = jnp.where(
        lane < half, pltpu.roll(values, WIDTH - half, 1), pltpu.roll(values, half, 1)
    )
    return values * cosine + partner * (sine * direction)


def head_window(head):
    start = min(head * HEAD // 128 * 128, WIDTH - 256)
    lane = lax.broadcasted_iota(jnp.int32, (1, 256), 1) + start
    mask = jnp.where((lane >= head * HEAD) & (lane < (head + 1) * HEAD), 1.0, 0.0)
    return slice(start, start + 256), mask.astype(jnp.bfloat16)


def softmax_rows(scores):
    exponent = jnp.exp(scores - jnp.max(scores, axis=-1, keepdims=True))
    return exponent / jnp.sum(exponent, axis=-1, keepdims=True)


def head_back(weights, query, key, value, grad, mask):
    grad = grad * mask
    rounded = weights.astype(jnp.bfloat16)
    grad_weights = across_rows(grad, value)
    delta = jnp.sum(rounded.astype(jnp.float32) * grad_weights, axis=-1, keepdims=True)
    scores = (weights * (grad_weights - delta) * FACTOR).astype(jnp.bfloat16)
    return (
        jnp.dot(scores, key * mask, preferred_element_type=jnp.float32),
        down_rows(scores, query * mask),
        down_rows(rounded, grad),
    )


def space_forward(heads, turned_query, turned_key, value, weights_ref, mixed):
    for head in heads:
        window, mask = head_window(head)
        scores = across_rows(turned_query[:, window] * mask, turned_key[:, window]) * FACTOR
        weights = softmax_rows(scores)
        weights_ref[head] = weights
        mixed[:, window] += jnp.dot(
            weights.astype(jnp.bfloat16), value[:, window] * mask,
            preferred_element_type=jnp.float32,
        )


def space_back_heads(heads, weights, turned_query, turned_key, value, grad, totals):
    for head in heads:
        window, mask = head_window(head)
        parts = head_back(
            weights[head], turned_query[:, window], turned_key[:, window], value[:, window],
            grad[:, window], mask,
        )
        for total, part in zip(totals, parts):
            total[:, window] += part


def core_columns(rows, core):
    part = WIDTH // 4
    pieces = [rows[:, (hi * 2 + core) * part : (hi * 2 + core + 1) * part] for hi in range(2)]
    rest = jnp.zeros((rows.shape[0], HALF_LANES - 2 * part), rows.dtype)
    return jnp.concatenate(pieces + [rest], axis=1)


def stage(pairs, sems):
    copies = [
        pltpu.make_async_copy(source, target, sems.at[at]) for at, (source, target) in enumerate(pairs)
    ]
    for copy in copies:
        copy.start()
    return copies


ROWS = ((128, WIDTH), jnp.bfloat16)
WIDE_ROWS = ((128, WIDTH), jnp.float32)
RIGHT = ((2, 128, HALF_LANES), jnp.bfloat16)


def time_sublayer(
    rows, qkv_full, scale_ref, shift_ref, grad_ref, angles_ref,
    right_ref, projected_ref, sums_ref,
    normed_ref, wide, turned, total_back, modulated_ref,
):
    rows = rows.astype(jnp.float32)
    centered = rows - jnp.mean(rows, axis=-1, keepdims=True)
    inverse = lax.rsqrt(jnp.mean(centered * centered, axis=-1, keepdims=True) + epsilon)
    normed = centered * inverse
    normed_ref[...] = normed
    scale = 1.0 + scale_ref[...]
    modulated = (normed * scale + shift_ref[...]).astype(jnp.bfloat16)
    modulated_ref[...] = modulated
    for core in range(2):
        right_ref[core] = core_columns(modulated, core)
    for block in range(9):
        columns = slice(block * 384, block * 384 + 384)
        wide[:, columns] = jnp.dot(
            modulated_ref[...], weight_rows(qkv_full, columns), preferred_element_type=jnp.float32
        )
    cosine, sine = turn_tables(angles_ref[...], HEAD // 2)
    for block in range(2):
        columns = slice(block * WIDTH, block * WIDTH + WIDTH)
        turned[:, columns] = turn(wide[:, columns], cosine, sine, HEAD // 2, 1.0).astype(jnp.bfloat16)
    turned[:, 2 * WIDTH :] = wide[:, 2 * WIDTH :].astype(jnp.bfloat16)
    wide[...] = jnp.zeros_like(wide)
    spot_row = lax.broadcasted_iota(jnp.int32, (128, 128), 0) % 2
    spot_column = lax.broadcasted_iota(jnp.int32, (128, 128), 1) % 2
    together = spot_row == spot_column
    for head in range(HEADS):
        window, mask = head_window(head)
        windows = [slice(window.start + WIDTH * j, window.stop + WIDTH * j) for j in range(3)]
        query, key, value = [turned[:, columns] for columns in windows]
        scores = across_rows(query * mask, key) * FACTOR
        weights = softmax_rows(jnp.where(together, scores, -jnp.inf))
        parts = head_back(weights, query, key, value, grad_ref[:, window], mask)
        for columns, part in zip(windows, parts):
            wide[:, columns] += part
    for block in range(2):
        columns = slice(block * WIDTH, block * WIDTH + WIDTH)
        projected_ref[:, columns] = turn(wide[:, columns], cosine, sine, HEAD // 2, -1.0).astype(
            jnp.bfloat16
        )
    projected_ref[:, 2 * WIDTH :] = wide[:, 2 * WIDTH :].astype(jnp.bfloat16)
    for block in range(9):
        columns = slice(block * 384, block * 384 + 384)
        part = across_rows(projected_ref[:, columns], weight_rows(qkv_full, columns))
        if block == 0:
            total_back[...] = part
        else:
            total_back[...] += part
    grad = total_back[...]
    normed = normed_ref[...]
    sums_ref[0:1] = jnp.sum(grad, axis=0, keepdims=True)
    sums_ref[1:2] = jnp.sum(grad * normed, axis=0, keepdims=True)
    grad = grad * scale
    return (
        (
            grad
            - jnp.mean(grad, axis=-1, keepdims=True)
            - normed * jnp.mean(grad * normed, axis=-1, keepdims=True)
        )
        * inverse
    ).astype(jnp.bfloat16)


def piece_rows(values_ref, turned_rows, tall):
    for block in range(27):
        rows = slice(block * 128, block * 128 + 128)
        tall[rows] = values_ref[:, rows].astype(jnp.float32).T
    piece = 3 * WIDTH // 64
    for at in range(16):
        parts = [tall[(16 * k + at) * piece : (16 * k + at + 1) * piece] for k in range(4)]
        parts.append(jnp.zeros((QKV_ROWS - 4 * piece, 128), jnp.float32))
        turned_rows[at] = jnp.concatenate(parts, axis=0).astype(jnp.bfloat16)


def whole_kernel(
    scale_in, shift_in, positions_in, rates_in,
    query_in, key_in, value_in, hidden_in, grad_time_in, resid_in, proj_ref, qkv_ref,
    hidden_out, query_out, key_out, value_out, total_ref, qkv_out, proj_out,
    query_ref, key_ref, value_ref, hidden_ref, grad_time, resid_ref,
    scale_ref, shift_ref, positions, rates, angles_ref, time_angles, stage_sems,
    turned_query, turned_key, weights_ref, proj_full, qkv_full,
    wide, mixed_ref, right_qkv, right_proj, projected, sums_ref, normed, time_wide, turned,
    total_back, modulated, tall,
    left_qkv, left_proj, both_qkv, both_proj, twin_qkv, twin_proj, twin_send, twin_recv,
    total_query, total_key, total_value, grad,
    plane_sums, line_sums, sum_sends, sum_recvs,
    step_send, step_recv, qkv_last, proj_last, qkv_final, proj_final, final_send, final_recv,
    *scratch,
):
    staged = stage(
        [
            (query_in, query_ref), (key_in, key_ref), (value_in, value_ref),
            (hidden_in, hidden_ref), (grad_time_in, grad_time), (resid_in, resid_ref),
            (scale_in, scale_ref), (shift_in, shift_ref), (positions_in, positions), (rates_in, rates),
        ],
        stage_sems,
    )
    hi, core, z, lo, x = place()
    near, pair = z % 2, z // 2
    twin = device(hi, 1 - core, z, lo, x)
    count = len(GROUPS)
    proj = Gather(proj_ref, proj_full, 640, True, *scratch[:3])
    thirds = []
    for third in range(3):
        columns = pl.ds(third * WIDTH, WIDTH)
        thirds.append(
            Gather(
                qkv_ref.at[:, columns], qkv_full.at[:, :, :, columns], 640, third == 1,
                *scratch[3 * third + 3 : 3 * third + 6],
            )
        )
    one, two, three = thirds
    exchange = Exchange(*scratch[12:18])
    exchange_back = Exchange(*scratch[18:24])
    group_at = exchange.group
    work, got = scratch[24 : 24 + count], scratch[24 + count :]
    got = [got[4 * group : 4 * group + 4] for group in range(count)]
    halving = Halving(
        (both_qkv, both_proj), (left_qkv, left_proj), (twin_qkv, twin_proj), work, got,
        step_send, step_recv,
    )
    others = []
    for step_hi in range(2):
        for step_pair in range(4):
            if step_hi + step_pair > 0:
                to_hi, to_pair = (hi + step_hi) % 2, (pair + step_pair) % 4
                others.append(
                    (step_hi * 4 + step_pair, to_hi, to_pair,
                     device(to_hi, core, to_pair * 2 + near, lo, x))
                )
    peers = [twin, proj.across] + [other[3] for other in others[3:]] + exchange.plane + exchange.line
    greet(peers)
    for copy in staged:
        copy.wait()
    make_angles(positions, rates, angles_ref, time_angles)
    cosine, sine = turn_tables(angles_ref[...], HEAD // 4)
    for source, target in ((query_ref, turned_query), (key_ref, turned_key)):
        values = source[...].astype(jnp.float32)
        target[...] = turn(values, cosine, sine, HEAD // 4, 1.0).astype(jnp.bfloat16)
    wide[...] = jnp.zeros_like(wide)
    pl.semaphore_wait(pltpu.get_barrier_semaphore(), len(peers))
    for gather in (proj, one, two, three):
        gather.start()

    def heads(first):
        space_forward(
            range(first, first + 4), turned_query, turned_key, value_ref, weights_ref, wide
        )

    proj.spread()
    heads(0)
    one.spread()
    heads(4)
    proj.pass_on()
    heads(8)
    two.spread()
    proj.last()
    heads(12)
    one.pass_on()
    mixed = wide[...].astype(jnp.bfloat16)
    mixed_ref[...] = mixed
    proj.arrive()
    for block in range(3):
        columns = slice(block * 384, block * 384 + 384)
        wide[:, columns] = hidden_ref[:, columns].astype(jnp.float32) + jnp.dot(
            mixed_ref[...], weight_rows(proj_full, columns), preferred_element_type=jnp.float32
        )
    exchange.start_plane(wide[...].astype(jnp.bfloat16))
    three.spread()
    one.last()
    for side in range(2):
        right_proj[side] = core_columns(mixed_ref[...], side)
    exchange.start_line()
    two.pass_on()
    two.last()
    three.pass_on()
    three.last()
    for gather in thirds:
        gather.arrive()
    back_rows = time_sublayer(
        exchange.finish(), qkv_full, scale_ref, shift_ref, grad_time, time_angles,
        right_qkv, projected, sums_ref, normed, time_wide, turned, total_back, modulated,
    )
    own, other = pl.ds(0, 128), pl.ds(128, 128)
    exchange_back.start_plane(back_rows)
    sums = [
        send(sums_ref, plane_sums.at[group_at], sum_sends, sum_recvs, step, exchange.plane[step - 1])
        for step in range(1, 8)
    ]
    plane_sums[group_at] = sums_ref[...]
    piece_rows(projected, left_qkv, tall)
    twins = [
        send(right_qkv.at[1 - core], both_qkv.at[other], twin_send, twin_recv, 0, twin),
        send(left_qkv, twin_qkv, twin_send, twin_recv, 1, twin),
        send(right_proj.at[1 - core], both_proj.at[other], twin_send, twin_recv, 2, twin),
    ]
    both_qkv[own] = right_qkv[core]
    both_proj[own] = right_proj[core]
    twins[0].wait_recv()
    twins[1].wait_recv()
    for group in range(2):
        halving.begin(group)
    exchange_back.start_line()
    for copy in sums:
        copy.wait_recv()
    line_sums[z] = jnp.sum(plane_sums[...], axis=0)
    more = [
        send(
            line_sums.at[z], line_sums.at[z], sum_sends, sum_recvs, 8 + step,
            exchange.line[step - 1],
        )
        for step in range(1, 8)
    ]
    for group in range(2, 4):
        halving.begin(group)
    for group in range(4):
        halving.keep(group)
    row = lax.broadcasted_iota(jnp.int32, (PROJ_ROWS, WIDTH), 0)
    column = lax.broadcasted_iota(jnp.int32, (PROJ_ROWS, WIDTH), 1)
    piece = WIDTH // 64
    wanted = jnp.where(row < 4 * piece, row // piece * (16 * piece) + row % piece, -WIDTH)
    ahead = column - wanted
    frames = exchange_back.finish()
    hidden = resid_ref[...].astype(jnp.float32) + frames.astype(jnp.float32)
    hidden_out[...] = hidden.astype(jnp.bfloat16)
    for block in range(16):
        chosen = jnp.where(ahead == block * piece, 1.0, 0.0).astype(jnp.bfloat16)
        left_proj[block] = across_rows(chosen, hidden_out[...]).astype(jnp.bfloat16)
    twins.append(send(left_proj, twin_proj, twin_send, twin_recv, 3, twin))
    for block in range(3):
        columns = slice(block * 384, block * 384 + 384)
        part = across_rows(hidden_out[:, columns], weight_rows(proj_full, columns))
        if block == 0:
            total_query[...] = part
        else:
            total_query[...] += part
    grad[...] = total_query[...].astype(jnp.bfloat16)
    twins[2].wait_recv()
    twins[3].wait_recv()
    for group in range(4, 8):
        halving.begin(group)
    for group in range(4, 8):
        halving.keep(group)
    for group in range(4):
        halving.advance(group, 1)
    totals = (total_query, total_key, total_value)
    for total in totals:
        total[...] = jnp.zeros_like(total)

    def heads(first, end):
        space_back_heads(
            range(first, end), weights_ref, turned_query, turned_key, value_ref, grad, totals
        )

    heads(0, 10)
    for group in range(4):
        halving.advance(group, 2)
    heads(10, 16)
    for group in range(4, 8):
        halving.advance(group, 1)
    for group in range(4):
        halving.advance(group, 3)
    cosine, sine = turn_tables(angles_ref[...], HEAD // 4)
    for total, out in ((total_query, query_out), (total_key, key_out)):
        out[...] = turn(total[...], cosine, sine, HEAD // 4, -1.0).astype(jnp.bfloat16)
    value_out[...] = total_value[...].astype(jnp.bfloat16)
    for copy in more:
        copy.wait_recv()
    total_ref[...] = jnp.sum(line_sums[...], axis=0)
    for group in range(4, 8):
        halving.advance(group, 2)
    for group in range(4):
        halving.last(group, qkv_last)
    ends = []
    for slot, to_hi, to_pair, peer in others:
        rows = pl.ds(pl.multiple_of(to_pair * 48, 16), QKV_WINDOW)
        ends.append(
            send(qkv_last.at[to_hi, rows], qkv_final.at[slot], final_send, final_recv, slot, peer)
        )
    for group in range(4, 8):
        halving.advance(group, 3)
    for group in range(4, 8):
        halving.last(group, proj_last)
    for slot, to_hi, to_pair, peer in others:
        rows = pl.ds(pl.multiple_of(to_pair * 16, 16), PROJ_WINDOW)
        ends.append(
            send(
                proj_last.at[to_hi, rows], proj_final.at[slot], final_send, final_recv, 8 + slot,
                peer,
            )
        )
    total = qkv_last[hi, pl.ds(pl.multiple_of(pair * 48, 16), QKV_WINDOW)].astype(jnp.float32)
    for (slot, _, _, _), copy in zip(others, ends[:7]):
        copy.wait_recv()
        total += qkv_final[slot].astype(jnp.float32)
    total = pltpu.roll(pltpu.roll(total, (QKV_WINDOW - pair * 6) % QKV_WINDOW, 0), (KEEP_LANES - hi * 32) % KEEP_LANES, 1)
    qkv_out[...] = total
    total = proj_last[hi, pl.ds(pl.multiple_of(pair * 16, 16), PROJ_WINDOW)].astype(jnp.float32)
    for (slot, _, _, _), copy in zip(others, ends[7:]):
        copy.wait_recv()
        total += proj_final[slot].astype(jnp.float32)
    total = pltpu.roll(pltpu.roll(total, (PROJ_WINDOW - pair * 2) % PROJ_WINDOW, 0), (KEEP_LANES - hi * 32) % KEEP_LANES, 1)
    proj_out[...] = total
    for copy in twins + sums + more + list(halving.copies.values()) + ends:
        copy.wait_send()
    for gather in (proj, one, two, three):
        gather.finish()


def whole(scale, shift, positions, rates, query, key, value, hidden, grad_time, resid, proj, qkv):
    vmem, away = pl.BlockSpec(memory_space=pltpu.VMEM), pl.BlockSpec(memory_space=pltpu.HBM)
    b16, f32 = jnp.bfloat16, jnp.float32
    shape, dma = pltpu.VMEM, pltpu.SemaphoreType.DMA
    wide, sums = (128, 3 * WIDTH), (2, WIDTH)
    outs = [ROWS] * 4 + [
        (sums, f32), ((QKV_WINDOW, KEEP_LANES), f32), ((PROJ_WINDOW, KEEP_LANES), f32)
    ]
    counts = [last - first for _, first, last, _ in GROUPS]
    scratch = [shape(*ROWS)] * 6 + [
        shape(scale.shape, f32), shape(scale.shape, f32), shape(positions.shape, positions.dtype),
        shape(rates.shape, f32), shape((128, 128), f32), shape((128, 128), f32), dma((10,)),
        shape(*ROWS), shape(*ROWS), shape((HEADS, 128, 128), f32),
        shape((4, 4, 80, WIDTH), b16), shape((4, 4, 80, 3 * WIDTH), b16),
        shape(*WIDE_ROWS), shape(*ROWS), shape(*RIGHT), shape(*RIGHT), shape(wide, b16),
        shape(sums, f32), shape(*WIDE_ROWS), shape(wide, f32), shape(wide, b16),
        shape(*WIDE_ROWS), shape(*ROWS), shape((3 * WIDTH, 128), f32),
        shape((16, QKV_ROWS, 128), b16), shape((16, PROJ_ROWS, 128), b16),
        shape((256, HALF_LANES), b16), shape((256, HALF_LANES), b16),
        shape((16, QKV_ROWS, 128), b16), shape((16, PROJ_ROWS, 128), b16), dma((4,)), dma((4,)),
        shape(*WIDE_ROWS), shape(*WIDE_ROWS), shape(*WIDE_ROWS), shape(*ROWS),
        shape((8,) + sums, f32), shape((8,) + sums, f32), dma((16,)), dma((16,)),
        dma((8, 4)), dma((8, 4)),
        shape((2, QKV_ROWS, KEEP_LANES), b16), shape((2, PROJ_ROWS, KEEP_LANES), b16),
        shape((8, QKV_WINDOW, KEEP_LANES), b16), shape((8, PROJ_WINDOW, KEEP_LANES), b16),
        dma((16,)), dma((16,)),
    ] + GATHER_SCRATCH * 4 + EXCHANGE_SCRATCH * 2
    scratch += [shape((16, count, HALF_LANES), b16) for count in counts]
    scratch += [
        shape((8 >> step, count, HALF_LANES), b16) for count in counts for step in range(4)
    ]
    return pl.pallas_call(
        whole_kernel,
        out_shape=tuple(jax.ShapeDtypeStruct(*out) for out in outs),
        in_specs=[away] * 12,
        out_specs=(vmem,) * len(outs),
        scratch_shapes=scratch,
        compiler_params=pltpu.CompilerParams(
            collective_id=1, has_side_effects=True, vmem_limit_bytes=58 * 1024 * 1024
        ),
    )(scale, shift, positions, rates, query, key, value, hidden, grad_time, resid, proj, qkv)


def results_kernel(*refs):
    given, outs, (sums_ref, qkv_ref, proj_ref, sems) = refs[:7], refs[7:15], refs[15:]
    copies = stage(
        list(zip(given[4:], (sums_ref, qkv_ref, proj_ref))) + list(zip(given[:4], outs[:4])), sems
    )
    for copy in copies[:3]:
        copy.wait()
    part = WIDTH // 4
    outs[4][...] = proj_ref[: WIDTH // 64, :part]
    outs[5][...] = qkv_ref[: 3 * WIDTH // 64, :part]
    outs[6][...] = sums_ref[0:1]
    outs[7][...] = sums_ref[1:2]
    for copy in copies[3:]:
        copy.wait()


def results(*args):
    f32, part = jnp.float32, WIDTH // 4
    outs = [ROWS] * 4 + [
        ((WIDTH // 64, part), f32), ((3 * WIDTH // 64, part), f32), ((1, WIDTH), f32), ((1, WIDTH), f32)
    ]
    vmem, away = pl.BlockSpec(memory_space=pltpu.VMEM), pl.BlockSpec(memory_space=pltpu.HBM)
    return pl.pallas_call(
        results_kernel,
        out_shape=tuple(jax.ShapeDtypeStruct(shape, kind) for shape, kind in outs),
        in_specs=[away] * 7,
        out_specs=(vmem,) * 8,
        scratch_shapes=[pltpu.VMEM(arg.shape, arg.dtype) for arg in args[4:]]
        + [pltpu.SemaphoreType.DMA((7,))],
        compiler_params=pltpu.CompilerParams(vmem_limit_bytes=58 * 1024 * 1024),
    )(*args)


def turn_rates():
    rows = []
    for half in (HEAD // 4, HEAD // 2):
        frequency = np.float32(10000.0) ** (-np.arange(half, dtype=np.float32) / np.float32(half))
        rows.append(np.pad(np.tile(frequency, HEAD // half), (0, 56)))
    return np.stack(rows + [np.zeros(128)] * 6).astype(np.float32)


def body(
    hidden,
    query_space,
    key_space,
    value_space,
    positions,
    proj_space,
    shift_time,
    scale_time,
    qkv_time,
    grad_attn_time,
    grad_resid,
):
    def flat(values):
        return values.reshape(128, WIDTH)

    outs = results(
        *whole(
            scale_time, shift_time, positions, turn_rates(), flat(query_space), flat(key_space),
            flat(value_space), flat(hidden), flat(grad_attn_time), flat(grad_resid), proj_space,
            qkv_time,
        )
    )
    grads = tuple(out.reshape(hidden.shape) for out in outs[:4])
    return grads + (outs[4].T, outs[5].T, outs[6], outs[7])


def solution(mesh):
    in_specs = (
        P("dp", "seq", None, None),
        P("dp", "seq", None, None),
        P("dp", "seq", None, None),
        P("dp", "seq", None, None),
        P(None, "dp", None, None),
        P("dp", None),
        P("dp", None),
        P("dp", None),
        P("dp", None),
        P("dp", None, "seq", None),
        P("dp", "seq", None, None),
    )
    out_specs = (
        P("dp", "seq", None, None),
        P("dp", "seq", None, None),
        P("dp", "seq", None, None),
        P("dp", "seq", None, None),
        P("dp", "seq"),
        P("dp", "seq"),
        P("dp", None),
        P("dp", None),
    )
    return jax.shard_map(body, mesh=mesh, in_specs=in_specs, out_specs=out_specs, check_vma=False)
```

```python
import math

import jax
import jax.numpy as jnp
import numpy as np
from jax import lax
from jax.experimental import pallas as pl
from jax.experimental.pallas import tpu as pltpu
from jax.sharding import PartitionSpec as P

HEADS = 16


epsilon = 1e-06


MESH = pl.DeviceIdType.MESH

HALF_LANES = 640
KEEP_LANES = 384
ORDER = ("x_near", "y_near", "x_far", "z_near")
GROUPS = (
    (0, 0, 64, 0), (0, 64, 128, 1), (0, 128, 176, 2), (0, 176, 224, 3), (1, 0, 16, 0), (1, 16, 32, 1),
    (1, 32, 48, 2), (1, 48, 80, 3),
)
QKV_ROWS, PROJ_ROWS = 224, 80
QKV_WINDOW, PROJ_WINDOW = 80, 32


def place():
    dp, seq = lax.axis_index("dp"), lax.axis_index("seq")
    hi, core = dp // 2, dp % 2
    z, lo, x = seq // 8, (seq // 4) % 2, seq % 4
    return hi, core, z, lo, x


def device(hi, core, z, lo, x):
    return (hi * 2 + core, z * 8 + lo * 4 + x)


def send(source, target, sends, recvs, at, peer):
    copy = pltpu.make_async_remote_copy(
        src_ref=source, dst_ref=target, send_sem=sends.at[at], recv_sem=recvs.at[at],
        device_id=peer, device_id_type=MESH,
    )
    copy.start()
    return copy


def greet(peers):
    barrier = pltpu.get_barrier_semaphore()
    for peer in peers:
        pl.semaphore_signal(barrier, inc=1, device_id=peer, device_id_type=MESH)


def order_of(group):
    return [ORDER[(GROUPS[group][3] + step) % 4] for step in range(4)]


def combination(group, block):
    bits = {name: (block // (8 >> step)) % 2 for step, name in enumerate(order_of(group))}
    x = bits["x_far"] * 2 + (bits["x_near"] + bits["x_far"]) % 2
    return bits["z_near"] * 8 + bits["y_near"] * 4 + x


class Halving:
    def __init__(self, right, left, twin_left, work, got, sends, recvs):
        self.right, self.left, self.twin_left = right, left, twin_left
        self.work, self.got, self.sends, self.recvs = work, got, sends, recvs
        hi, core, z, lo, x = place()
        near = z % 2
        self.bits = {"x_near": (x % 2 + x // 2) % 2, "x_far": x // 2, "y_near": lo, "z_near": near}
        self.partners = {
            "x_near": device(hi, core, z, lo, x + 1 - 2 * (x % 2)),
            "x_far": device(hi, core, z, lo, 3 - x),
            "y_near": device(hi, core, z, 1 - lo, x),
            "z_near": device(hi, core, z + 1 - 2 * near, lo, x),
        }
        self.base = [0] * len(GROUPS)
        self.copies = {}

    def fill(self, group, start):
        kind, first_row, last_row, _ = GROUPS[group]
        count, rows = last_row - first_row, slice(first_row, last_row)
        left, other = self.left[kind], self.twin_left[kind]
        work, right = self.work[group], self.right[kind]

        def four(at, _):
            first = start + at * 4
            parts = []
            for j in range(4):
                block = combination(group, first + j)
                parts.append(jnp.concatenate([left[block, rows], other[block, rows]], axis=1))
            total = jnp.dot(
                jnp.concatenate(parts, axis=0), right[...], preferred_element_type=jnp.float32
            )
            work[pl.ds(first, 4)] = total.astype(jnp.bfloat16).reshape(4, count, HALF_LANES)
            return 0

        lax.fori_loop(0, 2, four, 0)

    def send(self, group, step, first):
        name = order_of(group)[step]
        self.copies[group, step] = send(
            self.work[group].at[pl.ds(first, 8 >> step)], self.got[group][step],
            self.sends, self.recvs, (group, step), self.partners[name],
        )

    def begin(self, group):
        bit = self.bits[order_of(group)[0]]
        self.fill(group, (1 - bit) * 8)
        self.send(group, 0, (1 - bit) * 8)

    def keep(self, group):
        self.base[group] = self.bits[order_of(group)[0]] * 8
        self.fill(group, self.base[group])

    def take(self, group, step, start, count, offset):
        work, got = self.work[group], self.got[group][step]

        def one(at, _):
            total = work[start + at].astype(jnp.float32) + got[offset + at].astype(jnp.float32)
            work[start + at] = total.astype(jnp.bfloat16)
            return 0

        lax.fori_loop(0, count, one, 0)

    def advance(self, group, step):
        half, bit = 8 >> step, self.bits[order_of(group)[step]]
        away, mine = (1 - bit) * half, bit * half
        self.copies[group, step - 1].wait_recv()
        self.take(group, step - 1, self.base[group] + away, half, away)
        self.send(group, step, self.base[group] + away)
        self.take(group, step - 1, self.base[group] + mine, half, mine)
        self.base[group] = self.base[group] + mine

    def last(self, group, target):
        _, first_row, last_row, _ = GROUPS[group]
        self.copies[group, 3].wait_recv()
        total = self.work[group][self.base[group]].astype(jnp.float32)
        total = (total + self.got[group][3][0].astype(jnp.float32)).astype(jnp.bfloat16)
        target[0, first_row:last_row] = total[:, :KEEP_LANES]
        target[1, first_row:last_row] = total[:, HALF_LANES - KEEP_LANES :]


def near_peers():
    hi, core, z, lo, x = place()
    group = lo * 4 + x
    plane = [(hi * 2 + core, z * 8 + (group + step) % 8) for step in range(1, 8)]
    line = [(hi * 2 + core, ((z + step) % 8) * 8 + group) for step in range(1, 8)]
    return plane, line


def swap_eights(rows):
    count = rows.shape[0]
    at = lax.broadcasted_iota(jnp.int32, (count, count), 0)
    origin = lax.broadcasted_iota(jnp.int32, (count, count), 1)
    wanted = (at // 2 % 8) * 16 + at // 16 * 2 + at % 2
    chosen = jnp.where(origin == wanted, 1.0, 0.0).astype(jnp.bfloat16)
    moved = jnp.dot(chosen, rows, preferred_element_type=jnp.float32)
    return moved.astype(jnp.bfloat16)


class Exchange:
    def __init__(self, first, got_first, second, got_second, sends, recvs):
        self.first, self.got_first = first, got_first
        self.second, self.got_second = second, got_second
        self.sends, self.recvs = sends, recvs
        self.plane, self.line = near_peers()
        _, _, self.z, lo, x = place()
        self.group = lo * 4 + x

    def start_plane(self, rows):
        self.first[...] = swap_eights(rows).reshape(self.first.shape)
        self.copies = [
            send(
                self.first.at[(self.group + step) % 8], self.got_first.at[self.group],
                self.sends, self.recvs, step, self.plane[step - 1],
            )
            for step in range(1, 8)
        ]
        self.got_first[self.group] = self.first[self.group]

    def start_line(self):
        for copy in self.copies:
            copy.wait_recv()
        rows = self.got_first[...].reshape(128, -1)
        self.second[...] = swap_eights(rows).reshape(self.second.shape)
        more = [
            send(
                self.second.at[(self.z + step) % 8], self.got_second.at[self.z],
                self.sends, self.recvs, 8 + step, self.line[step - 1],
            )
            for step in range(1, 8)
        ]
        self.got_second[self.z] = self.second[self.z]
        self.copies = self.copies + more
        return more

    def finish(self):
        for copy in self.copies[7:]:
            copy.wait_recv()
        for copy in self.copies:
            copy.wait_send()
        return self.got_second[...].reshape(128, -1)


EXCHANGE_SCRATCH = [pltpu.VMEM((8, 16, 1152), jnp.bfloat16)] * 4 + [
    pltpu.SemaphoreType.DMA((16,)),
    pltpu.SemaphoreType.DMA((16,)),
]


class Gather:
    def __init__(self, own, full, cut, along_x, sends, recvs, local):
        self.own, self.full, self.cut = own, full, cut
        self.sends, self.recvs, self.local = sends, recvs, local
        hi, core, z, lo, x = place()
        self.mine, self.far = hi * 2 + core, (1 - hi) * 2 + core
        self.twin = device(hi, 1 - core, z, lo, x)
        self.across = device(1 - hi, core, z, 1 - lo, x)
        if along_x:
            self.spot, self.there = x, x
            self.right = device(hi, core, z, lo, (x + 1) % 4)
            self.left = device(hi, core, z, lo, (x + 3) % 4)
        else:
            self.spot = lo * 2 + (lo + z) % 2
            self.there = 3 - self.spot
            self.right, self.left = [
                device(hi, core, z // 2 * 2 + (at % 2 + at // 2) % 2, at // 2, x)
                for at in ((self.spot + 1) % 4, (self.spot + 3) % 4)
            ]
        self.copies = {}

    def go(self, at, source, target, peer):
        self.copies[at] = send(source, target, self.sends, self.recvs, at, peer)

    def same(self, at, ref, peer):
        self.go(at, ref, ref, peer)

    def start(self):
        start = pl.multiple_of(self.there * 64 + self.there // 2 * 16, 16)
        self.go(0, self.own.at[pl.ds(start, 80)], self.full.at[self.mine, self.there], self.across)
        self.locals = []
        for quarter, first in enumerate(STARTS):
            source, target = self.own.at[pl.ds(first, 80)], self.full.at[self.mine, quarter]
            self.go(10 + quarter, source, target, self.twin)
            copy = pltpu.make_async_copy(source, target, self.local.at[quarter])
            copy.start()
            self.locals.append(copy)

    def spread(self):
        self.copies[0].wait_recv()
        piece = self.full.at[self.far, self.spot]
        self.same(2, piece, self.right)
        self.same(3, piece, self.left)
        self.same(4, piece, self.twin)

    def pass_on(self):
        cut, width = self.cut, self.full.shape[3]
        self.copies[2].wait_recv()
        from_left = (self.far, (self.spot + 3) % 4)
        self.same(5, self.full.at[from_left + (slice(None), pl.ds(0, cut))], self.right)
        self.same(6, self.full.at[from_left], self.twin)
        self.copies[3].wait_recv()
        from_right = (self.far, (self.spot + 1) % 4)
        self.same(7, self.full.at[from_right + (slice(None), pl.ds(cut, width - cut))], self.left)
        self.same(8, self.full.at[from_right], self.twin)

    def last(self):
        self.copies[5].wait_recv()
        self.copies[7].wait_recv()
        self.same(9, self.full.at[self.far, (self.spot + 2) % 4], self.twin)

    def arrive(self):
        for copy in self.locals:
            copy.wait()
        for at in (4, 6, 8, 9, 10, 11, 12, 13):
            self.copies[at].wait_recv()

    def finish(self):
        for copy in self.copies.values():
            copy.wait_send()


STARTS = (0, 64, 144, 208)
GATHER_SCRATCH = [
    pltpu.SemaphoreType.DMA((14,)), pltpu.SemaphoreType.DMA((14,)), pltpu.SemaphoreType.DMA((4,))
]


def weight_rows(full, columns):
    return jnp.concatenate(
        [
            full[block, quarter, 16 * (quarter % 2) : 80, columns]
            for block in range(4)
            for quarter in range(4)
        ],
        axis=0,
    )


WIDTH = 1152
HEAD = WIDTH // HEADS
FACTOR = 1.0 / math.sqrt(HEAD)


def across_rows(left, right):
    return lax.dot_general(
        left, right, (((1,), (1,)), ((), ())), preferred_element_type=jnp.float32
    )


def down_rows(left, right):
    return lax.dot_general(
        left, right, (((0,), (0,)), ((), ())), preferred_element_type=jnp.float32
    )


def turn_tables(angles, half):
    lane = lax.broadcasted_iota(jnp.int32, (1, WIDTH), 1) % HEAD
    first = lane % (2 * half) < half
    origin = lane // (2 * half) * half + lane % half
    row = lax.broadcasted_iota(jnp.int32, (128, WIDTH), 0)
    cosine_at = jnp.where(row == origin, 1.0, 0.0).astype(jnp.bfloat16)
    sine_at = jnp.where(row == origin + 36, 1.0, 0.0) * jnp.where(first, -1.0, 1.0)
    sine_at = sine_at.astype(jnp.bfloat16)
    cosine = jnp.zeros((128, WIDTH), jnp.float32)
    sine = jnp.zeros((128, WIDTH), jnp.float32)
    rest = angles
    for _ in range(3):
        part = rest.astype(jnp.bfloat16)
        rest = rest - part.astype(jnp.float32)
        cosine += jnp.dot(part, cosine_at, preferred_element_type=jnp.float32)
        sine += jnp.dot(part, sine_at, preferred_element_type=jnp.float32)
    return cosine, sine


def make_angles(positions, rates, space_angles, time_angles):
    lane = lax.broadcasted_iota(jnp.int32, (128, 128), 1)
    token = lax.broadcasted_iota(jnp.int32, (128, 128), 0)
    frame = pl.ds(lax.axis_index("seq"), 1)

    def spots(axis):
        places = positions[axis, 0, frame, :].astype(jnp.float32)
        return jnp.broadcast_to(places, (128, 128)).T

    stride = positions[0, 0, 1:2, 0:1].astype(jnp.float32)
    frames = jnp.broadcast_to(stride, (128, 128)) * (token // 2).astype(jnp.float32)
    by_row = lane % (HEAD // 2) < HEAD // 4
    for at, places, out in (
        (0, jnp.where(by_row, spots(1), spots(2)), space_angles), (1, frames, time_angles)
    ):
        angles = places * rates[at : at + 1]
        turned = jnp.where(lane < HEAD // 2, jnp.cos(angles), jnp.sin(angles))
        out[...] = jnp.where(lane < HEAD, turned, 0.0)


def turn(values, cosine, sine, half, direction):
    lane = lax.broadcasted_iota(jnp.int32, (1, WIDTH), 1) % (2 * half)
    partner = jnp.where(
        lane < half, pltpu.roll(values, WIDTH - half, 1), pltpu.roll(values, half, 1)
    )
    return values * cosine + partner * (sine * direction)


def head_window(head):
    start = min(head * HEAD // 128 * 128, WIDTH - 256)
    lane = lax.broadcasted_iota(jnp.int32, (1, 256), 1) + start
    mask = jnp.where((lane >= head * HEAD) & (lane < (head + 1) * HEAD), 1.0, 0.0)
    return slice(start, start + 256), mask.astype(jnp.bfloat16)


def softmax_rows(scores):
    exponent = jnp.exp(scores - jnp.max(scores, axis=-1, keepdims=True))
    return exponent / jnp.sum(exponent, axis=-1, keepdims=True)


def head_back(weights, query, key, value, grad, mask):
    grad = grad * mask
    rounded = weights.astype(jnp.bfloat16)
    grad_weights = across_rows(grad, value)
    delta = jnp.sum(rounded.astype(jnp.float32) * grad_weights, axis=-1, keepdims=True)
    scores = (weights * (grad_weights - delta) * FACTOR).astype(jnp.bfloat16)
    return (
        jnp.dot(scores, key * mask, preferred_element_type=jnp.float32),
        down_rows(scores, query * mask),
        down_rows(rounded, grad),
    )


def space_forward(heads, turned_query, turned_key, value, weights_ref, mixed):
    for head in heads:
        window, mask = head_window(head)
        scores = across_rows(turned_query[:, window] * mask, turned_key[:, window]) * FACTOR
        weights = softmax_rows(scores)
        weights_ref[head] = weights
        mixed[:, window] += jnp.dot(
            weights.astype(jnp.bfloat16), value[:, window] * mask,
            preferred_element_type=jnp.float32,
        )


def space_back_heads(heads, weights, turned_query, turned_key, value, grad, totals):
    for head in heads:
        window, mask = head_window(head)
        parts = head_back(
            weights[head], turned_query[:, window], turned_key[:, window], value[:, window],
            grad[:, window], mask,
        )
        for total, part in zip(totals, parts):
            total[:, window] += part


def core_columns(rows, core):
    part = WIDTH // 4
    pieces = [rows[:, (hi * 2 + core) * part : (hi * 2 + core + 1) * part] for hi in range(2)]
    rest = jnp.zeros((rows.shape[0], HALF_LANES - 2 * part), rows.dtype)
    return jnp.concatenate(pieces + [rest], axis=1)


def stage(pairs, sems):
    copies = [
        pltpu.make_async_copy(source, target, sems.at[at]) for at, (source, target) in enumerate(pairs)
    ]
    for copy in copies:
        copy.start()
    return copies


ROWS = ((128, WIDTH), jnp.bfloat16)
WIDE_ROWS = ((128, WIDTH), jnp.float32)
RIGHT = ((2, 128, HALF_LANES), jnp.bfloat16)


def time_sublayer(
    rows, gathers, qkv_full, scale_ref, shift_ref, grad_ref, angles_ref,
    right_ref, projected_ref, sums_ref,
    normed_ref, wide, turned, total_back, modulated_ref,
):
    rows = rows.astype(jnp.float32)
    centered = rows - jnp.mean(rows, axis=-1, keepdims=True)
    inverse = lax.rsqrt(jnp.mean(centered * centered, axis=-1, keepdims=True) + epsilon)
    normed = centered * inverse
    normed_ref[...] = normed
    scale = 1.0 + scale_ref[...]
    modulated = (normed * scale + shift_ref[...]).astype(jnp.bfloat16)
    modulated_ref[...] = modulated
    for core in range(2):
        right_ref[core] = core_columns(modulated, core)
    for block in range(9):
        if block % 3 == 0:
            gathers[block // 3].arrive()
        columns = slice(block * 384, block * 384 + 384)
        wide[:, columns] = jnp.dot(
            modulated_ref[...], weight_rows(qkv_full, columns), preferred_element_type=jnp.float32
        )
    cosine, sine = turn_tables(angles_ref[...], HEAD // 2)
    for block in range(2):
        columns = slice(block * WIDTH, block * WIDTH + WIDTH)
        turned[:, columns] = turn(wide[:, columns], cosine, sine, HEAD // 2, 1.0).astype(jnp.bfloat16)
    turned[:, 2 * WIDTH :] = wide[:, 2 * WIDTH :].astype(jnp.bfloat16)
    wide[...] = jnp.zeros_like(wide)
    spot_row = lax.broadcasted_iota(jnp.int32, (128, 128), 0) % 2
    spot_column = lax.broadcasted_iota(jnp.int32, (128, 128), 1) % 2
    together = spot_row == spot_column
    for head in range(HEADS):
        window, mask = head_window(head)
        windows = [slice(window.start + WIDTH * j, window.stop + WIDTH * j) for j in range(3)]
        query, key, value = [turned[:, columns] for columns in windows]
        scores = across_rows(query * mask, key) * FACTOR
        weights = softmax_rows(jnp.where(together, scores, -jnp.inf))
        parts = head_back(weights, query, key, value, grad_ref[:, window], mask)
        for columns, part in zip(windows, parts):
            wide[:, columns] += part
    for block in range(2):
        columns = slice(block * WIDTH, block * WIDTH + WIDTH)
        projected_ref[:, columns] = turn(wide[:, columns], cosine, sine, HEAD // 2, -1.0).astype(
            jnp.bfloat16
        )
    projected_ref[:, 2 * WIDTH :] = wide[:, 2 * WIDTH :].astype(jnp.bfloat16)
    for block in range(9):
        columns = slice(block * 384, block * 384 + 384)
        part = across_rows(projected_ref[:, columns], weight_rows(qkv_full, columns))
        if block == 0:
            total_back[...] = part
        else:
            total_back[...] += part
    grad = total_back[...]
    normed = normed_ref[...]
    sums_ref[0:1] = jnp.sum(grad, axis=0, keepdims=True)
    sums_ref[1:2] = jnp.sum(grad * normed, axis=0, keepdims=True)
    grad = grad * scale
    return (
        (
            grad
            - jnp.mean(grad, axis=-1, keepdims=True)
            - normed * jnp.mean(grad * normed, axis=-1, keepdims=True)
        )
        * inverse
    ).astype(jnp.bfloat16)


def tall_rows(values_ref, tall):
    for block in range(27):
        rows = slice(block * 128, block * 128 + 128)
        tall[rows] = values_ref[:, rows].astype(jnp.float32).T


def piece_rows(tall, turned_rows, combinations):
    piece = 3 * WIDTH // 64
    for at in combinations:
        parts = [tall[(16 * k + at) * piece : (16 * k + at + 1) * piece] for k in range(4)]
        parts.append(jnp.zeros((QKV_ROWS - 4 * piece, 128), jnp.float32))
        turned_rows[at] = jnp.concatenate(parts, axis=0).astype(jnp.bfloat16)


def whole_kernel(
    scale_in, shift_in, positions_in, rates_in,
    query_in, key_in, value_in, hidden_in, grad_time_in, resid_in, proj_ref, qkv_ref,
    hidden_out, query_out, key_out, value_out, total_ref, qkv_out, proj_out,
    query_ref, key_ref, value_ref, hidden_ref, grad_time, resid_ref,
    scale_ref, shift_ref, positions, rates, angles_ref, time_angles, stage_sems,
    turned_query, turned_key, weights_ref, proj_full, qkv_full,
    wide, mixed_ref, right_qkv, right_proj, projected, sums_ref, normed, time_wide, turned,
    total_back, modulated, tall,
    left_qkv, left_proj, both_qkv, both_proj, twin_qkv, twin_proj, twin_send, twin_recv,
    total_query, total_key, total_value, grad,
    plane_sums, line_sums, sum_sends, sum_recvs,
    step_send, step_recv, qkv_last, proj_last, qkv_final, proj_final, final_send, final_recv,
    *scratch,
):
    staged = stage(
        [
            (query_in, query_ref), (key_in, key_ref), (value_in, value_ref),
            (hidden_in, hidden_ref), (grad_time_in, grad_time), (resid_in, resid_ref),
            (scale_in, scale_ref), (shift_in, shift_ref), (positions_in, positions), (rates_in, rates),
        ],
        stage_sems,
    )
    hi, core, z, lo, x = place()
    near, pair = z % 2, z // 2
    twin = device(hi, 1 - core, z, lo, x)
    count = len(GROUPS)
    proj = Gather(proj_ref, proj_full, 640, True, *scratch[:3])
    thirds = []
    for third in range(3):
        columns = pl.ds(third * WIDTH, WIDTH)
        thirds.append(
            Gather(
                qkv_ref.at[:, columns], qkv_full.at[:, :, :, columns], 640, third == 1,
                *scratch[3 * third + 3 : 3 * third + 6],
            )
        )
    one, two, three = thirds
    exchange = Exchange(*scratch[12:18])
    exchange_back = Exchange(*scratch[18:24])
    group_at = exchange.group
    work, got = scratch[24 : 24 + count], scratch[24 + count :]
    got = [got[4 * group : 4 * group + 4] for group in range(count)]
    halving = Halving(
        (both_qkv, both_proj), (left_qkv, left_proj), (twin_qkv, twin_proj), work, got,
        step_send, step_recv,
    )
    others = []
    for step_hi in range(2):
        for step_pair in range(4):
            if step_hi + step_pair > 0:
                to_hi, to_pair = (hi + step_hi) % 2, (pair + step_pair) % 4
                others.append(
                    (step_hi * 4 + step_pair, to_hi, to_pair,
                     device(to_hi, core, to_pair * 2 + near, lo, x))
                )
    peers = [twin, proj.across] + [other[3] for other in others[3:]] + exchange.plane + exchange.line
    greet(peers)
    for copy in staged:
        copy.wait()
    make_angles(positions, rates, angles_ref, time_angles)
    cosine, sine = turn_tables(angles_ref[...], HEAD // 4)
    for source, target in ((query_ref, turned_query), (key_ref, turned_key)):
        values = source[...].astype(jnp.float32)
        target[...] = turn(values, cosine, sine, HEAD // 4, 1.0).astype(jnp.bfloat16)
    wide[...] = jnp.zeros_like(wide)
    pl.semaphore_wait(pltpu.get_barrier_semaphore(), len(peers))
    for gather in (proj, one, two, three):
        gather.start()

    def heads(first):
        space_forward(
            range(first, first + 4), turned_query, turned_key, value_ref, weights_ref, wide
        )

    proj.spread()
    heads(0)
    one.spread()
    heads(4)
    proj.pass_on()
    heads(8)
    two.spread()
    proj.last()
    heads(12)
    one.pass_on()
    mixed = wide[...].astype(jnp.bfloat16)
    mixed_ref[...] = mixed
    proj.arrive()
    for block in range(3):
        columns = slice(block * 384, block * 384 + 384)
        wide[:, columns] = hidden_ref[:, columns].astype(jnp.float32) + jnp.dot(
            mixed_ref[...], weight_rows(proj_full, columns), preferred_element_type=jnp.float32
        )
    exchange.start_plane(wide[...].astype(jnp.bfloat16))
    three.spread()
    one.last()
    for side in range(2):
        right_proj[side] = core_columns(mixed_ref[...], side)
    exchange.start_line()
    two.pass_on()
    two.last()
    three.pass_on()
    three.last()
    back_rows = time_sublayer(
        exchange.finish(), thirds, qkv_full, scale_ref, shift_ref, grad_time, time_angles,
        right_qkv, projected, sums_ref, normed, time_wide, turned, total_back, modulated,
    )
    own, other = pl.ds(0, 128), pl.ds(128, 128)
    exchange_back.start_plane(back_rows)
    sums = [
        send(sums_ref, plane_sums.at[group_at], sum_sends, sum_recvs, step, exchange.plane[step - 1])
        for step in range(1, 8)
    ]
    plane_sums[group_at] = sums_ref[...]
    to_right = [
        send(right_qkv.at[1 - core], both_qkv.at[other], twin_send, twin_recv, 0, twin),
        send(right_proj.at[1 - core], both_proj.at[other], twin_send, twin_recv, 2, twin),
    ]
    tall_rows(projected, tall)
    to_left = []
    for at, sem in ((0, 1), (8, 4)):
        piece_rows(tall, left_qkv, range(at, at + 8))
        half = pl.ds(at, 8)
        to_left.append(send(left_qkv.at[half], twin_qkv.at[half], twin_send, twin_recv, sem, twin))
    twins = [to_right[0], to_left[0], to_right[1]]
    both_qkv[own] = right_qkv[core]
    both_proj[own] = right_proj[core]
    twins[0].wait_recv()
    twins[1].wait_recv()
    to_left[1].wait_recv()
    for group in range(2):
        halving.begin(group)
    exchange_back.start_line()
    for copy in sums:
        copy.wait_recv()
    line_sums[z] = jnp.sum(plane_sums[...], axis=0)
    more = [
        send(
            line_sums.at[z], line_sums.at[z], sum_sends, sum_recvs, 8 + step,
            exchange.line[step - 1],
        )
        for step in range(1, 8)
    ]
    for group in range(2, 4):
        halving.begin(group)
    for group in range(4):
        halving.keep(group)
    row = lax.broadcasted_iota(jnp.int32, (PROJ_ROWS, WIDTH), 0)
    column = lax.broadcasted_iota(jnp.int32, (PROJ_ROWS, WIDTH), 1)
    piece = WIDTH // 64
    wanted = jnp.where(row < 4 * piece, row // piece * (16 * piece) + row % piece, -WIDTH)
    ahead = column - wanted
    frames = exchange_back.finish()
    hidden = resid_ref[...].astype(jnp.float32) + frames.astype(jnp.float32)
    hidden_out[...] = hidden.astype(jnp.bfloat16)
    for block in range(16):
        chosen = jnp.where(ahead == block * piece, 1.0, 0.0).astype(jnp.bfloat16)
        left_proj[block] = across_rows(chosen, hidden_out[...]).astype(jnp.bfloat16)
    twins.append(send(left_proj, twin_proj, twin_send, twin_recv, 3, twin))
    for block in range(3):
        columns = slice(block * 384, block * 384 + 384)
        part = across_rows(hidden_out[:, columns], weight_rows(proj_full, columns))
        if block == 0:
            total_query[...] = part
        else:
            total_query[...] += part
    grad[...] = total_query[...].astype(jnp.bfloat16)
    twins[2].wait_recv()
    twins[3].wait_recv()
    for group in range(4, 8):
        halving.begin(group)
    for group in range(4, 8):
        halving.keep(group)
    for group in range(4):
        halving.advance(group, 1)
    totals = (total_query, total_key, total_value)
    for total in totals:
        total[...] = jnp.zeros_like(total)

    def heads(first, end):
        space_back_heads(
            range(first, end), weights_ref, turned_query, turned_key, value_ref, grad, totals
        )

    heads(0, 10)
    for group in range(4):
        halving.advance(group, 2)
    heads(10, 16)
    for group in range(4, 8):
        halving.advance(group, 1)
    for group in range(4):
        halving.advance(group, 3)
    cosine, sine = turn_tables(angles_ref[...], HEAD // 4)
    for total, out in ((total_query, query_out), (total_key, key_out)):
        out[...] = turn(total[...], cosine, sine, HEAD // 4, -1.0).astype(jnp.bfloat16)
    value_out[...] = total_value[...].astype(jnp.bfloat16)
    for copy in more:
        copy.wait_recv()
    total_ref[...] = jnp.sum(line_sums[...], axis=0)
    for group in range(4, 8):
        halving.advance(group, 2)
    for group in range(4):
        halving.last(group, qkv_last)
    ends = []
    for slot, to_hi, to_pair, peer in others:
        rows = pl.ds(pl.multiple_of(to_pair * 48, 16), QKV_WINDOW)
        ends.append(
            send(qkv_last.at[to_hi, rows], qkv_final.at[slot], final_send, final_recv, slot, peer)
        )
    for group in range(4, 8):
        halving.advance(group, 3)
    for group in range(4, 8):
        halving.last(group, proj_last)
    for slot, to_hi, to_pair, peer in others:
        rows = pl.ds(pl.multiple_of(to_pair * 16, 16), PROJ_WINDOW)
        ends.append(
            send(
                proj_last.at[to_hi, rows], proj_final.at[slot], final_send, final_recv, 8 + slot,
                peer,
            )
        )
    total = qkv_last[hi, pl.ds(pl.multiple_of(pair * 48, 16), QKV_WINDOW)].astype(jnp.float32)
    for (slot, _, _, _), copy in zip(others, ends[:7]):
        copy.wait_recv()
        total += qkv_final[slot].astype(jnp.float32)
    total = pltpu.roll(pltpu.roll(total, (QKV_WINDOW - pair * 6) % QKV_WINDOW, 0), (KEEP_LANES - hi * 32) % KEEP_LANES, 1)
    qkv_out[...] = total
    total = proj_last[hi, pl.ds(pl.multiple_of(pair * 16, 16), PROJ_WINDOW)].astype(jnp.float32)
    for (slot, _, _, _), copy in zip(others, ends[7:]):
        copy.wait_recv()
        total += proj_final[slot].astype(jnp.float32)
    total = pltpu.roll(pltpu.roll(total, (PROJ_WINDOW - pair * 2) % PROJ_WINDOW, 0), (KEEP_LANES - hi * 32) % KEEP_LANES, 1)
    proj_out[...] = total
    for copy in twins + to_left[1:] + sums + more + list(halving.copies.values()) + ends:
        copy.wait_send()
    for gather in (proj, one, two, three):
        gather.finish()


def whole(scale, shift, positions, rates, query, key, value, hidden, grad_time, resid, proj, qkv):
    vmem, away = pl.BlockSpec(memory_space=pltpu.VMEM), pl.BlockSpec(memory_space=pltpu.HBM)
    b16, f32 = jnp.bfloat16, jnp.float32
    shape, dma = pltpu.VMEM, pltpu.SemaphoreType.DMA
    wide, sums = (128, 3 * WIDTH), (2, WIDTH)
    outs = [ROWS] * 4 + [
        (sums, f32), ((QKV_WINDOW, KEEP_LANES), f32), ((PROJ_WINDOW, KEEP_LANES), f32)
    ]
    counts = [last - first for _, first, last, _ in GROUPS]
    scratch = [shape(*ROWS)] * 6 + [
        shape(scale.shape, f32), shape(scale.shape, f32), shape(positions.shape, positions.dtype),
        shape(rates.shape, f32), shape((128, 128), f32), shape((128, 128), f32), dma((10,)),
        shape(*ROWS), shape(*ROWS), shape((HEADS, 128, 128), f32),
        shape((4, 4, 80, WIDTH), b16), shape((4, 4, 80, 3 * WIDTH), b16),
        shape(*WIDE_ROWS), shape(*ROWS), shape(*RIGHT), shape(*RIGHT), shape(wide, b16),
        shape(sums, f32), shape(*WIDE_ROWS), shape(wide, f32), shape(wide, b16),
        shape(*WIDE_ROWS), shape(*ROWS), shape((3 * WIDTH, 128), f32),
        shape((16, QKV_ROWS, 128), b16), shape((16, PROJ_ROWS, 128), b16),
        shape((256, HALF_LANES), b16), shape((256, HALF_LANES), b16),
        shape((16, QKV_ROWS, 128), b16), shape((16, PROJ_ROWS, 128), b16), dma((5,)), dma((5,)),
        shape(*WIDE_ROWS), shape(*WIDE_ROWS), shape(*WIDE_ROWS), shape(*ROWS),
        shape((8,) + sums, f32), shape((8,) + sums, f32), dma((16,)), dma((16,)),
        dma((8, 4)), dma((8, 4)),
        shape((2, QKV_ROWS, KEEP_LANES), b16), shape((2, PROJ_ROWS, KEEP_LANES), b16),
        shape((8, QKV_WINDOW, KEEP_LANES), b16), shape((8, PROJ_WINDOW, KEEP_LANES), b16),
        dma((16,)), dma((16,)),
    ] + GATHER_SCRATCH * 4 + EXCHANGE_SCRATCH * 2
    scratch += [shape((16, count, HALF_LANES), b16) for count in counts]
    scratch += [
        shape((8 >> step, count, HALF_LANES), b16) for count in counts for step in range(4)
    ]
    return pl.pallas_call(
        whole_kernel,
        out_shape=tuple(jax.ShapeDtypeStruct(*out) for out in outs),
        in_specs=[away] * 12,
        out_specs=(vmem,) * len(outs),
        scratch_shapes=scratch,
        compiler_params=pltpu.CompilerParams(
            collective_id=1, has_side_effects=True, vmem_limit_bytes=58 * 1024 * 1024
        ),
    )(scale, shift, positions, rates, query, key, value, hidden, grad_time, resid, proj, qkv)


def results_kernel(*refs):
    given, outs, (sums_ref, qkv_ref, proj_ref, sems) = refs[:7], refs[7:15], refs[15:]
    copies = stage(
        list(zip(given[4:], (sums_ref, qkv_ref, proj_ref))) + list(zip(given[:4], outs[:4])), sems
    )
    for copy in copies[:3]:
        copy.wait()
    part = WIDTH // 4
    outs[4][...] = proj_ref[: WIDTH // 64, :part]
    outs[5][...] = qkv_ref[: 3 * WIDTH // 64, :part]
    outs[6][...] = sums_ref[0:1]
    outs[7][...] = sums_ref[1:2]
    for copy in copies[3:]:
        copy.wait()


def results(*args):
    f32, part = jnp.float32, WIDTH // 4
    outs = [ROWS] * 4 + [
        ((WIDTH // 64, part), f32), ((3 * WIDTH // 64, part), f32), ((1, WIDTH), f32), ((1, WIDTH), f32)
    ]
    vmem, away = pl.BlockSpec(memory_space=pltpu.VMEM), pl.BlockSpec(memory_space=pltpu.HBM)
    return pl.pallas_call(
        results_kernel,
        out_shape=tuple(jax.ShapeDtypeStruct(shape, kind) for shape, kind in outs),
        in_specs=[away] * 7,
        out_specs=(vmem,) * 8,
        scratch_shapes=[pltpu.VMEM(arg.shape, arg.dtype) for arg in args[4:]]
        + [pltpu.SemaphoreType.DMA((7,))],
        compiler_params=pltpu.CompilerParams(vmem_limit_bytes=58 * 1024 * 1024),
    )(*args)


def turn_rates():
    rows = []
    for half in (HEAD // 4, HEAD // 2):
        frequency = np.float32(10000.0) ** (-np.arange(half, dtype=np.float32) / np.float32(half))
        rows.append(np.pad(np.tile(frequency, HEAD // half), (0, 56)))
    return np.stack(rows + [np.zeros(128)] * 6).astype(np.float32)


def body(
    hidden,
    query_space,
    key_space,
    value_space,
    positions,
    proj_space,
    shift_time,
    scale_time,
    qkv_time,
    grad_attn_time,
    grad_resid,
):
    def flat(values):
        return values.reshape(128, WIDTH)

    outs = results(
        *whole(
            scale_time, shift_time, positions, turn_rates(), flat(query_space), flat(key_space),
            flat(value_space), flat(hidden), flat(grad_attn_time), flat(grad_resid), proj_space,
            qkv_time,
        )
    )
    grads = tuple(out.reshape(hidden.shape) for out in outs[:4])
    return grads + (outs[4].T, outs[5].T, outs[6], outs[7])


def solution(mesh):
    in_specs = (
        P("dp", "seq", None, None),
        P("dp", "seq", None, None),
        P("dp", "seq", None, None),
        P("dp", "seq", None, None),
        P(None, "dp", None, None),
        P("dp", None),
        P("dp", None),
        P("dp", None),
        P("dp", None),
        P("dp", None, "seq", None),
        P("dp", "seq", None, None),
    )
    out_specs = (
        P("dp", "seq", None, None),
        P("dp", "seq", None, None),
        P("dp", "seq", None, None),
        P("dp", "seq", None, None),
        P("dp", "seq"),
        P("dp", "seq"),
        P("dp", None),
        P("dp", None),
    )
    return jax.shard_map(body, mesh=mesh, in_specs=in_specs, out_specs=out_specs, check_vma=False)
```
